128 devices in a mesh: dp: 16 (over x_hi, y, core), ctx: 8 (over x_lo, z).
Axes of the slice: x: 4 (x_hi: 2, x_lo: 2; x = x_hi * 2 + x_lo), y: 4, z: 4, core: 2. Of those that a mesh axis runs over, the one named last changes fastest.
Arguments:
- tokens: bfloat16 [16, 2048, 8192], P('dp', 'ctx'), may hold values from -16 to 16
- positions: int32 [2048], replicated, may hold values from 0 to 2047, as said below
- query_weight: float32 [8192, 512], P(('dp', 'ctx')), may hold values from -0.5 to 0.5
- key_weight: float32 [8192, 128], P(('dp', 'ctx')), may hold values from -0.5 to 0.5
- value_weight: float32 [8192, 128], P(('dp', 'ctx')), may hold values from -0.0625 to 0.0625
- grad_output: bfloat16 [16, 2048, 512], P('dp', 'ctx'), may hold values from -6 to 6
Outputs:
- attention: bfloat16 [16, 2048, 512], P('dp', 'ctx')
- grad_tokens: bfloat16 [16, 2048, 8192], P('dp', 'ctx')
- query_grad: float32 [8192, 512], P(('dp', 'ctx'))
- key_grad: float32 [8192, 128], P(('dp', 'ctx'))
- value_grad: float32 [8192, 128], P(('dp', 'ctx'))
The draws below stay inside these ranges and needn't reach their ends.
Inputs may be any that keep to these rules, and one draw needn't show every extreme that they name: Stored rows come in runs of 128; each run holds consecutive increasing positions starting at a multiple of 128; together the runs hold every position of the sequence once.
All inputs are finite; a program needn't handle non-finite values.
Results may differ from the reference program's by a relative error of at most 0.034.
Values may be sent and summed in bfloat16 or wider, within the bound.
A program may use at most 192 MiB of HBM per device.

```python
import jax
import jax.numpy as jnp
from jax import lax

D = 8192
HD = 128
HQ = 4
BATCH = 16
SEQ = 2048
RUN = 128


def draw_tokens(key, part):
    values_drawn = jax.random.normal(jax.random.fold_in(key, 1), (BATCH, SEQ, D), jnp.float32)
    values_drawn = jnp.clip(values_drawn, -5.0, 5.0)
    return values_drawn.astype(jnp.bfloat16)


def draw_positions(key, part):
    order_runs = jax.random.permutation(jax.random.fold_in(key, 3), SEQ // RUN)
    return (order_runs[:, None] * RUN + jnp.arange(RUN)[None, :]).reshape(SEQ).astype(jnp.int32)


def query_columns(key):
    drawn = jax.random.normal(jax.random.fold_in(key, 7), (D, HQ * HD), jnp.float32)
    return jnp.clip(drawn, -5.0, 5.0) * D ** (-0.5)


def draw_query_weight(key, part):
    return query_columns(key)


def draw_key_weight(key, part):
    fresh = jnp.clip(jax.random.normal(jax.random.fold_in(key, 8), (D, HD), jnp.float32), -5.0, 5.0) * D ** (-0.5)
    return fresh


def block_scale(key, dims, shards, least, largest):
    loudness = 1.0
    for axis_at, shards_of in shards:
        steps = jax.random.uniform(jax.random.fold_in(jax.random.fold_in(key, 6), axis_at), (shards_of,), jnp.float32, least / len(shards), largest / len(shards))
        loudness = loudness * jnp.repeat(jnp.exp(steps), dims[axis_at] // shards_of).reshape((-1,) + (1,) * (len(dims) - 1 - axis_at))
    return loudness


def bell_draw(stream_key, extent, scale, most, split=(), dtype=jnp.bfloat16):
    values = scale * jax.random.normal(stream_key, extent, jnp.float32)
    if split:
        values = values * block_scale(stream_key, extent, split, -0.22, 0.18)
    return jnp.clip(values, -most, most).astype(dtype)


def setup_inputs(seed: int = 0) -> dict:
    splits = jax.random.split(jax.random.key(seed), 7)
    return {
        "tokens": draw_tokens(jax.random.fold_in(splits[6], 71), 0),
        "positions": draw_positions(jax.random.fold_in(splits[6], 71), 0),
        "query_weight": draw_query_weight(jax.random.fold_in(splits[6], 71), 0),
        "key_weight": draw_key_weight(jax.random.fold_in(splits[6], 71), 0),
        "value_weight": bell_draw(splits[4], (D, HD), D ** -0.5, 0.0625, ((0, 128),), jnp.float32),
        "grad_output": bell_draw(splits[5], (BATCH, SEQ, HQ * HD), 1.0, 6.0, ((0, 16), (1, 8))),
    }


ROPE_BASE = 1000000.0
MASKED = -1.0e30


def rope_tables(positions_in, head_dim):
    half_width = head_dim // 2
    exponent = jnp.arange(half_width).astype(jnp.float32) * (2.0 / head_dim)
    frequency = jnp.power(ROPE_BASE, -exponent)
    angles = positions_in.astype(jnp.float32)[:, None] * frequency[None, :]
    angles = jnp.concatenate([angles, angles], axis=1)
    return jnp.cos(angles), jnp.sin(angles)


def rotate(field, cos_table, sin_table):
    half_width = field.shape[-1] // 2
    turned = jnp.concatenate([-field[..., half_width:], field[..., :half_width]], axis=-1)
    return field * cos_table + turned * sin_table


def unrotate(field, cos_table, sin_table):
    half_width = field.shape[-1] // 2
    turned = jnp.concatenate([field[..., half_width:], -field[..., :half_width]], axis=-1)
    return field * cos_table + turned * sin_table


def one_sequence(token_rows, weights_all, grad_rows, row_positions):
    score_scale = HD ** -0.5
    projected = jnp.dot(token_rows, weights_all, preferred_element_type=jnp.float32)
    cos_table, sin_table = rope_tables(row_positions, HD)
    query = projected[:, :HQ * HD].reshape(SEQ, HQ, HD)
    key_part = projected[:, HQ * HD:HQ * HD + HD]
    value_part = projected[:, HQ * HD + HD:]
    query_rot = rotate(query, cos_table[:, None, :], sin_table[:, None, :]).astype(jnp.bfloat16)
    key_rot = rotate(key_part, cos_table, sin_table).astype(jnp.bfloat16)
    value_b = value_part.astype(jnp.bfloat16)
    allowed = row_positions[None, :] <= row_positions[:, None]
    scores = jnp.einsum("qhd,kd->qhk", query_rot.astype(jnp.float32), key_rot.astype(jnp.float32)) * score_scale
    scores = jnp.where(allowed[:, None, :], scores, MASKED)
    row_max = jnp.max(scores, axis=-1)
    weight = jnp.where(allowed[:, None, :], jnp.exp(scores - row_max[..., None]), 0.0)
    denominator = jnp.sum(weight, axis=-1)
    log_total = row_max + jnp.log(denominator)
    weighted = jnp.einsum("qhk,kd->qhd", weight.astype(jnp.bfloat16).astype(jnp.float32), value_b.astype(jnp.float32))
    attention = (weighted / denominator[..., None]).astype(jnp.bfloat16)
    grad_heads = grad_rows.reshape(SEQ, HQ, HD).astype(jnp.float32)
    row_delta = jnp.sum(grad_heads * attention.astype(jnp.float32), axis=-1)
    probs = jnp.where(allowed[:, None, :], jnp.exp(scores - log_total[..., None]), 0.0)
    grad_probs = jnp.einsum("qhd,kd->qhk", grad_heads, value_b.astype(jnp.float32))
    dscore = (probs * (grad_probs - row_delta[..., None])).astype(jnp.bfloat16).astype(jnp.float32)
    probs_b = probs.astype(jnp.bfloat16).astype(jnp.float32)
    grad_query_rot = jnp.einsum("qhk,kd->qhd", dscore, key_rot.astype(jnp.float32)) * score_scale
    grad_key_rot = jnp.einsum("qhk,qhd->kd", dscore, query_rot.astype(jnp.float32)) * score_scale
    grad_value = jnp.einsum("qhk,qhd->kd", probs_b, grad_heads)
    grad_query = unrotate(grad_query_rot, cos_table[:, None, :], sin_table[:, None, :]).reshape(SEQ, HQ * HD)
    grad_key = unrotate(grad_key_rot, cos_table, sin_table)
    grad_proj = jnp.concatenate([grad_query, grad_key, grad_value], axis=1).astype(jnp.bfloat16)
    grad_input = jnp.dot(grad_proj, weights_all.T, preferred_element_type=jnp.float32).astype(jnp.bfloat16)
    grad_term = jnp.dot(token_rows.T, grad_proj, preferred_element_type=jnp.float32)
    return attention.reshape(SEQ, HQ * HD), grad_input, grad_term


def reference(tokens, positions, query_weight, key_weight, value_weight, grad_output):
    weights_all = jnp.concatenate([query_weight, key_weight, value_weight], axis=1).astype(jnp.bfloat16)

    def advance(grad_sum, inputs):
        attention, grad_input, grad_term = one_sequence(inputs[0], weights_all, inputs[1], positions)
        return grad_sum + grad_term, (attention, grad_input)

    initial = jnp.zeros((D, (HQ + 2) * HD), jnp.float32)
    weight_grads, (attention, grad_tokens) = lax.scan(advance, initial, (tokens, grad_output))
    query_grad = weight_grads[:, :HQ * HD]
    key_grad = weight_grads[:, HQ * HD:HQ * HD + HD]
    value_grad = weight_grads[:, HQ * HD + HD:]
    return attention, grad_tokens, query_grad, key_grad, value_grad
```

```python
import functools

import jax
import jax.numpy as jnp
from jax import lax
from jax.experimental import pallas as pl
from jax.experimental.pallas import tpu as pltpu
from jax.sharding import PartitionSpec as P

ROPE_BASE = 1000000.0
MASKED = -1e30
MESH = pl.DeviceIdType.MESH
BF16 = jnp.bfloat16
F32 = jnp.float32
AXES = ("x", "y", "z")
ORDERS = (("z", "y", "x"), ("x", "z", "y"), ("y", "x", "z"))


def place():
    dp, ctx = lax.axis_index("dp"), lax.axis_index("ctx")
    return {
        "x": lax.div(dp, 8) * 2 + lax.div(ctx, 4),
        "y": lax.rem(lax.div(dp, 2), 4),
        "z": lax.rem(ctx, 4),
        "core": lax.rem(dp, 2),
    }


def device(at):
    return (
        lax.div(at["x"], 2) * 8 + at["y"] * 2 + at["core"],
        lax.rem(at["x"], 2) * 4 + at["z"],
    )


def moved(at, axis, by):
    return {**at, axis: lax.rem(at[axis] + 4 + by, 4)}


def sibling(at):
    return {**at, "core": 1 - at["core"]}


def greet(targets):
    barrier = pltpu.get_barrier_semaphore()
    for target in targets:
        pl.semaphore_signal(barrier, inc=1, device_id=target, device_id_type=MESH)
    pl.semaphore_wait(barrier, len(targets))


def torus_neighbours(at):
    near = [device(moved(at, axis, by)) for axis in AXES for by in (1, -1)]
    return near + [device(sibling(at))]


def remote(src, dst, send, recv, target):
    return pltpu.make_async_remote_copy(
        src_ref=src, dst_ref=dst, send_sem=send, recv_sem=recv, device_id=target, device_id_type=MESH
    )


def gather_kernel(
    tokens, wq, wk, wv, w_all, tokens_twin,
    own, own_sem, send, recv, twin_send, twin_recv, token_send, token_recv,
):
    me = place()
    core = me["core"]
    twin = device(sibling(me))
    own[0] = wq[:, 0:256].astype(BF16)
    own[1] = wq[:, 256:512].astype(BF16)
    own[2, :, 0:128] = wk[...].astype(BF16)
    own[2, :, 128:256] = wv[...].astype(BF16)

    def block(part, where, core_at, rows=None):
        x, y, z = where.get("x"), where.get("y"), where.get("z")
        x_hi = slice(None) if x is None else lax.div(x, 2)
        x_lo = slice(None) if x is None else lax.rem(x, 2)
        y = slice(None) if y is None else y
        z = slice(None) if z is None else z
        rows = slice(None) if rows is None else pl.ds(rows * 32, 32)
        return w_all.at[part, x_hi, y, core_at, x_lo, z, rows]

    placed = []
    for part in range(3):
        copy = pltpu.make_async_copy(own.at[part], block(part, me, core), own_sem.at[part])
        copy.start()
        placed.append(copy)
    greet(torus_neighbours(me))
    started = []

    def send_to(src, dst, sems, k, target):
        copy = remote(src, dst, sems[0].at[k], sems[1].at[k], target)
        copy.start()
        started.append(copy)

    def arrival(ref, sems, k):
        remote(ref, ref, sems[0].at[k], sems[1].at[k], twin).wait_recv()

    ici = (send, recv)
    pair = (twin_send, twin_recv)
    for k in range(8):
        columns = tokens.at[:, pl.ds(pl.multiple_of(k * 1024 + (1 - core) * 512, 512), 512)]
        send_to(columns, tokens_twin.at[:, pl.ds(k * 512, 512)], (token_send, token_recv), k, twin)
    for copy in placed:
        copy.wait()

    def where_of(part, phase, index):
        order = ORDERS[part]
        where = {axis: me[axis] for axis in order[phase:]}
        where[order[phase]] = index
        return where

    for phase in range(3):
        for part in range(3):
            axis = ORDERS[part][phase]
            mine = block(part, where_of(part, phase, me[axis]), core)
            for d, by in enumerate((1, -1)):
                send_to(mine, mine, ici, (part * 3 + phase) * 4 + d, device(moved(me, axis, by)))
            if phase == 2:
                send_to(mine, mine, pair, part * 5, twin)
        for part in range(3):
            axis = ORDERS[part][phase]
            for d, by in enumerate((1, -1)):
                source = moved(me, axis, -by)[axis]
                where = where_of(part, phase, source)
                arrival(block(part, where, core), ici, (part * 3 + phase) * 4 + d)
                half = block(part, where, core, d)
                send_to(half, half, ici, (part * 3 + phase) * 4 + 2 + d, device(moved(me, axis, by)))
                if phase == 2:
                    whole = block(part, where, core)
                    send_to(whole, whole, pair, part * 5 + 1 + d, twin)
        for part in range(3):
            axis = ORDERS[part][phase]
            far = where_of(part, phase, moved(me, axis, 2)[axis])
            for d in range(2):
                half = block(part, far, core, d)
                arrival(half, ici, (part * 3 + phase) * 4 + 2 + d)
                if phase == 2:
                    send_to(half, half, pair, part * 5 + 3 + d, twin)
    for part in range(3):
        axis = ORDERS[part][2]
        for k in range(5):
            shift = (0, -1, 1, 2, 2)[k]
            where = where_of(part, 2, moved(me, axis, shift)[axis])
            arrival(block(part, where, 1 - core, None if k < 3 else k - 3), pair, part * 5 + k)
    for k in range(8):
        arrival(tokens_twin.at[:, pl.ds(k * 512, 512)], (token_send, token_recv), k)
    for copy in started:
        copy.wait_send()


def gather_weights(tokens, wq, wk, wv):
    vmem, anywhere = pl.BlockSpec(memory_space=pltpu.VMEM), pl.BlockSpec(memory_space=pl.ANY)
    w_all, tokens_twin = pl.pallas_call(
        gather_kernel,
        out_shape=(
            jax.ShapeDtypeStruct((3, 2, 4, 2, 2, 4, 64, 256), BF16),
            jax.ShapeDtypeStruct((256, 4096), BF16),
        ),
        in_specs=[anywhere, vmem, vmem, vmem],
        out_specs=(anywhere, anywhere),
        scratch_shapes=[
            pltpu.VMEM((3, 64, 256), BF16),
            pltpu.SemaphoreType.DMA((3,)),
            pltpu.SemaphoreType.DMA((36,)),
            pltpu.SemaphoreType.DMA((36,)),
            pltpu.SemaphoreType.DMA((15,)),
            pltpu.SemaphoreType.DMA((15,)),
            pltpu.SemaphoreType.DMA((8,)),
            pltpu.SemaphoreType.DMA((8,)),
        ],
        compiler_params=pltpu.CompilerParams(
            collective_id=0, has_side_effects=True, vmem_limit_bytes=16 * 2**20
        ),
        name="gather_weights",
    )(tokens, wq, wk, wv)
    return w_all.reshape(3, 8192, 256), tokens_twin


def ctx_peers():
    dp, ctx = lax.axis_index("dp"), lax.axis_index("ctx")
    return [(dp, lax.rem(ctx + k, 8)) for k in range(1, 8)]


def gather_kv_kernel(kv, kv_all, local_sem, send, recv):
    ctx = lax.axis_index("ctx")
    peers = ctx_peers()
    greet(peers)
    copies = []
    for k in (4, 2, 6, 1, 3, 5, 7):
        copy = remote(kv, kv_all.at[ctx], send.at[k - 1], recv.at[k - 1], peers[k - 1])
        copy.start()
        copies.append(copy)
    keep = pltpu.make_async_copy(kv, kv_all.at[ctx], local_sem.at[0])
    keep.start()
    keep.wait()
    for k in range(1, 8):
        source = lax.rem(ctx + 8 - k, 8)
        remote(kv, kv_all.at[source], send.at[k - 1], recv.at[k - 1], peers[k - 1]).wait_recv()
    for copy in copies:
        copy.wait_send()


def gather_kv(kv):
    vmem = pl.BlockSpec(memory_space=pltpu.VMEM)
    out = pl.pallas_call(
        gather_kv_kernel,
        out_shape=jax.ShapeDtypeStruct((8, 256, 256), BF16),
        in_specs=[vmem],
        out_specs=vmem,
        scratch_shapes=[
            pltpu.SemaphoreType.DMA((1,)),
            pltpu.SemaphoreType.DMA((7,)),
            pltpu.SemaphoreType.DMA((7,)),
        ],
        compiler_params=pltpu.CompilerParams(
            collective_id=1, has_side_effects=True, vmem_limit_bytes=16 * 2**20
        ),
        name="gather_kv",
    )(kv)
    return out.reshape(2048, 256)


def scatter_kv_kernel(terms, out, landed, send, recv):
    ctx = lax.axis_index("ctx")
    peers = ctx_peers()
    greet(peers)
    copies = []
    for k in (4, 2, 6, 1, 3, 5, 7):
        to = lax.rem(ctx + k, 8)
        copy = remote(terms.at[to], landed.at[k - 1], send.at[k - 1], recv.at[k - 1], peers[k - 1])
        copy.start()
        copies.append(copy)
    out[...] = terms[ctx].astype(F32)
    for copy in copies:
        copy.wait_recv()
    for k in range(7):
        out[...] += landed[k].astype(F32)
    for copy in copies:
        copy.wait_send()


def scatter_kv(terms):
    vmem = pl.BlockSpec(memory_space=pltpu.VMEM)
    return pl.pallas_call(
        scatter_kv_kernel,
        out_shape=jax.ShapeDtypeStruct((256, 256), F32),
        in_specs=[vmem],
        out_specs=vmem,
        scratch_shapes=[
            pltpu.VMEM((7, 256, 256), BF16),
            pltpu.SemaphoreType.DMA((7,)),
            pltpu.SemaphoreType.DMA((7,)),
        ],
        compiler_params=pltpu.CompilerParams(
            collective_id=2, has_side_effects=True, vmem_limit_bytes=16 * 2**20
        ),
        name="scatter_kv",
    )(terms.reshape(8, 256, 256))


def scatter_kernel(
    tokens, tokens_twin, grad_proj, out,
    held, grads, acc1, acc2, acc3, via1, via2, via3, end1, end2, end3,
    load_sem, twin_sem, send, recv,
):
    me = place()
    core = me["core"]
    twin = device(sibling(me))
    greet(torus_neighbours(me))
    swap = remote(grad_proj, grads.at[1], twin_sem.at[0], twin_sem.at[1], twin)
    swap.start()
    loads = []
    for k in range(8):
        columns = tokens.at[:, pl.ds(pl.multiple_of(k * 1024 + core * 512, 512), 512)]
        loads.append(pltpu.make_async_copy(columns, held.at[k, pl.ds(0, 256)], load_sem.at[2 * k]))
        columns = tokens_twin.at[:, pl.ds(k * 512, 512)]
        loads.append(pltpu.make_async_copy(columns, held.at[k, pl.ds(256, 256)], load_sem.at[2 * k + 1]))
    for copy in loads:
        copy.start()
    grads[0] = grad_proj[...]
    for copy in loads:
        copy.wait()
    swap.wait_recv()

    def product(k, _):
        x_hi, y = lax.div(k, 4), lax.rem(k, 4)
        for x_lo in range(2):
            lhs = held[k, :, x_lo * 256 : x_lo * 256 + 256]
            x = x_hi * 2 + x_lo
            for part in range(3):
                cols = slice(part * 256, part * 256 + 256)
                rhs = grads[:, :, cols].reshape(512, 256)
                term = lax.dot_general(lhs, rhs, (((0,), (0,)), ((), ())), preferred_element_type=F32)
                term = term.astype(BF16).reshape(4, 2, 32, 256)
                for z in range(4):
                    at = {"x": x, "y": y, "z": z}
                    first, second, third = (at[axis] for axis in reversed(ORDERS[part]))
                    for half in range(2):
                        acc1[part, first, half, second, third] = term[z, half]
        return 0

    lax.fori_loop(0, 8, product, 0)

    started = []

    def launch(src, dst, k, target):
        copy = remote(src, dst, send.at[k], recv.at[k], target)
        copy.start()
        started.append(copy)

    def arrival(ref, k):
        remote(ref, ref, send.at[k], recv.at[k], twin).wait_recv()

    accs, vias, ends = (acc1, acc2, acc3), (via1, via2, via3), (end1, end2, end3)

    def add_into(dst, src):
        def one(r, _):
            dst[r] = (dst[r].astype(F32) + src[r].astype(F32)).astype(BF16)
            return 0

        lax.fori_loop(0, dst.shape[0], one, 0)

    for phase in range(3):
        acc, via, end = accs[phase], vias[phase], ends[phase]
        for part in range(3):
            axis = ORDERS[part][2 - phase]
            base = (part * 3 + phase) * 6
            for d, by in enumerate((1, -1)):
                near, far = moved(me, axis, by), moved(me, axis, 2)
                launch(acc.at[part, far[axis], d], via.at[part, d], base + d, device(near))
            for d, by in enumerate((1, -1)):
                near = moved(me, axis, by)
                launch(acc.at[part, near[axis], 1 - d], end.at[part, d, 1 - d], base + 2 + d, device(near))
        for part in range(3):
            axis = ORDERS[part][2 - phase]
            base = (part * 3 + phase) * 6
            for d, by in enumerate((1, -1)):
                near = moved(me, axis, by)
                arrival(via.at[part, d], base + d)
                if phase == 0:
                    for j in range(4):
                        add_into(acc.at[part, near[axis], d, j], via.at[part, d, j])
                elif phase == 1:
                    add_into(acc.at[part, near[axis], d], via.at[part, d])
                else:
                    total = acc[part, near[axis], d].astype(F32) + via[part, d].astype(F32)
                    acc[part, near[axis], d] = total.astype(BF16)
                launch(acc.at[part, near[axis], d], end.at[part, d, d], base + 4 + d, device(near))
        for part in range(3):
            axis = ORDERS[part][2 - phase]
            base = (part * 3 + phase) * 6
            mine = me[axis]
            for half in range(2):
                arrival(end.at[part, 1 - half, half], base + 2 + (1 - half))
                arrival(end.at[part, half, half], base + 4 + half)

                def total(*index):
                    at = (half, *index)
                    return (
                        acc[(part, mine, *at)].astype(F32)
                        + end[(part, 0, *at)].astype(F32)
                        + end[(part, 1, *at)].astype(F32)
                    )

                if phase == 0:
                    for j in range(4):

                        def one(r, _):
                            acc2[part, j, half, r] = total(j, r).astype(BF16)
                            return 0

                        lax.fori_loop(0, 4, one, 0)
                elif phase == 1:
                    for j in range(4):
                        acc3[part, j, half] = total(j).astype(BF16)
                else:
                    out[half * 32 : half * 32 + 32, part * 256 : part * 256 + 256] = total()
    for copy in started:
        copy.wait_send()
    swap.wait_send()


def scatter_grads(tokens, tokens_twin, grad_proj):
    vmem, anywhere = pl.BlockSpec(memory_space=pltpu.VMEM), pl.BlockSpec(memory_space=pl.ANY)
    tile = (32, 256)
    return pl.pallas_call(
        scatter_kernel,
        out_shape=jax.ShapeDtypeStruct((64, 768), F32),
        in_specs=[anywhere, anywhere, vmem],
        out_specs=vmem,
        scratch_shapes=[
            pltpu.VMEM((8, 512, 512), BF16),
            pltpu.VMEM((2, 256, 768), BF16),
            pltpu.VMEM((3, 4, 2, 4, 4) + tile, BF16),
            pltpu.VMEM((3, 4, 2, 4) + tile, BF16),
            pltpu.VMEM((3, 4, 2) + tile, BF16),
            pltpu.VMEM((3, 2, 4, 4) + tile, BF16),
            pltpu.VMEM((3, 2, 4) + tile, BF16),
            pltpu.VMEM((3, 2) + tile, BF16),
            pltpu.VMEM((3, 2, 2, 4, 4) + tile, BF16),
            pltpu.VMEM((3, 2, 2, 4) + tile, BF16),
            pltpu.VMEM((3, 2, 2) + tile, BF16),
            pltpu.SemaphoreType.DMA((16,)),
            pltpu.SemaphoreType.DMA((2,)),
            pltpu.SemaphoreType.DMA((54,)),
            pltpu.SemaphoreType.DMA((54,)),
        ],
        compiler_params=pltpu.CompilerParams(
            collective_id=3, has_side_effects=True, vmem_limit_bytes=40 * 2**20
        ),
        name="scatter_grads",
    )(tokens, tokens_twin, grad_proj)


def rope_tables(positions_in, head_dim):
    half_width = head_dim // 2
    exponent = jnp.arange(half_width).astype(jnp.float32) * (2.0 / head_dim)
    frequency = jnp.power(ROPE_BASE, -exponent)
    angles = positions_in.astype(jnp.float32)[:, None] * frequency[None, :]
    angles = jnp.concatenate([angles, angles], axis=1)
    return (jnp.cos(angles), jnp.sin(angles))


def rotate(field, cos_table, sin_table):
    half_width = field.shape[-1] // 2
    turned = jnp.concatenate([-field[..., half_width:], field[..., :half_width]], axis=-1)
    return field * cos_table + turned * sin_table


def unrotate(field, cos_table, sin_table):
    half_width = field.shape[-1] // 2
    turned = jnp.concatenate([field[..., half_width:], -field[..., :half_width]], axis=-1)
    return field * cos_table + turned * sin_table


def body(tokens, positions, query_weight, key_weight, value_weight, grad_output):
    token_rows = tokens[0]
    local_rows = token_rows.shape[0]
    head_dim = key_weight.shape[1]
    query_width = query_weight.shape[1]
    head_count = query_width // head_dim
    score_scale = head_dim ** (-0.5)
    w_all, tokens_twin = gather_weights(token_rows, query_weight, key_weight, value_weight)
    projected = jnp.concatenate(
        [jnp.dot(token_rows, w_all[k], preferred_element_type=jnp.float32) for k in range(3)], axis=1
    )
    place_index = lax.axis_index("ctx")
    own_positions = lax.dynamic_slice_in_dim(positions, place_index * local_rows, local_rows)
    cos_table, sin_table = rope_tables(own_positions, head_dim)
    query = projected[:, :query_width].reshape(local_rows, head_count, head_dim)
    query_heads = rotate(query, cos_table[:, None, :], sin_table[:, None, :]).astype(jnp.bfloat16)
    key_rot = rotate(
        projected[:, query_width : query_width + head_dim], cos_table, sin_table
    ).astype(jnp.bfloat16)
    value_b = projected[:, query_width + head_dim :].astype(jnp.bfloat16)
    key_value = jnp.concatenate([key_rot, value_b], axis=1)
    keys_values = gather_kv(key_value)
    key_all = keys_values[:, :head_dim]
    value_all = keys_values[:, head_dim:]
    allowed = positions[None, :] <= own_positions[:, None]
    scores = (
        jnp.einsum("qhd,kd->qhk", query_heads, key_all, preferred_element_type=jnp.float32)
        * score_scale
    )
    scores = jnp.where(allowed[:, None, :], scores, MASKED)
    row_max = jnp.max(scores, axis=-1)
    weight = jnp.where(allowed[:, None, :], jnp.exp(scores - row_max[..., None]), 0.0)
    denominator = jnp.sum(weight, axis=-1)
    weighted = jnp.einsum(
        "qhk,kd->qhd", weight.astype(jnp.bfloat16), value_all, preferred_element_type=jnp.float32
    )
    log_total = row_max + jnp.log(denominator)
    attention = (weighted / denominator[..., None]).astype(jnp.bfloat16)
    grad_heads = grad_output[0].reshape(local_rows, head_count, head_dim)
    row_delta = jnp.sum(grad_heads.astype(jnp.float32) * attention.astype(jnp.float32), axis=-1)
    probs = jnp.where(allowed[:, None, :], jnp.exp(scores - log_total[..., None]), 0.0)
    grad_probs = jnp.einsum(
        "qhd,kd->qhk", grad_heads, value_all, preferred_element_type=jnp.float32
    )
    dscore = (probs * (grad_probs - row_delta[..., None])).astype(jnp.bfloat16)
    probs_b = probs.astype(jnp.bfloat16)
    grad_query_rot = (
        jnp.einsum("qhk,kd->qhd", dscore, key_all, preferred_element_type=jnp.float32) * score_scale
    )
    key_term = (
        jnp.einsum("qhk,qhd->kd", dscore, query_heads, preferred_element_type=jnp.float32)
        * score_scale
    )
    value_term = jnp.einsum("qhk,qhd->kd", probs_b, grad_heads, preferred_element_type=jnp.float32)
    keyval_term = jnp.concatenate([key_term, value_term], axis=1)
    keyval_grad = scatter_kv(keyval_term.astype(jnp.bfloat16))
    grad_query = unrotate(grad_query_rot, cos_table[:, None, :], sin_table[:, None, :]).reshape(
        local_rows, query_width
    )
    grad_key = unrotate(keyval_grad[:, :head_dim], cos_table, sin_table)
    grad_proj = jnp.concatenate([grad_query, grad_key, keyval_grad[:, head_dim:]], axis=1).astype(
        jnp.bfloat16
    )
    weight_grads = scatter_grads(token_rows, tokens_twin, grad_proj)
    grad_input = sum(
        lax.dot_general(
            grad_proj[:, k * 256 : k * 256 + 256],
            w_all[k],
            (((1,), (1,)), ((), ())),
            preferred_element_type=jnp.float32,
        )
        for k in range(3)
    ).astype(jnp.bfloat16)
    query_grad = weight_grads[:, :query_width]
    key_grad = weight_grads[:, query_width : query_width + head_dim]
    value_grad = weight_grads[:, query_width + head_dim :]
    attention_rows = attention.reshape(local_rows, query_width)
    return (attention_rows[None], grad_input[None], query_grad, key_grad, value_grad)


def solution(mesh):
    in_specs = (
        P("dp", "ctx", None),
        P(),
        P(("dp", "ctx"), None),
        P(("dp", "ctx"), None),
        P(("dp", "ctx"), None),
        P("dp", "ctx", None),
    )
    out_specs = (
        P("dp", "ctx", None),
        P("dp", "ctx", None),
        P(("dp", "ctx"), None),
        P(("dp", "ctx"), None),
        P(("dp", "ctx"), None),
    )
    return jax.shard_map(body, mesh=mesh, in_specs=in_specs, out_specs=out_specs, check_vma=False)
```

```python
import functools

import jax
import jax.numpy as jnp
from jax import lax
from jax.experimental import pallas as pl
from jax.experimental.pallas import tpu as pltpu
from jax.sharding import PartitionSpec as P

ROPE_BASE = 1000000.0
MASKED = -1e30
MESH = pl.DeviceIdType.MESH
BF16 = jnp.bfloat16
F32 = jnp.float32
AXES = ("x", "y", "z")
PIECES = (
    (2, 0, 64, 0, 128, ("y", "x", "z")),
    (2, 0, 32, 128, 128, ("z", "y", "x")),
    (2, 32, 32, 128, 128, ("z", "x", "y")),
    (0, 0, 64, 0, 256, ("z", "y", "x")),
    (1, 0, 64, 0, 256, ("z", "x", "y")),
)
KV_PIECES = (0, 1, 2)
Q_PIECES = (3, 4)
SCALE = 128 ** (-0.5)
LOG2E = 1.4426950408889634


def place():
    dp, ctx = lax.axis_index("dp"), lax.axis_index("ctx")
    return {
        "x": lax.div(dp, 8) * 2 + lax.div(ctx, 4),
        "y": lax.rem(lax.div(dp, 2), 4),
        "z": lax.rem(ctx, 4),
        "core": lax.rem(dp, 2),
    }


def device(at):
    return (
        lax.div(at["x"], 2) * 8 + at["y"] * 2 + at["core"],
        lax.rem(at["x"], 2) * 4 + at["z"],
    )


def moved(at, axis, by):
    return {**at, axis: lax.rem(at[axis] + 4 + by, 4)}


def sibling(at):
    return {**at, "core": 1 - at["core"]}


def greet(targets):
    barrier = pltpu.get_barrier_semaphore()
    for target in targets:
        pl.semaphore_signal(barrier, inc=1, device_id=target, device_id_type=MESH)
    pl.semaphore_wait(barrier, len(targets))


def partners(at):
    near = [device(moved(at, axis, by)) for axis in AXES for by in (1, -1, 2)]
    return near + [device(sibling(at))] + ctx_peers()


def ctx_peers():
    dp, ctx = lax.axis_index("dp"), lax.axis_index("ctx")
    return [(dp, lax.rem(ctx + k, 8)) for k in range(1, 8)]


def remote(src, dst, send, recv, target):
    return pltpu.make_async_remote_copy(
        src_ref=src, dst_ref=dst, send_sem=send, recv_sem=recv, device_id=target, device_id_type=MESH
    )


class Links:
    def __init__(self, send, recv, twin):
        self.send, self.recv, self.twin = send, recv, twin
        self.slots, self.started = {}, []

    def slot(self, key):
        return self.slots.setdefault(key, len(self.slots))

    def launch(self, key, src, dst, target):
        k = self.slot(key)
        copy = remote(src, dst, self.send.at[k], self.recv.at[k], target)
        copy.start()
        self.started.append(copy)

    def arrival(self, key, ref):
        k = self.slot(key)
        remote(ref, ref, self.send.at[k], self.recv.at[k], self.twin).wait_recv()

    def finish(self):
        for copy in self.started:
            copy.wait_send()


def turn_half(a):
    return pltpu.roll(a, 64, 1)


def gather_kernel(
    tokens, wq, wk, wv, cos_table, sin_table,
    w_out, turned_out, q_out, kv_out,
    w, tok, twin_tok, turned, copy_sem, send, recv,
):
    me = place()
    core = me["core"]
    twin = device(sibling(me))
    links = Links(send, recv, twin)
    load = pltpu.make_async_copy(tokens, tok, copy_sem.at[0])
    load.start()
    x_hi, x_lo = lax.div(me["x"], 2), lax.rem(me["x"], 2)
    w[2, x_hi, me["y"], core, x_lo, me["z"], :, 0:128] = wk[...].astype(BF16)
    w[2, x_hi, me["y"], core, x_lo, me["z"], :, 128:256] = wv[...].astype(BF16)
    w[0, x_hi, me["y"], core, x_lo, me["z"]] = wq[:, 0:256].astype(BF16)
    w[1, x_hi, me["y"], core, x_lo, me["z"]] = wq[:, 256:512].astype(BF16)

    def block(n, first, second, third, core_at=core, half=None):
        part, row, rows, col, cols, order = PIECES[n]
        at = dict(zip(order, (first, second, third)))
        x, y, z = (at[axis] for axis in AXES)
        if half is not None:
            rows = rows // 2
            row = row + half * rows
        return w.at[
            part,
            slice(None) if x is None else lax.div(x, 2),
            slice(None) if y is None else y,
            core_at,
            slice(None) if x is None else lax.rem(x, 2),
            slice(None) if z is None else z,
            pl.ds(row, rows),
            pl.ds(col, cols),
        ]

    def shifted(n, phase, by):
        axis = PIECES[n][5][phase]
        return moved(me, axis, by)

    def index(n, phase, by=0):
        axis = PIECES[n][5][phase]
        return moved(me, axis, by)[axis]

    greet(partners(me))
    everything = KV_PIECES + Q_PIECES
    for n in everything:
        mine = block(n, *(me[axis] for axis in PIECES[n][5]))
        for by in (1, -1, 2):
            links.launch((n, 0, by), mine, mine, device(shifted(n, 0, by)))
    for k in range(8):
        columns = tokens.at[:, pl.ds(pl.multiple_of(k * 1024 + (1 - core) * 512, 512), 512)]
        links.launch(("tokens", k), columns, twin_tok.at[k], twin)

    def spread(n, key, axis_at, ref):
        for by in (1, -1):
            links.launch((n, key, by), ref, ref, device(shifted(n, axis_at, by)))

    def pass_on(n, key, axis_at, where):
        for d, by in enumerate((1, -1)):
            source = index(n, axis_at, -by)
            links.arrival((n, key, by), block(n, *where(source)))
            half = block(n, *where(source), half=d)
            links.launch((n, key, "far", by), half, half, device(shifted(n, axis_at, by)))

    def far_arrival(n, key, axis_at, where):
        far = index(n, axis_at, 2)
        for d, by in enumerate((1, -1)):
            links.arrival((n, key, "far", by), block(n, *where(far), half=d))

    SHIFTS = (0, -1, 1, 2)

    def chunk(n, c):
        return lambda third: (None, index(n, 1, SHIFTS[c]), third)

    def to_twin(n, key, where):
        links.launch((n, "twin", key), block(n, *where), block(n, *where), twin)

    def from_twin(n):
        for key in range(3):
            links.arrival((n, "twin", key), block(n, None, None, index(n, 2, (0, -1, 1)[key]), 1 - core))
        for c in range(4):
            where = (None, index(n, 1, SHIFTS[c]), index(n, 2, 2))
            links.arrival((n, "twin", 3 + c), block(n, *where, core_at=1 - core))

    def step_first(n):
        second, third = index(n, 1), index(n, 2)
        for by in (1, -1, 2):
            links.arrival((n, 0, by), block(n, index(n, 0, -by), second, third))
        line = block(n, None, second, third)
        spread(n, 1, 1, line)
        spread(n, (2, 0), 2, line)

    def step_second(n):
        third = index(n, 2)
        second_at = lambda second: (None, second, third)
        pass_on(n, 1, 1, second_at)
        for c in (1, 2):
            spread(n, (2, c), 2, block(n, *chunk(n, c)(third)))

    def step_third(n):
        third = index(n, 2)
        pass_on(n, (2, 0), 2, chunk(n, 0))
        far_arrival(n, 1, 1, lambda second: (None, second, third))
        spread(n, (2, 3), 2, block(n, *chunk(n, 3)(third)))
        to_twin(n, 0, (None, None, third))

    def step_chunks(n, cs):
        for c in cs:
            pass_on(n, (2, c), 2, chunk(n, c))

    def step_near_twin(n):
        for key, by in ((1, -1), (2, 1)):
            to_twin(n, key, (None, None, index(n, 2, by)))

    def step_far(n, c):
        far_arrival(n, (2, c), 2, chunk(n, c))
        to_twin(n, 3 + c, chunk(n, c)(index(n, 2, 2)))

    for step in (step_first, step_second, step_third):
        for n in everything:
            step(n)

    load.wait()
    for k in range(8):
        links.arrival(("tokens", k), twin_tok.at[k])

    def turn(k):
        at = pl.multiple_of(k * 1024 + core * 512, 512)
        turned[k, :, 0:256] = tok[:, pl.ds(at, 512)].T
        turned[k, :, 256:512] = twin_tok[k].T

    def finish_piece(n):
        for c in range(4):
            step_far(n, c)

    for n in KV_PIECES:
        step_chunks(n, (1, 2, 3))
    for n in Q_PIECES:
        step_chunks(n, (1,))
    for n in KV_PIECES:
        step_near_twin(n)
        finish_piece(n)
    for n in Q_PIECES:
        step_chunks(n, (2,))
    for n in KV_PIECES:
        from_twin(n)

    def project(part):
        def add(k, total):
            lhs = tok[:, pl.ds(pl.multiple_of(k * 2048, 2048), 2048)]
            rows = w[part, lax.div(k, 2), pl.ds(lax.rem(k, 2) * 2, 2)].reshape(2048, 256)
            return total + jnp.dot(lhs, rows, preferred_element_type=F32)

        return lax.fori_loop(0, 4, add, jnp.zeros((256, 256), F32))

    cos, sin = cos_table[...], sin_table[...]
    keep = []

    def store(part):
        copy = pltpu.make_async_copy(w.at[part], w_out.at[part], copy_sem.at[1 + part])
        copy.start()
        keep.append(copy)

    ctx = lax.axis_index("ctx")
    both = project(2)
    key = both[:, 0:128]
    kv_out[ctx, :, 0:128] = (key * cos + turn_half(key) * sin).astype(BF16)
    kv_out[ctx, :, 128:256] = both[:, 128:256].astype(BF16)
    peers = ctx_peers()
    for k in (4, 2, 6, 1, 3, 5, 7):
        links.launch(("kv", k), kv_out.at[ctx], kv_out.at[ctx], peers[k - 1])
    store(2)
    for n in Q_PIECES:
        step_chunks(n, (3,))
    for n in Q_PIECES:
        step_near_twin(n)

    def turn_step(k, _):
        turn(k)
        return 0

    lax.fori_loop(0, 8, turn_step, 0)
    copy = pltpu.make_async_copy(turned, turned_out, copy_sem.at[4])
    copy.start()
    keep.append(copy)
    for c in range(4):
        for n in Q_PIECES:
            step_far(n, c)
    for n in Q_PIECES:
        from_twin(n)
        part = PIECES[n][0]
        store(part)
        both = project(part)
        for h in range(2):
            query = both[:, h * 128 : h * 128 + 128]
            rotated = (query * cos + turn_half(query) * sin).astype(BF16)
            q_out[:, part * 256 + h * 128 : part * 256 + h * 128 + 128] = rotated
    for k in range(1, 8):
        links.arrival(("kv", k), kv_out.at[lax.rem(ctx + 8 - k, 8)])
    for copy in keep:
        copy.wait()
    links.finish()


def gather_weights(tokens, wq, wk, wv, cos_table, sin_table):
    vmem, anywhere = pl.BlockSpec(memory_space=pltpu.VMEM), pl.BlockSpec(memory_space=pl.ANY)
    shape = jax.ShapeDtypeStruct
    return pl.pallas_call(
        gather_kernel,
        out_shape=(
            shape((3, 2, 4, 2, 2, 4, 64, 256), BF16),
            shape((8, 512, 512), BF16),
            shape((256, 512), BF16),
            shape((8, 256, 256), BF16),
        ),
        in_specs=[anywhere, vmem, vmem, vmem, vmem, vmem],
        out_specs=(anywhere, anywhere, vmem, vmem),
        scratch_shapes=[
            pltpu.VMEM((3, 2, 4, 2, 2, 4, 64, 256), BF16),
            pltpu.VMEM((256, 8192), BF16),
            pltpu.VMEM((8, 256, 512), BF16),
            pltpu.VMEM((8, 512, 512), BF16),
            pltpu.SemaphoreType.DMA((5,)),
            pltpu.SemaphoreType.DMA((176,)),
            pltpu.SemaphoreType.DMA((176,)),
        ],
        compiler_params=pltpu.CompilerParams(
            collective_id=0, has_side_effects=True, vmem_limit_bytes=44 * 2**20
        ),
        name="gather_weights",
    )(tokens, wq, wk, wv, cos_table, sin_table)


def attention_kernel(
    positions, own_positions, q, kv, grad, cos_table, sin_table,
    attention, grad_q, terms,
    qs, gs, gs_t, keys_t, values_t, scores, top, total, att_t, gq_t,
):
    for h in range(4):
        rows = slice(h * 256, h * 256 + 256)
        qs[rows] = q[:, h * 128 : h * 128 + 128]
        gs[rows] = grad[:, h * 128 : h * 128 + 128]
        gs_t[:, rows] = grad[:, h * 128 : h * 128 + 128].T
    for k in range(8):
        cols = slice(k * 256, k * 256 + 256)
        keys_t[:, cols] = kv[k, :, 0:128].T
        values_t[:, cols] = kv[k, :, 128:256].T
    nt = (((1,), (1,)), ((), ()))
    lead = own_positions[...] - lax.broadcasted_iota(jnp.int32, (128, 256), 0)
    top[...] = jnp.full(top.shape, MASKED, F32)

    def score(k, _):
        for h in range(4):
            cols = slice(h * 256, h * 256 + 256)
            s = lax.dot_general(kv[k, :, 0:128], qs[cols], nt, preferred_element_type=F32)
            upper = jnp.where(lead >= positions[k * 256], s[0:128], MASKED)
            lower = jnp.where(lead >= positions[k * 256 + 128], s[128:256], MASKED)
            scores[k, 0:128, cols] = upper
            scores[k, 128:256, cols] = lower
            high = jnp.max(jnp.maximum(upper, lower), axis=0, keepdims=True)
            top[:, cols] = jnp.maximum(top[:, cols], high)
        return 0

    lax.fori_loop(0, 8, score, 0)
    total[...] = jnp.zeros(total.shape, F32)
    att_t[...] = jnp.zeros(att_t.shape, F32)

    def weigh(k, _):
        at = pl.ds(pl.multiple_of(k * 256, 256), 256)
        for h in range(4):
            cols = slice(h * 256, h * 256 + 256)
            weight = jnp.exp2((scores[k, :, cols] - top[:, cols]) * (SCALE * LOG2E))
            scores[k, :, cols] = weight
            total[:, cols] += jnp.sum(weight, axis=0, keepdims=True)
            att_t[:, cols] += jnp.dot(values_t[:, at], weight.astype(BF16), preferred_element_type=F32)
        return 0

    lax.fori_loop(0, 8, weigh, 0)
    for h in range(4):
        cols = slice(h * 256, h * 256 + 256)
        inverse = 1.0 / total[:, cols]
        out = (att_t[:, cols] / total[:, cols]).astype(BF16)
        attention[:, h * 128 : h * 128 + 128] = out.T
        total[:, cols] = inverse
        top[:, cols] = jnp.sum(gs_t[:, cols].astype(F32) * out.astype(F32), axis=0, keepdims=True)
    gq_t[...] = jnp.zeros(gq_t.shape, F32)

    def back(k, _):
        at = pl.ds(pl.multiple_of(k * 256, 256), 256)
        key_term = jnp.zeros((256, 128), F32)
        value_term = jnp.zeros((256, 128), F32)
        for h in range(4):
            cols = slice(h * 256, h * 256 + 256)
            probs = scores[k, :, cols] * total[:, cols]
            grad_probs = lax.dot_general(kv[k, :, 128:256], gs[cols], nt, preferred_element_type=F32)
            dscore = (probs * (grad_probs - top[:, cols])).astype(BF16)
            key_term += jnp.dot(dscore, qs[cols], preferred_element_type=F32)
            value_term += jnp.dot(probs.astype(BF16), gs[cols], preferred_element_type=F32)
            gq_t[:, cols] += jnp.dot(keys_t[:, at], dscore, preferred_element_type=F32)
        terms[k, :, 0:128] = (key_term * SCALE).astype(BF16)
        terms[k, :, 128:256] = value_term.astype(BF16)
        return 0

    lax.fori_loop(0, 8, back, 0)
    for h in range(4):
        a = gq_t[:, h * 256 : h * 256 + 256].T * SCALE
        unrotated = a * cos_table[...] - turn_half(a) * sin_table[...]
        grad_q[:, h * 128 : h * 128 + 128] = unrotated.astype(BF16)


def attend(positions, own_positions, q, kv, grad, cos_table, sin_table):
    vmem = pl.BlockSpec(memory_space=pltpu.VMEM)
    shape = jax.ShapeDtypeStruct
    return pl.pallas_call(
        attention_kernel,
        out_shape=(shape((256, 512), BF16), shape((256, 512), BF16), shape((8, 256, 256), BF16)),
        in_specs=[pl.BlockSpec(memory_space=pltpu.SMEM)] + [vmem] * 6,
        out_specs=(vmem, vmem, vmem),
        scratch_shapes=[
            pltpu.VMEM((1024, 128), BF16),
            pltpu.VMEM((1024, 128), BF16),
            pltpu.VMEM((128, 1024), BF16),
            pltpu.VMEM((128, 2048), BF16),
            pltpu.VMEM((128, 2048), BF16),
            pltpu.VMEM((8, 256, 1024), F32),
            pltpu.VMEM((1, 1024), F32),
            pltpu.VMEM((1, 1024), F32),
            pltpu.VMEM((128, 1024), F32),
            pltpu.VMEM((128, 1024), F32),
        ],
        compiler_params=pltpu.CompilerParams(vmem_limit_bytes=32 * 2**20),
        name="attend",
    )(positions, own_positions, q, kv, grad, cos_table, sin_table)


def scatter_kernel(
    turned, w_all, grad_q, terms, cos_table, sin_table,
    tokens_out, out,
    held, w, grads, landed, grad_tok, copy_sem, send, recv, *buffers,
):
    me = place()
    core = me["core"]
    ctx = lax.axis_index("ctx")
    twin = device(sibling(me))
    links = Links(send, recv, twin)
    accs = [buffers[9 * n : 9 * n + 3] for n in range(len(PIECES))]
    vias = [buffers[9 * n + 3 : 9 * n + 5] for n in range(len(PIECES))]
    ends = [buffers[9 * n + 5 : 9 * n + 8] for n in range(len(PIECES))]
    load = pltpu.make_async_copy(turned, held, copy_sem.at[0])
    load.start()
    load_w = pltpu.make_async_copy(w_all, w, copy_sem.at[1])
    load_w.start()
    greet(partners(me))
    links.launch("grad_q", grad_q, grads.at[1, :, pl.ds(0, 512)], twin)
    peers = ctx_peers()
    for k in (4, 2, 6, 1, 3, 5, 7):
        links.launch(("kv", k), terms.at[lax.rem(ctx + k, 8)], landed.at[k - 1], peers[k - 1])
    grads[0, :, 0:512] = grad_q[...]
    load.wait()
    links.arrival("grad_q", grads.at[1, :, pl.ds(0, 512)])

    def axes(n):
        return tuple(reversed(PIECES[n][5]))

    def near(n, phase, by):
        return device(moved(me, axes(n)[phase], by))

    def at(n, phase, by=0):
        axis = axes(n)[phase]
        return moved(me, axis, by)[axis]

    def product(pieces, x, y):
        part = PIECES[pieces[0]][0]
        k = lax.div(x, 2) * 4 + y
        lhs = held[k, pl.ds(pl.multiple_of(lax.rem(x, 2) * 256, 256), 256)]
        rhs = grads[:, :, part * 256 : part * 256 + 256].reshape(512, 256)
        term = jnp.dot(lhs, rhs, preferred_element_type=F32).astype(BF16)
        for n in pieces:
            _, row, rows, col, cols, _ = PIECES[n]
            for z in range(4):
                first, second, third = ({"x": x, "y": y, "z": z}[axis] for axis in axes(n))
                for half in range(2):
                    start = z * 64 + row + half * rows // 2
                    accs[n][0][first, half, second, third] = term[
                        start : start + rows // 2, col : col + cols
                    ]

    SHIFTS = (2, 1, -1, 0)

    def send_far(n):
        for c in range(4):
            j = at(n, 1, SHIFTS[c])
            for d, by in enumerate((1, -1)):
                src = accs[n][0].at[at(n, 0, 2), d, j]
                links.launch((n, "via", c, d), src, vias[n][0].at[d, j], near(n, 0, by))

    def send_near(n, d, by):
        for c in range(4):
            j = at(n, 1, SHIFTS[c])
            src = accs[n][0].at[at(n, 0, by), 1 - d, j]
            links.launch((n, "end", c, d, 1 - d), src, ends[n][0].at[d, 1 - d, j], near(n, 0, by))

    def relay(n, c):
        j = at(n, 1, SHIFTS[c])
        acc, via, end = accs[n][0], vias[n][0], ends[n][0]
        for d, by in enumerate((1, -1)):
            links.arrival((n, "via", c, d), via.at[d, j])
            i = at(n, 0, by)
            acc[i, d, j] = (acc[i, d, j].astype(F32) + via[d, j].astype(F32)).astype(BF16)
            links.launch((n, "end", c, d, d), acc.at[i, d, j], end.at[d, d, j], near(n, 0, by))

    def gathered(n, c):
        j = at(n, 1, SHIFTS[c])
        acc, end, later = accs[n][0], ends[n][0], accs[n][1]
        for h in range(2):
            for d in range(2):
                links.arrival((n, "end", c, d, h), end.at[d, h, j])
            mine = acc[at(n, 0), h, j].astype(F32)
            later[j, h] = (mine + end[0, h, j].astype(F32) + end[1, h, j].astype(F32)).astype(BF16)
        if c == 0:
            for d, by in enumerate((1, -1)):
                links.launch((n, "via2", d), later.at[j, d], vias[n][1].at[d], near(n, 1, by))
        elif c < 3:
            d, by = c - 1, SHIFTS[c]
            src = later.at[j, 1 - d]
            links.launch((n, "end2", d, 1 - d), src, ends[n][1].at[d, 1 - d], near(n, 1, by))

    def second(n):
        acc, via, end = accs[n][1], vias[n][1], ends[n][1]
        for d, by in enumerate((1, -1)):
            links.arrival((n, "via2", d), via.at[d])
            i = at(n, 1, by)
            acc[i, d] = (acc[i, d].astype(F32) + via[d].astype(F32)).astype(BF16)
            links.launch((n, "end2", d, d), acc.at[i, d], end.at[d, d], near(n, 1, by))

    def third(n):
        acc, end, later = accs[n][1], ends[n][1], accs[n][2]
        for h in range(2):
            for d in range(2):
                links.arrival((n, "end2", d, h), end.at[d, h])
            mine = acc[at(n, 1), h].astype(F32)
            total = (mine + end[0, h].astype(F32) + end[1, h].astype(F32)).astype(BF16)
            for k in range(4):
                later[k, h] = total[k]
        for s, by in enumerate((1, -1, 2)):
            links.launch((n, "last", s), later.at[at(n, 2, by)], ends[n][2].at[s], near(n, 2, by))

    def last(n):
        part, row, rows, col, cols, _ = PIECES[n]
        acc, end = accs[n][2], ends[n][2]
        for s in range(3):
            links.arrival((n, "last", s), end.at[s])
        for h in range(2):
            total = acc[at(n, 2), h].astype(F32)
            for s in range(3):
                total = total + end[s, h].astype(F32)
            start = row + h * (rows // 2)
            out[start : start + rows // 2, part * 256 + col : part * 256 + col + cols] = total

    def products(n, by):
        axis = axes(n)[0]
        other = "y" if axis == "x" else "x"
        i = at(n, 0, by)

        def one(j, _):
            where = {axis: i, other: j}
            product((n,), where["x"], where["y"])
            return 0

        lax.fori_loop(0, 4, one, 0)

    for n in Q_PIECES:
        products(n, 2)
        send_far(n)
    for d, by in enumerate((1, -1)):
        for n in Q_PIECES:
            products(n, by)
            send_near(n, d, by)
    for n in Q_PIECES:
        products(n, 0)
    for c in range(4):
        for n in Q_PIECES:
            relay(n, c)

    for k in range(1, 8):
        links.arrival(("kv", k), landed.at[k - 1])
    keyval = terms[ctx].astype(F32)
    for k in range(7):
        keyval = keyval + landed[k].astype(F32)
    key = keyval[:, 0:128]
    grads[0, :, 512:640] = (key * cos_table[...] - turn_half(key) * sin_table[...]).astype(BF16)
    grads[0, :, 640:768] = keyval[:, 128:256].astype(BF16)
    columns = pl.ds(512, 256)
    links.launch("grad_kv", grads.at[0, :, columns], grads.at[1, :, columns], twin)
    load_w.wait()

    def input_slice(k, _):
        total = None
        for part in range(3):
            lhs = grads[0, :, part * 256 : part * 256 + 256]
            rows = w[part, lax.div(k, 8), lax.rem(lax.div(k, 2), 4), lax.rem(k, 2)].reshape(512, 256)
            term = lax.dot_general(lhs, rows, (((1,), (1,)), ((), ())), preferred_element_type=F32)
            total = term if total is None else total + term
        grad_tok[:, pl.ds(pl.multiple_of(k * 512, 512), 512)] = total.astype(BF16)
        return 0

    stores = []

    def inputs(quarter):
        lax.fori_loop(quarter * 4, quarter * 4 + 4, input_slice, 0)
        cols = pl.ds(quarter * 2048, 2048)
        copy = pltpu.make_async_copy(grad_tok.at[:, cols], tokens_out.at[:, cols], copy_sem.at[2 + quarter])
        copy.start()
        stores.append(copy)

    inputs(0)
    links.arrival("grad_kv", grads.at[1, :, columns])

    def kv_product(k, _):
        product(KV_PIECES, lax.div(k, 4), lax.rem(k, 4))
        return 0

    lax.fori_loop(0, 16, kv_product, 0)
    for n in KV_PIECES:
        send_far(n)
    for d, by in enumerate((1, -1)):
        for n in KV_PIECES:
            send_near(n, d, by)
    for n in Q_PIECES:
        gathered(n, 0)
    inputs(1)
    for c in range(4):
        for n in KV_PIECES:
            relay(n, c)
        if c < 3:
            for n in Q_PIECES:
                gathered(n, c + 1)
    inputs(2)
    for n in Q_PIECES:
        second(n)
    inputs(3)
    for n in Q_PIECES:
        third(n)
    for c in range(4):
        for n in KV_PIECES:
            gathered(n, c)
    for n in Q_PIECES:
        last(n)
    for step in (second, third, last):
        for n in KV_PIECES:
            step(n)
    for copy in stores:
        copy.wait()
    links.finish()


def scatter_grads(turned, w_all, grad_q, terms, cos_table, sin_table):
    vmem, anywhere = pl.BlockSpec(memory_space=pltpu.VMEM), pl.BlockSpec(memory_space=pl.ANY)
    shape = jax.ShapeDtypeStruct
    buffers = []
    for _, _, rows, _, cols, _ in PIECES:
        tile = (rows // 2, cols)
        for lead in (
            (4, 2, 4, 4), (4, 2, 4), (4, 2), (2, 4, 4), (2, 4), (2, 2, 4, 4), (2, 2, 4), (3, 2), (1,),
        ):
            buffers.append(pltpu.VMEM(lead + tile, BF16))
    return pl.pallas_call(
        scatter_kernel,
        out_shape=(shape((256, 8192), BF16), shape((64, 768), F32)),
        in_specs=[anywhere, anywhere, vmem, vmem, vmem, vmem],
        out_specs=(anywhere, vmem),
        scratch_shapes=[
            pltpu.VMEM((8, 512, 512), BF16),
            pltpu.VMEM((3, 2, 4, 2, 2, 4, 64, 256), BF16),
            pltpu.VMEM((2, 256, 768), BF16),
            pltpu.VMEM((7, 256, 256), BF16),
            pltpu.VMEM((256, 8192), BF16),
            pltpu.SemaphoreType.DMA((6,)),
            pltpu.SemaphoreType.DMA((176,)),
            pltpu.SemaphoreType.DMA((176,)),
            *buffers,
        ],
        compiler_params=pltpu.CompilerParams(
            collective_id=1, has_side_effects=True, vmem_limit_bytes=56 * 2**20
        ),
        name="scatter_grads",
    )(turned, w_all, grad_q, terms, cos_table, sin_table)


def rope_tables(positions_in, head_dim):
    half_width = head_dim // 2
    exponent = jnp.arange(half_width).astype(F32) * (2.0 / head_dim)
    frequency = jnp.power(ROPE_BASE, -exponent)
    angles = positions_in.astype(F32)[:, None] * frequency[None, :]
    cos, sin = jnp.cos(angles), jnp.sin(angles)
    return jnp.concatenate([cos, cos], axis=1), jnp.concatenate([-sin, sin], axis=1)


def body(tokens, positions, query_weight, key_weight, value_weight, grad_output):
    own_positions = lax.dynamic_slice_in_dim(positions, lax.axis_index("ctx") * 256, 256)
    cos_table, sin_table = rope_tables(own_positions, 128)
    w_all, turned, q, kv = gather_weights(
        tokens[0], query_weight, key_weight, value_weight, cos_table, sin_table
    )
    attention, grad_q, terms = attend(
        positions, own_positions[None], q, kv, grad_output[0], cos_table, sin_table
    )
    grad_tokens, grads = scatter_grads(turned, w_all, grad_q, terms, cos_table, sin_table)
    return attention[None], grad_tokens[None], grads[:, :512], grads[:, 512:640], grads[:, 640:]


def solution(mesh):
    in_specs = (
        P("dp", "ctx", None),
        P(),
        P(("dp", "ctx"), None),
        P(("dp", "ctx"), None),
        P(("dp", "ctx"), None),
        P("dp", "ctx", None),
    )
    out_specs = (
        P("dp", "ctx", None),
        P("dp", "ctx", None),
        P(("dp", "ctx"), None),
        P(("dp", "ctx"), None),
        P(("dp", "ctx"), None),
    )
    return jax.shard_map(body, mesh=mesh, in_specs=in_specs, out_specs=out_specs, check_vma=False)
```

```python
import functools

import jax
import jax.numpy as jnp
from jax import lax
from jax.experimental import pallas as pl
from jax.experimental.pallas import tpu as pltpu
from jax.sharding import PartitionSpec as P

ROPE_BASE = 1000000.0
MASKED = -1e30
MESH = pl.DeviceIdType.MESH
BF16 = jnp.bfloat16
F32 = jnp.float32
AXES = ("x", "y", "z")
PIECES = (
    (2, 0, 64, 0, 128, ("y", "x", "z")),
    (2, 0, 32, 128, 128, ("z", "y", "x")),
    (2, 32, 32, 128, 128, ("z", "x", "y")),
    (0, 0, 64, 0, 256, ("z", "y", "x")),
    (1, 0, 64, 0, 256, ("z", "x", "y")),
)
KV_PIECES = (0, 1, 2)
Q_PIECES = (3, 4)
SCALE = 128 ** (-0.5)
LOG2E = 1.4426950408889634


def place():
    dp, ctx = lax.axis_index("dp"), lax.axis_index("ctx")
    return {
        "x": lax.div(dp, 8) * 2 + lax.div(ctx, 4),
        "y": lax.rem(lax.div(dp, 2), 4),
        "z": lax.rem(ctx, 4),
        "core": lax.rem(dp, 2),
    }


def device(at):
    return (
        lax.div(at["x"], 2) * 8 + at["y"] * 2 + at["core"],
        lax.rem(at["x"], 2) * 4 + at["z"],
    )


def moved(at, axis, by):
    return {**at, axis: lax.rem(at[axis] + 4 + by, 4)}


def sibling(at):
    return {**at, "core": 1 - at["core"]}


def greet(targets):
    barrier = pltpu.get_barrier_semaphore()
    for target in targets:
        pl.semaphore_signal(barrier, inc=1, device_id=target, device_id_type=MESH)
    pl.semaphore_wait(barrier, len(targets))


def partners(at):
    near = [device(moved(at, axis, by)) for axis in AXES for by in (1, -1, 2)]
    return near + [device(sibling(at))] + ctx_peers()


def ctx_peers():
    dp, ctx = lax.axis_index("dp"), lax.axis_index("ctx")
    return [(dp, lax.rem(ctx + k, 8)) for k in range(1, 8)]


def remote(src, dst, send, recv, target):
    return pltpu.make_async_remote_copy(
        src_ref=src, dst_ref=dst, send_sem=send, recv_sem=recv, device_id=target, device_id_type=MESH
    )


class Links:
    def __init__(self, send, recv, twin):
        self.send, self.recv, self.twin = send, recv, twin
        self.slots, self.started = {}, []

    def slot(self, key):
        return self.slots.setdefault(key, len(self.slots))

    def launch(self, key, src, dst, target):
        k = self.slot(key)
        copy = remote(src, dst, self.send.at[k], self.recv.at[k], target)
        copy.start()
        self.started.append(copy)

    def arrival(self, key, ref):
        k = self.slot(key)
        remote(ref, ref, self.send.at[k], self.recv.at[k], self.twin).wait_recv()

    def finish(self):
        for copy in self.started:
            copy.wait_send()


def turn_half(a):
    return pltpu.roll(a, 64, 1)


BYS = (2, 1, -1)


def gather_kernel(
    tokens, wq_hbm, wk_hbm, wv_hbm, tables_hbm,
    w_out, turned_out, q_out, kv_out,
    w, tok, twin_tok, turned, wq, wk, wv, tables, sums, copy_sem, send, recv,
):
    me = place()
    core = me["core"]
    twin = device(sibling(me))
    links = Links(send, recv, twin)
    loads = [
        pltpu.make_async_copy(src, dst, copy_sem.at[k])
        for k, (src, dst) in enumerate(
            ((wq_hbm, wq), (wk_hbm, wk), (wv_hbm, wv), (tables_hbm, tables), (tokens, tok))
        )
    ]
    for copy in loads:
        copy.start()
    for copy in loads[:3]:
        copy.wait()
    x_hi, x_lo = lax.div(me["x"], 2), lax.rem(me["x"], 2)
    w[2, x_hi, me["y"], core, x_lo, me["z"], :, 0:128] = wk[...].astype(BF16)
    w[2, x_hi, me["y"], core, x_lo, me["z"], :, 128:256] = wv[...].astype(BF16)
    w[0, x_hi, me["y"], core, x_lo, me["z"]] = wq[:, 0:256].astype(BF16)
    w[1, x_hi, me["y"], core, x_lo, me["z"]] = wq[:, 256:512].astype(BF16)

    def block(n, first, second, third, core_at=core):
        part, row, rows, col, cols, order = PIECES[n]
        at = dict(zip(order, (first, second, third)))
        x, y, z = (at[axis] for axis in AXES)
        return w.at[
            part,
            slice(None) if x is None else lax.div(x, 2),
            slice(None) if y is None else y,
            core_at,
            slice(None) if x is None else lax.rem(x, 2),
            slice(None) if z is None else z,
            pl.ds(row, rows),
            pl.ds(col, cols),
        ]

    def to(n, phase, by):
        return device(moved(me, PIECES[n][5][phase], by))

    def index(n, phase, by=0):
        axis = PIECES[n][5][phase]
        return moved(me, axis, by)[axis]

    greet(partners(me))
    everything = KV_PIECES + Q_PIECES
    for n in everything:
        mine = block(n, index(n, 0), index(n, 1), index(n, 2))
        for by in BYS:
            links.launch((n, 0, by), mine, mine, to(n, 0, by))
    for k in range(8):
        columns = tokens.at[:, pl.ds(pl.multiple_of(k * 1024 + (1 - core) * 512, 512), 512)]
        links.launch(("tokens", k), columns, twin_tok.at[k], twin)

    def send_chunk(n, c):
        chunk = block(n, None, index(n, 1, c), index(n, 2))
        for by in BYS:
            links.launch((n, 2, c, by), chunk, chunk, to(n, 2, by))

    for n in everything:
        second, third = index(n, 1), index(n, 2)
        for by in BYS:
            links.arrival((n, 0, by), block(n, index(n, 0, -by), second, third))
        line = block(n, None, second, third)
        for by in BYS:
            links.launch((n, 1, by), line, line, to(n, 1, by))
        send_chunk(n, 0)
    for n in everything:
        for by in BYS:
            links.arrival((n, 1, by), block(n, None, index(n, 1, -by), index(n, 2)))
            send_chunk(n, -by)

    CHUNKS = (0,) + tuple(-by for by in BYS)

    def chunk_in(n, c):
        second = index(n, 1, c)
        for by in BYS:
            links.arrival((n, 2, c, by), block(n, None, second, index(n, 2, -by)))
        whole = block(n, None, second, None)
        links.launch((n, "twin", c), whole, whole, twin)

    def twin_in(n, c):
        links.arrival((n, "twin", c), block(n, None, index(n, 1, c), None, 1 - core))

    for copy in loads[3:]:
        copy.wait()
    for k in range(8):
        links.arrival(("tokens", k), twin_tok.at[k])

    def turn(k, _):
        at = pl.multiple_of(k * 1024 + core * 512, 512)
        turned[k, :, 0:256] = tok[:, pl.ds(at, 512)].T
        turned[k, :, 256:512] = twin_tok[k].T
        return 0

    lax.fori_loop(0, 4, turn, 0)
    keep = []

    def store(k, src, dst):
        copy = pltpu.make_async_copy(src, dst, copy_sem.at[k])
        copy.start()
        keep.append(copy)

    for c in CHUNKS:
        for n in KV_PIECES:
            chunk_in(n, c)
    for c in CHUNKS:
        for n in KV_PIECES:
            twin_in(n, c)
    store(5, w.at[2], w_out.at[2])

    def add_kv(k, total):
        lhs = tok[:, pl.ds(pl.multiple_of(k * 2048, 2048), 2048)]
        rows = w[2, lax.div(k, 2), pl.ds(lax.rem(k, 2) * 2, 2)].reshape(2048, 256)
        return total + jnp.dot(lhs, rows, preferred_element_type=F32)

    both = lax.fori_loop(0, 4, add_kv, jnp.zeros((256, 256), F32))
    cos, sin = tables[0], tables[1]
    ctx = lax.axis_index("ctx")
    key = both[:, 0:128]
    kv_out[ctx, :, 0:128] = (key * cos + turn_half(key) * sin).astype(BF16)
    kv_out[ctx, :, 128:256] = both[:, 128:256].astype(BF16)
    peers = ctx_peers()
    for k in (4, 2, 6, 1, 3, 5, 7):
        links.launch(("kv", k), kv_out.at[ctx], kv_out.at[ctx], peers[k - 1])

    def project(c):
        y = index(3, 1, c)
        total = None
        for x_hi in range(2):
            lhs = tok[:, pl.ds(pl.multiple_of((x_hi * 4 + y) * 1024, 1024), 1024)]
            term = jnp.dot(lhs, w[0, x_hi, y].reshape(1024, 256), preferred_element_type=F32)
            total = term if total is None else total + term
        sums[0] = total if c == CHUNKS[0] else sums[0] + total
        x = index(4, 1, c)
        x_hi, x_lo = lax.div(x, 2), lax.rem(x, 2)
        total = None
        for y in range(4):
            for half in range(2):
                at = (x_hi * 4 + y) * 1024 + half * 512 + x_lo * 256
                lhs = tok[:, pl.ds(pl.multiple_of(at, 256), 256)]
                rows = w[1, x_hi, y, half, x_lo].reshape(256, 256)
                term = jnp.dot(lhs, rows, preferred_element_type=F32)
                total = term if total is None else total + term
        sums[1] = total if c == CHUNKS[0] else sums[1] + total

    def finish_chunk(c):
        for n in Q_PIECES:
            twin_in(n, c)
        k = CHUNKS.index(c)
        y = index(3, 1, c)
        store(6 + k, w.at[0, :, y], w_out.at[0, :, y])
        x = index(4, 1, c)
        x_hi, x_lo = lax.div(x, 2), lax.rem(x, 2)
        store(10 + k, w.at[1, x_hi, :, :, x_lo], w_out.at[1, x_hi, :, :, x_lo])
        project(c)

    for n in Q_PIECES:
        chunk_in(n, CHUNKS[0])
    lax.fori_loop(4, 8, turn, 0)
    store(14, turned, turned_out)
    for k in range(1, 4):
        for n in Q_PIECES:
            chunk_in(n, CHUNKS[k])
        finish_chunk(CHUNKS[k - 1])
    finish_chunk(CHUNKS[3])
    for part in range(2):
        for h in range(2):
            query = sums[part, :, h * 128 : h * 128 + 128]
            rotated = (query * cos + turn_half(query) * sin).astype(BF16)
            q_out[:, part * 256 + h * 128 : part * 256 + h * 128 + 128] = rotated
    for k in range(1, 8):
        links.arrival(("kv", k), kv_out.at[lax.rem(ctx + 8 - k, 8)])
    for copy in keep:
        copy.wait()
    links.finish()


def gather_weights(tokens, wq, wk, wv, tables):
    vmem, anywhere = pl.BlockSpec(memory_space=pltpu.VMEM), pl.BlockSpec(memory_space=pl.ANY)
    shape = jax.ShapeDtypeStruct
    return pl.pallas_call(
        gather_kernel,
        out_shape=(
            shape((3, 2, 4, 2, 2, 4, 64, 256), BF16),
            shape((8, 512, 512), BF16),
            shape((256, 512), BF16),
            shape((8, 256, 256), BF16),
        ),
        in_specs=[anywhere] * 5,
        out_specs=(anywhere, anywhere, vmem, vmem),
        scratch_shapes=[
            pltpu.VMEM((3, 2, 4, 2, 2, 4, 64, 256), BF16),
            pltpu.VMEM((256, 8192), BF16),
            pltpu.VMEM((8, 256, 512), BF16),
            pltpu.VMEM((8, 512, 512), BF16),
            pltpu.VMEM((64, 512), F32),
            pltpu.VMEM((64, 128), F32),
            pltpu.VMEM((64, 128), F32),
            pltpu.VMEM((2, 256, 128), F32),
            pltpu.VMEM((2, 256, 256), F32),
            pltpu.SemaphoreType.DMA((15,)),
            pltpu.SemaphoreType.DMA((128,)),
            pltpu.SemaphoreType.DMA((128,)),
        ],
        compiler_params=pltpu.CompilerParams(
            collective_id=0, has_side_effects=True, vmem_limit_bytes=60 * 2**20
        ),
        name="gather_weights",
    )(tokens, wq, wk, wv, tables)


def attention_kernel(
    positions, own_positions, q, kv, grad, tables,
    attention, grad_q, terms,
    qs, gs, gs_t, keys_t, values_t, scores, top, total, att_t, gq_t,
):
    for h in range(4):
        rows = slice(h * 256, h * 256 + 256)
        qs[rows] = q[:, h * 128 : h * 128 + 128]
        gs[rows] = grad[:, h * 128 : h * 128 + 128]
        gs_t[:, rows] = grad[:, h * 128 : h * 128 + 128].T
    for k in range(8):
        cols = slice(k * 256, k * 256 + 256)
        keys_t[:, cols] = kv[k, :, 0:128].T
        values_t[:, cols] = kv[k, :, 128:256].T
    nt = (((1,), (1,)), ((), ()))
    lead = own_positions[...] - lax.broadcasted_iota(jnp.int32, (128, 256), 0)
    top[...] = jnp.full(top.shape, MASKED, F32)

    def score(k, _):
        for h in range(4):
            cols = slice(h * 256, h * 256 + 256)
            s = lax.dot_general(kv[k, :, 0:128], qs[cols], nt, preferred_element_type=F32)
            upper = jnp.where(lead >= positions[k * 256], s[0:128], MASKED)
            lower = jnp.where(lead >= positions[k * 256 + 128], s[128:256], MASKED)
            scores[k, 0:128, cols] = upper
            scores[k, 128:256, cols] = lower
            high = jnp.max(jnp.maximum(upper, lower), axis=0, keepdims=True)
            top[:, cols] = jnp.maximum(top[:, cols], high)
        return 0

    lax.fori_loop(0, 8, score, 0)
    total[...] = jnp.zeros(total.shape, F32)
    att_t[...] = jnp.zeros(att_t.shape, F32)

    def weigh(k, _):
        at = pl.ds(pl.multiple_of(k * 256, 256), 256)
        for h in range(4):
            cols = slice(h * 256, h * 256 + 256)
            weight = jnp.exp2((scores[k, :, cols] - top[:, cols]) * (SCALE * LOG2E))
            scores[k, :, cols] = weight
            total[:, cols] += jnp.sum(weight, axis=0, keepdims=True)
            att_t[:, cols] += jnp.dot(values_t[:, at], weight.astype(BF16), preferred_element_type=F32)
        return 0

    lax.fori_loop(0, 8, weigh, 0)
    for h in range(4):
        cols = slice(h * 256, h * 256 + 256)
        inverse = 1.0 / total[:, cols]
        out = (att_t[:, cols] / total[:, cols]).astype(BF16)
        attention[:, h * 128 : h * 128 + 128] = out.T
        total[:, cols] = inverse
        top[:, cols] = jnp.sum(gs_t[:, cols].astype(F32) * out.astype(F32), axis=0, keepdims=True)
    gq_t[...] = jnp.zeros(gq_t.shape, F32)

    def back(k, _):
        at = pl.ds(pl.multiple_of(k * 256, 256), 256)
        key_term = jnp.zeros((256, 128), F32)
        value_term = jnp.zeros((256, 128), F32)
        for h in range(4):
            cols = slice(h * 256, h * 256 + 256)
            probs = scores[k, :, cols] * total[:, cols]
            grad_probs = lax.dot_general(kv[k, :, 128:256], gs[cols], nt, preferred_element_type=F32)
            dscore = (probs * (grad_probs - top[:, cols])).astype(BF16)
            key_term += jnp.dot(dscore, qs[cols], preferred_element_type=F32)
            value_term += jnp.dot(probs.astype(BF16), gs[cols], preferred_element_type=F32)
            gq_t[:, cols] += jnp.dot(keys_t[:, at], dscore, preferred_element_type=F32)
        terms[k, :, 0:128] = (key_term * SCALE).astype(BF16)
        terms[k, :, 128:256] = value_term.astype(BF16)
        return 0

    lax.fori_loop(0, 8, back, 0)
    for h in range(4):
        a = gq_t[:, h * 256 : h * 256 + 256].T * SCALE
        unrotated = a * tables[0] - turn_half(a) * tables[1]
        grad_q[:, h * 128 : h * 128 + 128] = unrotated.astype(BF16)


def attend(positions, own_positions, q, kv, grad, tables):
    vmem = pl.BlockSpec(memory_space=pltpu.VMEM)
    shape = jax.ShapeDtypeStruct
    return pl.pallas_call(
        attention_kernel,
        out_shape=(shape((256, 512), BF16), shape((256, 512), BF16), shape((8, 256, 256), BF16)),
        in_specs=[pl.BlockSpec(memory_space=pltpu.SMEM)] + [vmem] * 5,
        out_specs=(vmem, vmem, vmem),
        scratch_shapes=[
            pltpu.VMEM((1024, 128), BF16),
            pltpu.VMEM((1024, 128), BF16),
            pltpu.VMEM((128, 1024), BF16),
            pltpu.VMEM((128, 2048), BF16),
            pltpu.VMEM((128, 2048), BF16),
            pltpu.VMEM((8, 256, 1024), F32),
            pltpu.VMEM((1, 1024), F32),
            pltpu.VMEM((1, 1024), F32),
            pltpu.VMEM((128, 1024), F32),
            pltpu.VMEM((128, 1024), F32),
        ],
        compiler_params=pltpu.CompilerParams(vmem_limit_bytes=32 * 2**20),
        name="attend",
    )(positions, own_positions, q, kv, grad, tables)


def scatter_kernel(
    turned, w_all, grad_q, terms, tables,
    tokens_out, out,
    held, w, grads, landed, grad_tok, copy_sem, send, recv, *buffers,
):
    me = place()
    core = me["core"]
    ctx = lax.axis_index("ctx")
    twin = device(sibling(me))
    links = Links(send, recv, twin)
    accs = [buffers[6 * n : 6 * n + 3] for n in range(len(PIECES))]
    ends = [buffers[6 * n + 3 : 6 * n + 6] for n in range(len(PIECES))]
    load = pltpu.make_async_copy(turned, held, copy_sem.at[0])
    load.start()
    load_w = pltpu.make_async_copy(w_all, w, copy_sem.at[1])
    load_w.start()
    greet(partners(me))
    links.launch("grad_q", grad_q, grads.at[1, :, pl.ds(0, 512)], twin)
    peers = ctx_peers()
    for k in (4, 2, 6, 1, 3, 5, 7):
        links.launch(("kv", k), terms.at[lax.rem(ctx + k, 8)], landed.at[k - 1], peers[k - 1])
    grads[0, :, 0:512] = grad_q[...]
    load.wait()
    links.arrival("grad_q", grads.at[1, :, pl.ds(0, 512)])

    def axes(n):
        return tuple(reversed(PIECES[n][5]))

    def to(n, phase, by):
        return device(moved(me, axes(n)[phase], by))

    def at(n, phase, by=0):
        axis = axes(n)[phase]
        return moved(me, axis, by)[axis]

    def product(pieces, x, y):
        part = PIECES[pieces[0]][0]
        k = lax.div(x, 2) * 4 + y
        lhs = held[k, pl.ds(pl.multiple_of(lax.rem(x, 2) * 256, 256), 256)]
        rhs = grads[:, :, part * 256 : part * 256 + 256].reshape(512, 256)
        term = jnp.dot(lhs, rhs, preferred_element_type=F32).astype(BF16)
        for n in pieces:
            _, row, rows, col, cols, _ = PIECES[n]
            for z in range(4):
                first, second, third = ({"x": x, "y": y, "z": z}[axis] for axis in axes(n))
                start = z * 64 + row
                accs[n][0][first, second, third] = term[start : start + rows, col : col + cols]

    CHUNKS = (2, 1, -1, 0)

    def products(n, c):
        axis, other = axes(n)[:2]
        j = at(n, 1, c)

        def one(i, _):
            where = {axis: i, other: j}
            product((n,), where["x"], where["y"])
            return 0

        lax.fori_loop(0, 4, one, 0)

    def send_chunk(n, c):
        j = at(n, 1, c)
        for s, by in enumerate(BYS):
            links.launch((n, 0, c, s), accs[n][0].at[at(n, 0, by), j], ends[n][0].at[s, j], to(n, 0, by))

    def summed(n, phase, index):
        lead = (at(n, phase),) + index
        total = accs[n][phase][lead].astype(F32)
        for s in range(3):
            total = total + ends[n][phase][(s,) + index].astype(F32)
        return total

    def chunk_in(n, c):
        j = at(n, 1, c)
        for s in range(3):
            links.arrival((n, 0, c, s), ends[n][0].at[s, j])
        accs[n][1][j] = summed(n, 0, (j,)).astype(BF16)
        if c != 0:
            s = BYS.index(c)
            links.launch((n, 1, s), accs[n][1].at[j], ends[n][1].at[s], to(n, 1, c))

    def second(n):
        for s in range(3):
            links.arrival((n, 1, s), ends[n][1].at[s])
        accs[n][2][...] = summed(n, 1, ()).astype(BF16)
        for s, by in enumerate(BYS):
            links.launch((n, 2, s), accs[n][2].at[at(n, 2, by)], ends[n][2].at[s], to(n, 2, by))

    def last(n):
        part, row, rows, col, cols, _ = PIECES[n]
        for s in range(3):
            links.arrival((n, 2, s), ends[n][2].at[s])
        out[row : row + rows, part * 256 + col : part * 256 + col + cols] = summed(n, 2, ())

    for c in CHUNKS:
        for n in Q_PIECES:
            products(n, c)
            send_chunk(n, c)

    load_w.wait()

    def input_slice(k, _):
        total = None
        for part in range(3):
            lhs = grads[0, :, part * 256 : part * 256 + 256]
            rows = w[part, lax.div(k, 8), lax.rem(lax.div(k, 2), 4), lax.rem(k, 2)].reshape(512, 256)
            term = lax.dot_general(lhs, rows, (((1,), (1,)), ((), ())), preferred_element_type=F32)
            total = term if total is None else total + term
        grad_tok[:, pl.ds(pl.multiple_of(k * 512, 512), 512)] = total.astype(BF16)
        return 0

    stores = []

    def inputs(quarter):
        lax.fori_loop(quarter * 4, quarter * 4 + 4, input_slice, 0)
        cols = pl.ds(quarter * 2048, 2048)
        copy = pltpu.make_async_copy(grad_tok.at[:, cols], tokens_out.at[:, cols], copy_sem.at[2 + quarter])
        copy.start()
        stores.append(copy)

    for k in range(1, 8):
        links.arrival(("kv", k), landed.at[k - 1])
    keyval = terms[ctx].astype(F32)
    for k in range(7):
        keyval = keyval + landed[k].astype(F32)
    key = keyval[:, 0:128]
    grads[0, :, 512:640] = (key * tables[0] - turn_half(key) * tables[1]).astype(BF16)
    grads[0, :, 640:768] = keyval[:, 128:256].astype(BF16)
    columns = pl.ds(512, 256)
    links.launch("grad_kv", grads.at[0, :, columns], grads.at[1, :, columns], twin)
    inputs(0)
    links.arrival("grad_kv", grads.at[1, :, columns])

    def kv_product(k, _):
        product(KV_PIECES, lax.div(k, 4), lax.rem(k, 4))
        return 0

    lax.fori_loop(0, 16, kv_product, 0)
    for c in CHUNKS:
        for n in KV_PIECES:
            send_chunk(n, c)
    for k, c in enumerate(CHUNKS):
        for n in Q_PIECES:
            chunk_in(n, c)
        if k < 3:
            inputs(k + 1)
    for c in CHUNKS:
        for n in KV_PIECES:
            chunk_in(n, c)
    for step in (second, last):
        for n in Q_PIECES + KV_PIECES:
            step(n)
    for copy in stores:
        copy.wait()
    links.finish()


def scatter_grads(turned, w_all, grad_q, terms, tables):
    vmem, anywhere = pl.BlockSpec(memory_space=pltpu.VMEM), pl.BlockSpec(memory_space=pl.ANY)
    shape = jax.ShapeDtypeStruct
    buffers = []
    for _, _, rows, _, cols, _ in PIECES:
        for lead in ((4, 4, 4), (4, 4), (4,), (3, 4, 4), (3, 4), (3,)):
            buffers.append(pltpu.VMEM(lead + (rows, cols), BF16))
    return pl.pallas_call(
        scatter_kernel,
        out_shape=(shape((256, 8192), BF16), shape((64, 768), F32)),
        in_specs=[anywhere, anywhere, vmem, vmem, vmem],
        out_specs=(anywhere, vmem),
        scratch_shapes=[
            pltpu.VMEM((8, 512, 512), BF16),
            pltpu.VMEM((3, 2, 4, 2, 2, 4, 64, 256), BF16),
            pltpu.VMEM((2, 256, 768), BF16),
            pltpu.VMEM((7, 256, 256), BF16),
            pltpu.VMEM((256, 8192), BF16),
            pltpu.SemaphoreType.DMA((6,)),
            pltpu.SemaphoreType.DMA((100,)),
            pltpu.SemaphoreType.DMA((100,)),
            *buffers,
        ],
        compiler_params=pltpu.CompilerParams(
            collective_id=1, has_side_effects=True, vmem_limit_bytes=48 * 2**20
        ),
        name="scatter_grads",
    )(turned, w_all, grad_q, terms, tables)


def rope_tables(positions_in, head_dim):
    half_width = head_dim // 2
    exponent = jnp.arange(half_width).astype(F32) * (2.0 / head_dim)
    frequency = jnp.power(ROPE_BASE, -exponent)
    angles = positions_in.astype(F32)[:, None] * frequency[None, :]
    cos, sin = jnp.cos(angles), jnp.sin(angles)
    return jnp.stack([jnp.concatenate([cos, cos], axis=1), jnp.concatenate([-sin, sin], axis=1)])


def body(tokens, positions, query_weight, key_weight, value_weight, grad_output):
    own_positions = lax.dynamic_slice_in_dim(positions, lax.axis_index("ctx") * 256, 256)
    tables = rope_tables(own_positions, 128)
    w_all, turned, q, kv = gather_weights(
        tokens[0], query_weight, key_weight, value_weight, tables
    )
    attention, grad_q, terms = attend(
        positions, own_positions[None], q, kv, grad_output[0], tables
    )
    grad_tokens, grads = scatter_grads(turned, w_all, grad_q, terms, tables)
    return attention[None], grad_tokens[None], grads[:, :512], grads[:, 512:640], grads[:, 640:]


def solution(mesh):
    in_specs = (
        P("dp", "ctx", None),
        P(),
        P(("dp", "ctx"), None),
        P(("dp", "ctx"), None),
        P(("dp", "ctx"), None),
        P("dp", "ctx", None),
    )
    out_specs = (
        P("dp", "ctx", None),
        P("dp", "ctx", None),
        P(("dp", "ctx"), None),
        P(("dp", "ctx"), None),
        P(("dp", "ctx"), None),
    )
    return jax.shard_map(body, mesh=mesh, in_specs=in_specs, out_specs=out_specs, check_vma=False)
```

```python
import functools

import jax
import jax.numpy as jnp
from jax import lax
from jax.experimental import pallas as pl
from jax.experimental.pallas import tpu as pltpu
from jax.sharding import PartitionSpec as P

ROPE_BASE = 1000000.0
MASKED = -1e30
MESH = pl.DeviceIdType.MESH
BF16 = jnp.bfloat16
F32 = jnp.float32
AXES = ("x", "y", "z")
PIECES = (
    (2, 0, 64, 0, 128, ("y", "x", "z")),
    (2, 0, 32, 128, 128, ("z", "y", "x")),
    (2, 32, 32, 128, 128, ("z", "x", "y")),
    (0, 0, 64, 0, 256, ("z", "y", "x")),
    (1, 0, 64, 0, 256, ("z", "x", "y")),
)
KV_PIECES = (0, 1, 2)
Q_PIECES = (3, 4)
SCALE = 128 ** (-0.5)
LOG2E = 1.4426950408889634


def place():
    dp, ctx = lax.axis_index("dp"), lax.axis_index("ctx")
    return {
        "x": lax.div(dp, 8) * 2 + lax.div(ctx, 4),
        "y": lax.rem(lax.div(dp, 2), 4),
        "z": lax.rem(ctx, 4),
        "core": lax.rem(dp, 2),
    }


def device(at):
    return (
        lax.div(at["x"], 2) * 8 + at["y"] * 2 + at["core"],
        lax.rem(at["x"], 2) * 4 + at["z"],
    )


def moved(at, axis, by):
    return {**at, axis: lax.rem(at[axis] + 4 + by, 4)}


def sibling(at):
    return {**at, "core": 1 - at["core"]}


def greet(targets):
    barrier = pltpu.get_barrier_semaphore()
    for target in targets:
        pl.semaphore_signal(barrier, inc=1, device_id=target, device_id_type=MESH)
    pl.semaphore_wait(barrier, len(targets))


def partners(at):
    near = [device(moved(at, axis, by)) for axis in AXES for by in (1, -1, 2)]
    return near + [device(sibling(at))] + ctx_peers()


def ctx_peers():
    dp, ctx = lax.axis_index("dp"), lax.axis_index("ctx")
    return [(dp, lax.rem(ctx + k, 8)) for k in range(1, 8)]


def remote(src, dst, send, recv, target):
    return pltpu.make_async_remote_copy(
        src_ref=src, dst_ref=dst, send_sem=send, recv_sem=recv, device_id=target, device_id_type=MESH
    )


class Links:
    def __init__(self, send, recv, twin):
        self.send, self.recv, self.twin = send, recv, twin
        self.slots, self.started = {}, []

    def slot(self, key):
        return self.slots.setdefault(key, len(self.slots))

    def launch(self, key, src, dst, target):
        k = self.slot(key)
        copy = remote(src, dst, self.send.at[k], self.recv.at[k], target)
        copy.start()
        self.started.append(copy)

    def arrival(self, key, ref):
        k = self.slot(key)
        remote(ref, ref, self.send.at[k], self.recv.at[k], self.twin).wait_recv()

    def finish(self):
        for copy in self.started:
            copy.wait_send()


def turn_half(a):
    return pltpu.roll(a, 64, 1)


BYS = (2, 1, -1)


def gather_kernel(
    tokens, wq_hbm, wk_hbm, wv_hbm, tables_hbm,
    w_out, turned_out, q_out, kv_out,
    w, tok, twin_tok, turned, wq, wk, wv, tables, sums, copy_sem, send, recv,
):
    me = place()
    core = me["core"]
    twin = device(sibling(me))
    links = Links(send, recv, twin)
    loads = [
        pltpu.make_async_copy(src, dst, copy_sem.at[k])
        for k, (src, dst) in enumerate(
            ((wq_hbm, wq), (wk_hbm, wk), (wv_hbm, wv), (tables_hbm, tables), (tokens, tok))
        )
    ]
    for copy in loads:
        copy.start()
    for copy in loads[:3]:
        copy.wait()
    x_hi, x_lo = lax.div(me["x"], 2), lax.rem(me["x"], 2)
    w[2, x_hi, me["y"], core, x_lo, me["z"], :, 0:128] = wk[...].astype(BF16)
    w[2, x_hi, me["y"], core, x_lo, me["z"], :, 128:256] = wv[...].astype(BF16)
    w[0, x_hi, me["y"], core, x_lo, me["z"]] = wq[:, 0:256].astype(BF16)
    w[1, x_hi, me["y"], core, x_lo, me["z"]] = wq[:, 256:512].astype(BF16)

    def block(n, first, second, third, core_at=core, half=None):
        part, row, rows, col, cols, order = PIECES[n]
        if half is not None:
            rows = rows // 2
            row = row + half * rows
        at = dict(zip(order, (first, second, third)))
        x, y, z = (at[axis] for axis in AXES)
        return w.at[
            part,
            slice(None) if x is None else lax.div(x, 2),
            slice(None) if y is None else y,
            core_at,
            slice(None) if x is None else lax.rem(x, 2),
            slice(None) if z is None else z,
            pl.ds(row, rows),
            pl.ds(col, cols),
        ]

    def to(n, phase, by):
        return device(moved(me, PIECES[n][5][phase], by))

    def index(n, phase, by=0):
        axis = PIECES[n][5][phase]
        return moved(me, axis, by)[axis]

    greet(partners(me))
    everything = KV_PIECES + Q_PIECES
    for n in everything:
        mine = block(n, index(n, 0), index(n, 1), index(n, 2))
        for by in BYS:
            links.launch((n, 0, by), mine, mine, to(n, 0, by))
    for k in range(8):
        columns = tokens.at[:, pl.ds(pl.multiple_of(k * 1024 + (1 - core) * 512, 512), 512)]
        links.launch(("tokens", k), columns, twin_tok.at[k], twin)

    def send_chunk(n, c):
        chunk = block(n, None, index(n, 1, c), index(n, 2))
        for by in (1, -1):
            links.launch((n, 2, c, by), chunk, chunk, to(n, 2, by))

    def pass_on(pieces, c):
        for n in pieces:
            second = index(n, 1, c)
            for half, by in enumerate((1, -1)):
                third = index(n, 2, -by)
                links.arrival((n, 2, c, by), block(n, None, second, third))
                part = block(n, None, second, third, half=half)
                links.launch((n, 3, c, by), part, part, to(n, 2, by))

    for n in everything:
        second, third = index(n, 1), index(n, 2)
        for by in BYS:
            links.arrival((n, 0, by), block(n, index(n, 0, -by), second, third))
        line = block(n, None, second, third)
        for by in BYS:
            links.launch((n, 1, by), line, line, to(n, 1, by))
        send_chunk(n, 0)
    for n in everything:
        for by in BYS:
            links.arrival((n, 1, by), block(n, None, index(n, 1, -by), index(n, 2)))
            send_chunk(n, -by)

    CHUNKS = (0,) + tuple(-by for by in BYS)

    def chunk_in(n, c):
        second = index(n, 1, c)
        for half, by in enumerate((1, -1)):
            links.arrival((n, 3, c, by), block(n, None, second, index(n, 2, 2), half=half))
        whole = block(n, None, second, None)
        links.launch((n, "twin", c), whole, whole, twin)

    def twin_in(n, c):
        links.arrival((n, "twin", c), block(n, None, index(n, 1, c), None, 1 - core))

    for copy in loads[3:]:
        copy.wait()
    for k in range(8):
        links.arrival(("tokens", k), twin_tok.at[k])

    def turn(k, _):
        at = pl.multiple_of(k * 1024 + core * 512, 512)
        turned[k, :, 0:256] = tok[:, pl.ds(at, 512)].T
        turned[k, :, 256:512] = twin_tok[k].T
        return 0

    lax.fori_loop(0, 4, turn, 0)
    keep = []

    def store(k, src, dst):
        copy = pltpu.make_async_copy(src, dst, copy_sem.at[k])
        copy.start()
        keep.append(copy)

    pass_on(KV_PIECES, CHUNKS[0])
    pass_on(Q_PIECES, CHUNKS[0])
    for c in CHUNKS[1:]:
        pass_on(KV_PIECES, c)
    pass_on(Q_PIECES, CHUNKS[1])
    for c in CHUNKS:
        for n in KV_PIECES:
            chunk_in(n, c)
    pass_on(Q_PIECES, CHUNKS[2])
    for c in CHUNKS:
        for n in KV_PIECES:
            twin_in(n, c)
    store(5, w.at[2], w_out.at[2])

    def add_kv(k, total):
        lhs = tok[:, pl.ds(pl.multiple_of(k * 2048, 2048), 2048)]
        rows = w[2, lax.div(k, 2), pl.ds(lax.rem(k, 2) * 2, 2)].reshape(2048, 256)
        return total + jnp.dot(lhs, rows, preferred_element_type=F32)

    both = lax.fori_loop(0, 4, add_kv, jnp.zeros((256, 256), F32))
    cos, sin = tables[0], tables[1]
    ctx = lax.axis_index("ctx")
    key = both[:, 0:128]
    kv_out[ctx, :, 0:128] = (key * cos + turn_half(key) * sin).astype(BF16)
    kv_out[ctx, :, 128:256] = both[:, 128:256].astype(BF16)
    peers = ctx_peers()
    for k in (4, 2, 6, 1, 3, 5, 7):
        links.launch(("kv", k), kv_out.at[ctx], kv_out.at[ctx], peers[k - 1])

    def project(c):
        y = index(3, 1, c)
        total = None
        for x_hi in range(2):
            lhs = tok[:, pl.ds(pl.multiple_of((x_hi * 4 + y) * 1024, 1024), 1024)]
            term = jnp.dot(lhs, w[0, x_hi, y].reshape(1024, 256), preferred_element_type=F32)
            total = term if total is None else total + term
        sums[0] = total if c == CHUNKS[0] else sums[0] + total
        x = index(4, 1, c)
        x_hi, x_lo = lax.div(x, 2), lax.rem(x, 2)
        total = None
        for y in range(4):
            for half in range(2):
                at = (x_hi * 4 + y) * 1024 + half * 512 + x_lo * 256
                lhs = tok[:, pl.ds(pl.multiple_of(at, 256), 256)]
                rows = w[1, x_hi, y, half, x_lo].reshape(256, 256)
                term = jnp.dot(lhs, rows, preferred_element_type=F32)
                total = term if total is None else total + term
        sums[1] = total if c == CHUNKS[0] else sums[1] + total

    def finish_chunk(c):
        for n in Q_PIECES:
            twin_in(n, c)
        k = CHUNKS.index(c)
        y = index(3, 1, c)
        store(6 + k, w.at[0, :, y], w_out.at[0, :, y])
        x = index(4, 1, c)
        x_hi, x_lo = lax.div(x, 2), lax.rem(x, 2)
        store(10 + k, w.at[1, x_hi, :, :, x_lo], w_out.at[1, x_hi, :, :, x_lo])
        project(c)

    pass_on(Q_PIECES, CHUNKS[3])
    for n in Q_PIECES:
        chunk_in(n, CHUNKS[0])
    lax.fori_loop(4, 8, turn, 0)
    store(14, turned, turned_out)
    for k in range(1, 4):
        for n in Q_PIECES:
            chunk_in(n, CHUNKS[k])
        finish_chunk(CHUNKS[k - 1])
    finish_chunk(CHUNKS[3])
    for part in range(2):
        for h in range(2):
            query = sums[part, :, h * 128 : h * 128 + 128]
            rotated = (query * cos + turn_half(query) * sin).astype(BF16)
            q_out[:, part * 256 + h * 128 : part * 256 + h * 128 + 128] = rotated
    for k in range(1, 8):
        links.arrival(("kv", k), kv_out.at[lax.rem(ctx + 8 - k, 8)])
    for copy in keep:
        copy.wait()
    links.finish()


def gather_weights(tokens, wq, wk, wv, tables):
    vmem, anywhere = pl.BlockSpec(memory_space=pltpu.VMEM), pl.BlockSpec(memory_space=pl.ANY)
    shape = jax.ShapeDtypeStruct
    return pl.pallas_call(
        gather_kernel,
        out_shape=(
            shape((3, 2, 4, 2, 2, 4, 64, 256), BF16),
            shape((8, 512, 512), BF16),
            shape((256, 512), BF16),
            shape((8, 256, 256), BF16),
        ),
        in_specs=[anywhere] * 5,
        out_specs=(anywhere, anywhere, vmem, vmem),
        scratch_shapes=[
            pltpu.VMEM((3, 2, 4, 2, 2, 4, 64, 256), BF16),
            pltpu.VMEM((256, 8192), BF16),
            pltpu.VMEM((8, 256, 512), BF16),
            pltpu.VMEM((8, 512, 512), BF16),
            pltpu.VMEM((64, 512), F32),
            pltpu.VMEM((64, 128), F32),
            pltpu.VMEM((64, 128), F32),
            pltpu.VMEM((2, 256, 128), F32),
            pltpu.VMEM((2, 256, 256), F32),
            pltpu.SemaphoreType.DMA((15,)),
            pltpu.SemaphoreType.DMA((148,)),
            pltpu.SemaphoreType.DMA((148,)),
        ],
        compiler_params=pltpu.CompilerParams(
            collective_id=0, has_side_effects=True, vmem_limit_bytes=60 * 2**20
        ),
        name="gather_weights",
    )(tokens, wq, wk, wv, tables)


def attention_kernel(
    positions, own_positions, q, kv, grad, tables,
    attention, grad_q, terms,
    qs, gs, gs_t, keys_t, values_t, scores, top, total, att_t, gq_t,
):
    for h in range(4):
        rows = slice(h * 256, h * 256 + 256)
        qs[rows] = q[:, h * 128 : h * 128 + 128]
        gs[rows] = grad[:, h * 128 : h * 128 + 128]
        gs_t[:, rows] = grad[:, h * 128 : h * 128 + 128].T
    for k in range(8):
        cols = slice(k * 256, k * 256 + 256)
        keys_t[:, cols] = kv[k, :, 0:128].T
        values_t[:, cols] = kv[k, :, 128:256].T
    nt = (((1,), (1,)), ((), ()))
    lead = own_positions[...] - lax.broadcasted_iota(jnp.int32, (128, 256), 0)
    top[...] = jnp.full(top.shape, MASKED, F32)

    def score(k, _):
        for h in range(4):
            cols = slice(h * 256, h * 256 + 256)
            s = lax.dot_general(kv[k, :, 0:128], qs[cols], nt, preferred_element_type=F32)
            upper = jnp.where(lead >= positions[k * 256], s[0:128], MASKED)
            lower = jnp.where(lead >= positions[k * 256 + 128], s[128:256], MASKED)
            scores[k, 0:128, cols] = upper
            scores[k, 128:256, cols] = lower
            high = jnp.max(jnp.maximum(upper, lower), axis=0, keepdims=True)
            top[:, cols] = jnp.maximum(top[:, cols], high)
        return 0

    lax.fori_loop(0, 8, score, 0)
    total[...] = jnp.zeros(total.shape, F32)
    att_t[...] = jnp.zeros(att_t.shape, F32)

    def weigh(k, _):
        at = pl.ds(pl.multiple_of(k * 256, 256), 256)
        for h in range(4):
            cols = slice(h * 256, h * 256 + 256)
            weight = jnp.exp2((scores[k, :, cols] - top[:, cols]) * (SCALE * LOG2E))
            scores[k, :, cols] = weight
            total[:, cols] += jnp.sum(weight, axis=0, keepdims=True)
            att_t[:, cols] += jnp.dot(values_t[:, at], weight.astype(BF16), preferred_element_type=F32)
        return 0

    lax.fori_loop(0, 8, weigh, 0)
    for h in range(4):
        cols = slice(h * 256, h * 256 + 256)
        inverse = 1.0 / total[:, cols]
        out = (att_t[:, cols] / total[:, cols]).astype(BF16)
        attention[:, h * 128 : h * 128 + 128] = out.T
        total[:, cols] = inverse
        top[:, cols] = jnp.sum(gs_t[:, cols].astype(F32) * out.astype(F32), axis=0, keepdims=True)
    gq_t[...] = jnp.zeros(gq_t.shape, F32)

    def back(k, _):
        at = pl.ds(pl.multiple_of(k * 256, 256), 256)
        key_term = jnp.zeros((256, 128), F32)
        value_term = jnp.zeros((256, 128), F32)
        for h in range(4):
            cols = slice(h * 256, h * 256 + 256)
            probs = scores[k, :, cols] * total[:, cols]
            grad_probs = lax.dot_general(kv[k, :, 128:256], gs[cols], nt, preferred_element_type=F32)
            dscore = (probs * (grad_probs - top[:, cols])).astype(BF16)
            key_term += jnp.dot(dscore, qs[cols], preferred_element_type=F32)
            value_term += jnp.dot(probs.astype(BF16), gs[cols], preferred_element_type=F32)
            gq_t[:, cols] += jnp.dot(keys_t[:, at], dscore, preferred_element_type=F32)
        terms[k, :, 0:128] = (key_term * SCALE).astype(BF16)
        terms[k, :, 128:256] = value_term.astype(BF16)
        return 0

    lax.fori_loop(0, 8, back, 0)
    for h in range(4):
        a = gq_t[:, h * 256 : h * 256 + 256].T * SCALE
        unrotated = a * tables[0] - turn_half(a) * tables[1]
        grad_q[:, h * 128 : h * 128 + 128] = unrotated.astype(BF16)


def attend(positions, own_positions, q, kv, grad, tables):
    vmem = pl.BlockSpec(memory_space=pltpu.VMEM)
    shape = jax.ShapeDtypeStruct
    return pl.pallas_call(
        attention_kernel,
        out_shape=(shape((256, 512), BF16), shape((256, 512), BF16), shape((8, 256, 256), BF16)),
        in_specs=[pl.BlockSpec(memory_space=pltpu.SMEM)] + [vmem] * 5,
        out_specs=(vmem, vmem, vmem),
        scratch_shapes=[
            pltpu.VMEM((1024, 128), BF16),
            pltpu.VMEM((1024, 128), BF16),
            pltpu.VMEM((128, 1024), BF16),
            pltpu.VMEM((128, 2048), BF16),
            pltpu.VMEM((128, 2048), BF16),
            pltpu.VMEM((8, 256, 1024), F32),
            pltpu.VMEM((1, 1024), F32),
            pltpu.VMEM((1, 1024), F32),
            pltpu.VMEM((128, 1024), F32),
            pltpu.VMEM((128, 1024), F32),
        ],
        compiler_params=pltpu.CompilerParams(vmem_limit_bytes=32 * 2**20),
        name="attend",
    )(positions, own_positions, q, kv, grad, tables)


def scatter_kernel(
    turned, w_all, grad_q, terms, tables,
    tokens_out, out,
    held, w, grads, landed, grad_tok, copy_sem, send, recv, *buffers,
):
    me = place()
    core = me["core"]
    ctx = lax.axis_index("ctx")
    twin = device(sibling(me))
    links = Links(send, recv, twin)
    accs = [buffers[7 * n : 7 * n + 3] for n in range(len(PIECES))]
    ends = [buffers[7 * n + 3 : 7 * n + 6] for n in range(len(PIECES))]
    vias = [buffers[7 * n + 6] for n in range(len(PIECES))]
    load = pltpu.make_async_copy(turned, held, copy_sem.at[0])
    load.start()
    load_w = pltpu.make_async_copy(w_all, w, copy_sem.at[1])
    load_w.start()
    greet(partners(me))
    links.launch("grad_q", grad_q, grads.at[1, :, pl.ds(0, 512)], twin)
    peers = ctx_peers()
    for k in (4, 2, 6, 1, 3, 5, 7):
        links.launch(("kv", k), terms.at[lax.rem(ctx + k, 8)], landed.at[k - 1], peers[k - 1])
    grads[0, :, 0:512] = grad_q[...]
    load.wait()
    links.arrival("grad_q", grads.at[1, :, pl.ds(0, 512)])

    def axes(n):
        return tuple(reversed(PIECES[n][5]))

    def to(n, phase, by):
        return device(moved(me, axes(n)[phase], by))

    def at(n, phase, by=0):
        axis = axes(n)[phase]
        return moved(me, axis, by)[axis]

    def product(pieces, x, y):
        part = PIECES[pieces[0]][0]
        k = lax.div(x, 2) * 4 + y
        lhs = held[k, pl.ds(pl.multiple_of(lax.rem(x, 2) * 256, 256), 256)]
        rhs = grads[:, :, part * 256 : part * 256 + 256].reshape(512, 256)
        term = jnp.dot(lhs, rhs, preferred_element_type=F32).astype(BF16)
        for n in pieces:
            _, row, rows, col, cols, _ = PIECES[n]
            for z in range(4):
                first, second, third = ({"x": x, "y": y, "z": z}[axis] for axis in axes(n))
                for half in range(2):
                    start = z * 64 + row + half * (rows // 2)
                    accs[n][0][first, half, second, third] = term[
                        start : start + rows // 2, col : col + cols
                    ]

    CHUNKS = (2, 1, -1, 0)

    def products(n, c):
        axis, other = axes(n)[:2]
        j = at(n, 1, c)

        def one(i, _):
            where = {axis: i, other: j}
            product((n,), where["x"], where["y"])
            return 0

        lax.fori_loop(0, 4, one, 0)

    def send_far(n, c):
        j = at(n, 1, c)
        for d, by in enumerate((1, -1)):
            src = accs[n][0].at[at(n, 0, 2), d, j]
            links.launch((n, "via", c, d), src, vias[n].at[d, j], to(n, 0, by))

    def send_near(n, c):
        j = at(n, 1, c)
        for d, by in enumerate((1, -1)):
            src = accs[n][0].at[at(n, 0, by), 1 - d, j]
            links.launch((n, "end", c, d, 1 - d), src, ends[n][0].at[d, 1 - d, j], to(n, 0, by))

    def relay(n, c):
        j = at(n, 1, c)
        acc, via, end = accs[n][0], vias[n], ends[n][0]
        for d, by in enumerate((1, -1)):
            links.arrival((n, "via", c, d), via.at[d, j])
            i = at(n, 0, by)
            acc[i, d, j] = (acc[i, d, j].astype(F32) + via[d, j].astype(F32)).astype(BF16)
            links.launch((n, "end", c, d, d), acc.at[i, d, j], end.at[d, d, j], to(n, 0, by))

    def chunk_in(n, c):
        j = at(n, 1, c)
        acc, end = accs[n][0], ends[n][0]
        rows = PIECES[n][2] // 2
        for h in range(2):
            for d in range(2):
                links.arrival((n, "end", c, d, h), end.at[d, h, j])
            total = acc[at(n, 0), h, j].astype(F32)
            total = total + end[0, h, j].astype(F32) + end[1, h, j].astype(F32)
            accs[n][1][j, :, h * rows : h * rows + rows] = total.astype(BF16)
        if c != 0:
            s = BYS.index(c)
            links.launch((n, 1, s), accs[n][1].at[j], ends[n][1].at[s], to(n, 1, c))

    def summed(n, phase):
        total = accs[n][phase][at(n, phase)].astype(F32)
        for s in range(3):
            total = total + ends[n][phase][s].astype(F32)
        return total

    def second(n):
        for s in range(3):
            links.arrival((n, 1, s), ends[n][1].at[s])
        accs[n][2][...] = summed(n, 1).astype(BF16)
        for s, by in enumerate(BYS):
            links.launch((n, 2, s), accs[n][2].at[at(n, 2, by)], ends[n][2].at[s], to(n, 2, by))

    def last(n):
        part, row, rows, col, cols, _ = PIECES[n]
        for s in range(3):
            links.arrival((n, 2, s), ends[n][2].at[s])
        out[row : row + rows, part * 256 + col : part * 256 + col + cols] = summed(n, 2)

    for c in CHUNKS:
        for n in Q_PIECES:
            products(n, c)
            send_far(n, c)
    for c in CHUNKS:
        for n in Q_PIECES:
            send_near(n, c)
    for c in CHUNKS:
        for n in Q_PIECES:
            relay(n, c)

    load_w.wait()

    def input_slice(k, _):
        total = None
        for part in range(3):
            lhs = grads[0, :, part * 256 : part * 256 + 256]
            rows = w[part, lax.div(k, 8), lax.rem(lax.div(k, 2), 4), lax.rem(k, 2)].reshape(512, 256)
            term = lax.dot_general(lhs, rows, (((1,), (1,)), ((), ())), preferred_element_type=F32)
            total = term if total is None else total + term
        grad_tok[:, pl.ds(pl.multiple_of(k * 512, 512), 512)] = total.astype(BF16)
        return 0

    stores = []

    def inputs(quarter):
        lax.fori_loop(quarter * 4, quarter * 4 + 4, input_slice, 0)
        cols = pl.ds(quarter * 2048, 2048)
        copy = pltpu.make_async_copy(grad_tok.at[:, cols], tokens_out.at[:, cols], copy_sem.at[2 + quarter])
        copy.start()
        stores.append(copy)

    for k in range(1, 8):
        links.arrival(("kv", k), landed.at[k - 1])
    keyval = terms[ctx].astype(F32)
    for k in range(7):
        keyval = keyval + landed[k].astype(F32)
    key = keyval[:, 0:128]
    grads[0, :, 512:640] = (key * tables[0] - turn_half(key) * tables[1]).astype(BF16)
    grads[0, :, 640:768] = keyval[:, 128:256].astype(BF16)
    columns = pl.ds(512, 256)
    links.launch("grad_kv", grads.at[0, :, columns], grads.at[1, :, columns], twin)
    inputs(0)
    links.arrival("grad_kv", grads.at[1, :, columns])

    def kv_product(k, _):
        product(KV_PIECES, lax.div(k, 4), lax.rem(k, 4))
        return 0

    lax.fori_loop(0, 16, kv_product, 0)
    for step in (send_far, send_near):
        for c in CHUNKS:
            for n in KV_PIECES:
                step(n, c)
    for k, c in enumerate(CHUNKS):
        for n in Q_PIECES:
            chunk_in(n, c)
        for n in KV_PIECES:
            relay(n, c)
        if k < 3:
            inputs(k + 1)
    for n in Q_PIECES:
        second(n)
    for c in CHUNKS:
        for n in KV_PIECES:
            chunk_in(n, c)
    for n in KV_PIECES:
        second(n)
    for n in Q_PIECES + KV_PIECES:
        last(n)
    for copy in stores:
        copy.wait()
    links.finish()


def scatter_grads(turned, w_all, grad_q, terms, tables):
    vmem, anywhere = pl.BlockSpec(memory_space=pltpu.VMEM), pl.BlockSpec(memory_space=pl.ANY)
    shape = jax.ShapeDtypeStruct
    buffers = []
    for _, _, rows, _, cols, _ in PIECES:
        half, whole = (rows // 2, cols), (rows, cols)
        for shape_of in (
            (4, 2, 4, 4) + half, (4, 4) + whole, (4,) + whole,
            (2, 2, 4, 4) + half, (3, 4) + whole, (3,) + whole, (2, 4, 4) + half,
        ):
            buffers.append(pltpu.VMEM(shape_of, BF16))
    return pl.pallas_call(
        scatter_kernel,
        out_shape=(shape((256, 8192), BF16), shape((64, 768), F32)),
        in_specs=[anywhere, anywhere, vmem, vmem, vmem],
        out_specs=(anywhere, vmem),
        scratch_shapes=[
            pltpu.VMEM((8, 512, 512), BF16),
            pltpu.VMEM((3, 2, 4, 2, 2, 4, 64, 256), BF16),
            pltpu.VMEM((2, 256, 768), BF16),
            pltpu.VMEM((7, 256, 256), BF16),
            pltpu.VMEM((256, 8192), BF16),
            pltpu.SemaphoreType.DMA((6,)),
            pltpu.SemaphoreType.DMA((160,)),
            pltpu.SemaphoreType.DMA((160,)),
            *buffers,
        ],
        compiler_params=pltpu.CompilerParams(
            collective_id=1, has_side_effects=True, vmem_limit_bytes=48 * 2**20
        ),
        name="scatter_grads",
    )(turned, w_all, grad_q, terms, tables)


def rope_tables(positions_in, head_dim):
    half_width = head_dim // 2
    exponent = jnp.arange(half_width).astype(F32) * (2.0 / head_dim)
    frequency = jnp.power(ROPE_BASE, -exponent)
    angles = positions_in.astype(F32)[:, None] * frequency[None, :]
    cos, sin = jnp.cos(angles), jnp.sin(angles)
    return jnp.stack([jnp.concatenate([cos, cos], axis=1), jnp.concatenate([-sin, sin], axis=1)])


def body(tokens, positions, query_weight, key_weight, value_weight, grad_output):
    own_positions = lax.dynamic_slice_in_dim(positions, lax.axis_index("ctx") * 256, 256)
    tables = rope_tables(own_positions, 128)
    w_all, turned, q, kv = gather_weights(
        tokens[0], query_weight, key_weight, value_weight, tables
    )
    attention, grad_q, terms = attend(
        positions, own_positions[None], q, kv, grad_output[0], tables
    )
    grad_tokens, grads = scatter_grads(turned, w_all, grad_q, terms, tables)
    return attention[None], grad_tokens[None], grads[:, :512], grads[:, 512:640], grads[:, 640:]


def solution(mesh):
    in_specs = (
        P("dp", "ctx", None),
        P(),
        P(("dp", "ctx"), None),
        P(("dp", "ctx"), None),
        P(("dp", "ctx"), None),
        P("dp", "ctx", None),
    )
    out_specs = (
        P("dp", "ctx", None),
        P("dp", "ctx", None),
        P(("dp", "ctx"), None),
        P(("dp", "ctx"), None),
        P(("dp", "ctx"), None),
    )
    return jax.shard_map(body, mesh=mesh, in_specs=in_specs, out_specs=out_specs, check_vma=False)
```

```python
import functools

import jax
import jax.numpy as jnp
from jax import lax
from jax.experimental import pallas as pl
from jax.experimental.pallas import tpu as pltpu
from jax.sharding import PartitionSpec as P

ROPE_BASE = 1000000.0
MASKED = -1e30
MESH = pl.DeviceIdType.MESH
BF16 = jnp.bfloat16
F32 = jnp.float32
AXES = ("x", "y", "z")
PIECES = (
    (2, 0, 48, 0, 128, ("z", "y", "x")),
    (2, 0, 48, 128, 128, ("x", "z", "y")),
    (2, 48, 16, 0, 256, ("y", "x", "z")),
    (0, 0, 64, 0, 128, ("z", "y", "x")),
    (0, 0, 64, 128, 128, ("x", "z", "y")),
    (1, 0, 64, 0, 128, ("y", "x", "z")),
    (1, 0, 32, 128, 128, ("y", "z", "x")),
    (1, 32, 32, 128, 128, ("z", "x", "y")),
)
KV_PIECES = (0, 1, 2)
Q_PIECES = (3, 4, 5, 6, 7)
Q_PARTS = ((3, 4), (5, 6, 7))
SCALE = 128 ** (-0.5)
LOG2E = 1.4426950408889634


def place():
    dp, ctx = lax.axis_index("dp"), lax.axis_index("ctx")
    return {
        "x": lax.div(dp, 8) * 2 + lax.div(ctx, 4),
        "y": lax.rem(lax.div(dp, 2), 4),
        "z": lax.rem(ctx, 4),
        "core": lax.rem(dp, 2),
    }


def device(at):
    return (
        lax.div(at["x"], 2) * 8 + at["y"] * 2 + at["core"],
        lax.rem(at["x"], 2) * 4 + at["z"],
    )


def moved(at, axis, by):
    return {**at, axis: lax.rem(at[axis] + 4 + by, 4)}


def sibling(at):
    return {**at, "core": 1 - at["core"]}


def greet(targets):
    barrier = pltpu.get_barrier_semaphore()
    for target in targets:
        pl.semaphore_signal(barrier, inc=1, device_id=target, device_id_type=MESH)
    pl.semaphore_wait(barrier, len(targets))


def partners(at):
    near = [device(moved(at, axis, by)) for axis in AXES for by in (1, -1, 2)]
    return near + [device(sibling(at))] + ctx_peers()


def ctx_peers():
    dp, ctx = lax.axis_index("dp"), lax.axis_index("ctx")
    return [(dp, lax.rem(ctx + k, 8)) for k in range(1, 8)]


def remote(src, dst, send, recv, target):
    return pltpu.make_async_remote_copy(
        src_ref=src, dst_ref=dst, send_sem=send, recv_sem=recv, device_id=target, device_id_type=MESH
    )


class Links:
    def __init__(self, send, recv, twin):
        self.send, self.recv, self.twin = send, recv, twin
        self.slots, self.started = {}, []

    def slot(self, key):
        return self.slots.setdefault(key, len(self.slots))

    def launch(self, key, src, dst, target):
        k = self.slot(key)
        copy = remote(src, dst, self.send.at[k], self.recv.at[k], target)
        copy.start()
        self.started.append(copy)

    def arrival(self, key, ref):
        k = self.slot(key)
        remote(ref, ref, self.send.at[k], self.recv.at[k], self.twin).wait_recv()

    def finish(self):
        for copy in self.started:
            copy.wait_send()


def turn_half(a):
    return pltpu.roll(a, 64, 1)


BYS = (2, 1, -1)


def gather_kernel(
    tokens, wq_hbm, wk_hbm, wv_hbm, tables_hbm,
    w_out, turned_out, q_out, kv_out,
    w, tok, twin_tok, turned, wq, wk, wv, tables, copy_sem, send, recv,
):
    me = place()
    core = me["core"]
    twin = device(sibling(me))
    links = Links(send, recv, twin)
    loads = [
        pltpu.make_async_copy(src, dst, copy_sem.at[k])
        for k, (src, dst) in enumerate(
            ((wq_hbm, wq), (wk_hbm, wk), (wv_hbm, wv), (tables_hbm, tables), (tokens, tok))
        )
    ]
    for copy in loads:
        copy.start()
    for copy in loads[:3]:
        copy.wait()
    x_hi, x_lo = lax.div(me["x"], 2), lax.rem(me["x"], 2)
    w[2, x_hi, me["y"], core, x_lo, me["z"], :, 0:128] = wk[...].astype(BF16)
    w[2, x_hi, me["y"], core, x_lo, me["z"], :, 128:256] = wv[...].astype(BF16)
    w[0, x_hi, me["y"], core, x_lo, me["z"]] = wq[:, 0:256].astype(BF16)
    w[1, x_hi, me["y"], core, x_lo, me["z"]] = wq[:, 256:512].astype(BF16)

    def block(n, first, second, third, core_at=core, half=None):
        part, row, rows, col, cols, order = PIECES[n]
        if half is not None:
            rows = rows // 2
            row = row + half * rows
        at = dict(zip(order, (first, second, third)))
        x, y, z = (at[axis] for axis in AXES)
        return w.at[
            part,
            slice(None) if x is None else lax.div(x, 2),
            slice(None) if y is None else y,
            core_at,
            slice(None) if x is None else lax.rem(x, 2),
            slice(None) if z is None else z,
            pl.ds(row, rows),
            pl.ds(col, cols),
        ]

    def to(n, phase, by):
        return device(moved(me, PIECES[n][5][phase], by))

    def index(n, phase, by=0):
        axis = PIECES[n][5][phase]
        return moved(me, axis, by)[axis]

    greet(partners(me))
    everything = KV_PIECES + Q_PIECES
    for n in everything:
        mine = block(n, index(n, 0), index(n, 1), index(n, 2))
        for by in BYS:
            links.launch((n, 0, by), mine, mine, to(n, 0, by))
    for k in range(8):
        columns = tokens.at[:, pl.ds(pl.multiple_of(k * 1024 + (1 - core) * 512, 512), 512)]
        links.launch(("tokens", k), columns, twin_tok.at[k], twin)

    def send_chunk(n, c):
        chunk = block(n, None, index(n, 1, c), index(n, 2))
        for by in BYS if n in KV_PIECES else (1, -1):
            links.launch((n, 2, c, by), chunk, chunk, to(n, 2, by))

    def pass_on(pieces, c):
        for n in pieces:
            second = index(n, 1, c)
            for half, by in enumerate((1, -1)):
                third = index(n, 2, -by)
                links.arrival((n, 2, c, by), block(n, None, second, third))
                part = block(n, None, second, third, half=half)
                links.launch((n, 3, c, by), part, part, to(n, 2, by))

    for n in everything:
        second, third = index(n, 1), index(n, 2)
        for by in BYS:
            links.arrival((n, 0, by), block(n, index(n, 0, -by), second, third))
        line = block(n, None, second, third)
        for by in BYS:
            links.launch((n, 1, by), line, line, to(n, 1, by))
        send_chunk(n, 0)
    for n in everything:
        for by in BYS:
            links.arrival((n, 1, by), block(n, None, index(n, 1, -by), index(n, 2)))
            send_chunk(n, -by)

    CHUNKS = (0,) + tuple(-by for by in BYS)

    def chunk_in(n, c):
        second = index(n, 1, c)
        if n in KV_PIECES:
            for by in BYS:
                links.arrival((n, 2, c, by), block(n, None, second, index(n, 2, -by)))
        else:
            for half, by in enumerate((1, -1)):
                links.arrival((n, 3, c, by), block(n, None, second, index(n, 2, 2), half=half))
        whole = block(n, None, second, None)
        links.launch((n, "twin", c), whole, whole, twin)

    def twin_in(n, c):
        links.arrival((n, "twin", c), block(n, None, index(n, 1, c), None, 1 - core))

    for copy in loads[3:]:
        copy.wait()
    for k in range(8):
        links.arrival(("tokens", k), twin_tok.at[k])

    def turn(k, _):
        at = pl.multiple_of(k * 1024 + core * 512, 512)
        turned[k, :, 0:256] = tok[:, pl.ds(at, 512)].T
        turned[k, :, 256:512] = twin_tok[k].T
        return 0

    lax.fori_loop(0, 4, turn, 0)
    keep = []

    def store(k, src, dst):
        copy = pltpu.make_async_copy(src, dst, copy_sem.at[k])
        copy.start()
        keep.append(copy)

    for n in KV_PIECES:
        chunk_in(n, CHUNKS[0])
    pass_on(Q_PIECES, CHUNKS[0])
    for c in CHUNKS[1:]:
        for n in KV_PIECES:
            chunk_in(n, c)
    pass_on(Q_PIECES, CHUNKS[1])
    for c in CHUNKS:
        for n in KV_PIECES:
            twin_in(n, c)
    store(5, w.at[2], w_out.at[2])

    def project(part):
        def add(k, total):
            lhs = tok[:, pl.ds(pl.multiple_of(k * 2048, 2048), 2048)]
            rows = w[part, lax.div(k, 2), pl.ds(lax.rem(k, 2) * 2, 2)].reshape(2048, 256)
            return total + jnp.dot(lhs, rows, preferred_element_type=F32)

        return lax.fori_loop(0, 4, add, jnp.zeros((256, 256), F32))

    both = project(2)
    cos, sin = tables[0], tables[1]
    ctx = lax.axis_index("ctx")
    key = both[:, 0:128]
    kv_out[ctx, :, 0:128] = (key * cos + turn_half(key) * sin).astype(BF16)
    kv_out[ctx, :, 128:256] = both[:, 128:256].astype(BF16)
    peers = ctx_peers()
    for k in (4, 2, 6, 1, 3, 5, 7):
        links.launch(("kv", k), kv_out.at[ctx], kv_out.at[ctx], peers[k - 1])

    pass_on(Q_PIECES, CHUNKS[2])
    pass_on(Q_PIECES, CHUNKS[3])
    lax.fori_loop(4, 8, turn, 0)
    store(8, turned, turned_out)
    for c in CHUNKS:
        for n in Q_PIECES:
            chunk_in(n, c)
    for part in range(2):
        for c in CHUNKS:
            for n in Q_PARTS[part]:
                twin_in(n, c)
        store(6 + part, w.at[part], w_out.at[part])
        both = project(part)
        for h in range(2):
            query = both[:, h * 128 : h * 128 + 128]
            rotated = (query * cos + turn_half(query) * sin).astype(BF16)
            q_out[:, part * 256 + h * 128 : part * 256 + h * 128 + 128] = rotated
    for k in range(1, 8):
        links.arrival(("kv", k), kv_out.at[lax.rem(ctx + 8 - k, 8)])
    for copy in keep:
        copy.wait()
    links.finish()


def gather_weights(tokens, wq, wk, wv, tables):
    vmem, anywhere = pl.BlockSpec(memory_space=pltpu.VMEM), pl.BlockSpec(memory_space=pl.ANY)
    shape = jax.ShapeDtypeStruct
    return pl.pallas_call(
        gather_kernel,
        out_shape=(
            shape((3, 2, 4, 2, 2, 4, 64, 256), BF16),
            shape((8, 512, 512), BF16),
            shape((256, 512), BF16),
            shape((8, 256, 256), BF16),
        ),
        in_specs=[anywhere] * 5,
        out_specs=(anywhere, anywhere, vmem, vmem),
        scratch_shapes=[
            pltpu.VMEM((3, 2, 4, 2, 2, 4, 64, 256), BF16),
            pltpu.VMEM((256, 8192), BF16),
            pltpu.VMEM((8, 256, 512), BF16),
            pltpu.VMEM((8, 512, 512), BF16),
            pltpu.VMEM((64, 512), F32),
            pltpu.VMEM((64, 128), F32),
            pltpu.VMEM((64, 128), F32),
            pltpu.VMEM((2, 256, 128), F32),
            pltpu.SemaphoreType.DMA((9,)),
            pltpu.SemaphoreType.DMA((212,)),
            pltpu.SemaphoreType.DMA((212,)),
        ],
        compiler_params=pltpu.CompilerParams(
            collective_id=0, has_side_effects=True, vmem_limit_bytes=60 * 2**20
        ),
        name="gather_weights",
    )(tokens, wq, wk, wv, tables)


def attention_kernel(
    positions, own_positions, q_hbm, kv_hbm, grad, tables,
    attention, grad_q, terms,
    q, kv, load_sem, qs, gs, gs_t, keys_t, values_t, scores, top, total, att_t, gq_t,
):
    load_kv = pltpu.make_async_copy(kv_hbm, kv, load_sem.at[0])
    load_q = pltpu.make_async_copy(q_hbm, q, load_sem.at[1])
    load_kv.start()
    load_q.start()
    for h in range(4):
        rows = slice(h * 256, h * 256 + 256)
        gs[rows] = grad[:, h * 128 : h * 128 + 128]
        gs_t[:, rows] = grad[:, h * 128 : h * 128 + 128].T
    load_q.wait()
    for h in range(4):
        qs[h * 256 : h * 256 + 256] = q[:, h * 128 : h * 128 + 128]
    load_kv.wait()
    for k in range(8):
        cols = slice(k * 256, k * 256 + 256)
        keys_t[:, cols] = kv[k, :, 0:128].T
        values_t[:, cols] = kv[k, :, 128:256].T
    nt = (((1,), (1,)), ((), ()))
    lead = own_positions[...] - lax.broadcasted_iota(jnp.int32, (128, 256), 0)
    top[...] = jnp.full(top.shape, MASKED, F32)

    def score(k, _):
        for h in range(4):
            cols = slice(h * 256, h * 256 + 256)
            s = lax.dot_general(kv[k, :, 0:128], qs[cols], nt, preferred_element_type=F32)
            upper = jnp.where(lead >= positions[k * 256], s[0:128], MASKED)
            lower = jnp.where(lead >= positions[k * 256 + 128], s[128:256], MASKED)
            scores[k, 0:128, cols] = upper
            scores[k, 128:256, cols] = lower
            high = jnp.max(jnp.maximum(upper, lower), axis=0, keepdims=True)
            top[:, cols] = jnp.maximum(top[:, cols], high)
        return 0

    lax.fori_loop(0, 8, score, 0)
    total[...] = jnp.zeros(total.shape, F32)
    att_t[...] = jnp.zeros(att_t.shape, F32)

    def weigh(k, _):
        at = pl.ds(pl.multiple_of(k * 256, 256), 256)
        for h in range(4):
            cols = slice(h * 256, h * 256 + 256)
            weight = jnp.exp2((scores[k, :, cols] - top[:, cols]) * (SCALE * LOG2E))
            scores[k, :, cols] = weight
            total[:, cols] += jnp.sum(weight, axis=0, keepdims=True)
            att_t[:, cols] += jnp.dot(values_t[:, at], weight.astype(BF16), preferred_element_type=F32)
        return 0

    lax.fori_loop(0, 8, weigh, 0)
    for h in range(4):
        cols = slice(h * 256, h * 256 + 256)
        inverse = 1.0 / total[:, cols]
        out = (att_t[:, cols] / total[:, cols]).astype(BF16)
        attention[:, h * 128 : h * 128 + 128] = out.T
        total[:, cols] = inverse
        top[:, cols] = jnp.sum(gs_t[:, cols].astype(F32) * out.astype(F32), axis=0, keepdims=True)
    gq_t[...] = jnp.zeros(gq_t.shape, F32)

    def back(k, _):
        at = pl.ds(pl.multiple_of(k * 256, 256), 256)
        key_term = jnp.zeros((256, 128), F32)
        value_term = jnp.zeros((256, 128), F32)
        for h in range(4):
            cols = slice(h * 256, h * 256 + 256)
            probs = scores[k, :, cols] * total[:, cols]
            grad_probs = lax.dot_general(kv[k, :, 128:256], gs[cols], nt, preferred_element_type=F32)
            dscore = (probs * (grad_probs - top[:, cols])).astype(BF16)
            key_term += jnp.dot(dscore, qs[cols], preferred_element_type=F32)
            value_term += jnp.dot(probs.astype(BF16), gs[cols], preferred_element_type=F32)
            gq_t[:, cols] += jnp.dot(keys_t[:, at], dscore, preferred_element_type=F32)
        terms[k, :, 0:128] = (key_term * SCALE).astype(BF16)
        terms[k, :, 128:256] = value_term.astype(BF16)
        return 0

    lax.fori_loop(0, 8, back, 0)
    for h in range(4):
        a = gq_t[:, h * 256 : h * 256 + 256].T * SCALE
        unrotated = a * tables[0] - turn_half(a) * tables[1]
        grad_q[:, h * 128 : h * 128 + 128] = unrotated.astype(BF16)


def attend(positions, own_positions, q, kv, grad, tables):
    vmem, anywhere = pl.BlockSpec(memory_space=pltpu.VMEM), pl.BlockSpec(memory_space=pl.ANY)
    shape = jax.ShapeDtypeStruct
    return pl.pallas_call(
        attention_kernel,
        out_shape=(shape((256, 512), BF16), shape((256, 512), BF16), shape((8, 256, 256), BF16)),
        in_specs=[pl.BlockSpec(memory_space=pltpu.SMEM), vmem, anywhere, anywhere, vmem, vmem],
        out_specs=(vmem, vmem, vmem),
        scratch_shapes=[
            pltpu.VMEM((256, 512), BF16),
            pltpu.VMEM((8, 256, 256), BF16),
            pltpu.SemaphoreType.DMA((2,)),
            pltpu.VMEM((1024, 128), BF16),
            pltpu.VMEM((1024, 128), BF16),
            pltpu.VMEM((128, 1024), BF16),
            pltpu.VMEM((128, 2048), BF16),
            pltpu.VMEM((128, 2048), BF16),
            pltpu.VMEM((8, 256, 1024), F32),
            pltpu.VMEM((1, 1024), F32),
            pltpu.VMEM((1, 1024), F32),
            pltpu.VMEM((128, 1024), F32),
            pltpu.VMEM((128, 1024), F32),
        ],
        compiler_params=pltpu.CompilerParams(vmem_limit_bytes=60 * 2**20),
        name="attend",
    )(positions, own_positions, q, kv, grad, tables)


def scatter_kernel(
    turned, w_all, grad_q, terms, tables,
    tokens_out, out,
    held, w, grads, landed, grad_tok, copy_sem, send, recv, *buffers,
):
    me = place()
    core = me["core"]
    ctx = lax.axis_index("ctx")
    twin = device(sibling(me))
    links = Links(send, recv, twin)
    accs = [buffers[7 * n : 7 * n + 3] for n in range(len(PIECES))]
    ends = [buffers[7 * n + 3 : 7 * n + 6] for n in range(len(PIECES))]
    vias = [buffers[7 * n + 6] for n in range(len(PIECES))]
    load = pltpu.make_async_copy(turned, held, copy_sem.at[0])
    load.start()
    load_w = pltpu.make_async_copy(w_all, w, copy_sem.at[1])
    load_w.start()
    greet(partners(me))
    links.launch("grad_q", grad_q, grads.at[1, :, pl.ds(0, 512)], twin)
    peers = ctx_peers()
    for k in (4, 2, 6, 1, 3, 5, 7):
        links.launch(("kv", k), terms.at[lax.rem(ctx + k, 8)], landed.at[k - 1], peers[k - 1])
    grads[0, :, 0:512] = grad_q[...]
    load.wait()
    links.arrival("grad_q", grads.at[1, :, pl.ds(0, 512)])

    def axes(n):
        return tuple(reversed(PIECES[n][5]))

    def to(n, phase, by):
        return device(moved(me, axes(n)[phase], by))

    def at(n, phase, by=0):
        axis = axes(n)[phase]
        return moved(me, axis, by)[axis]

    def product(pieces, x, y):
        part = PIECES[pieces[0]][0]
        k = lax.div(x, 2) * 4 + y
        lhs = held[k, pl.ds(pl.multiple_of(lax.rem(x, 2) * 256, 256), 256)]
        rhs = grads[:, :, part * 256 : part * 256 + 256].reshape(512, 256)
        term = jnp.dot(lhs, rhs, preferred_element_type=F32).astype(BF16)
        for n in pieces:
            _, row, rows, col, cols, _ = PIECES[n]
            for z in range(4):
                first, second, third = ({"x": x, "y": y, "z": z}[axis] for axis in axes(n))
                start = z * 64 + row
                if n in KV_PIECES:
                    accs[n][0][first, second, third] = term[start : start + rows, col : col + cols]
                    continue
                for half in range(2):
                    start = z * 64 + row + half * (rows // 2)
                    accs[n][0][first, half, second, third] = term[
                        start : start + rows // 2, col : col + cols
                    ]

    CHUNKS = (2, 1, -1, 0)

    def products(pieces):
        def one(k, _):
            product(pieces, lax.div(k, 4), lax.rem(k, 4))
            return 0

        lax.fori_loop(0, 16, one, 0)

    def send_direct(n, c):
        j = at(n, 1, c)
        for s, by in enumerate(BYS):
            src = accs[n][0].at[at(n, 0, by), j]
            links.launch((n, 0, c, s), src, ends[n][0].at[s, j], to(n, 0, by))

    def send_far(n, c):
        j = at(n, 1, c)
        for d, by in enumerate((1, -1)):
            src = accs[n][0].at[at(n, 0, 2), d, j]
            links.launch((n, "via", c, d), src, vias[n].at[d, j], to(n, 0, by))

    def send_near(n, c):
        j = at(n, 1, c)
        for d, by in enumerate((1, -1)):
            src = accs[n][0].at[at(n, 0, by), 1 - d, j]
            links.launch((n, "end", c, d, 1 - d), src, ends[n][0].at[d, 1 - d, j], to(n, 0, by))

    def relay(n, c):
        j = at(n, 1, c)
        acc, via, end = accs[n][0], vias[n], ends[n][0]
        for d, by in enumerate((1, -1)):
            links.arrival((n, "via", c, d), via.at[d, j])
            i = at(n, 0, by)
            acc[i, d, j] = (acc[i, d, j].astype(F32) + via[d, j].astype(F32)).astype(BF16)
            links.launch((n, "end", c, d, d), acc.at[i, d, j], end.at[d, d, j], to(n, 0, by))

    def chunk_in(n, c):
        j = at(n, 1, c)
        acc, end = accs[n][0], ends[n][0]
        rows = PIECES[n][2] // 2
        if n in KV_PIECES:
            for s in range(3):
                links.arrival((n, 0, c, s), end.at[s, j])
            total = acc[at(n, 0), j].astype(F32)
            for s in range(3):
                total = total + end[s, j].astype(F32)
            accs[n][1][j] = total.astype(BF16)
        for h in range(2) if n in Q_PIECES else ():
            for d in range(2):
                links.arrival((n, "end", c, d, h), end.at[d, h, j])
            total = acc[at(n, 0), h, j].astype(F32)
            total = total + end[0, h, j].astype(F32) + end[1, h, j].astype(F32)
            accs[n][1][j, :, h * rows : h * rows + rows] = total.astype(BF16)
        if c != 0:
            s = BYS.index(c)
            links.launch((n, 1, s), accs[n][1].at[j], ends[n][1].at[s], to(n, 1, c))

    def summed(n, phase):
        total = accs[n][phase][at(n, phase)].astype(F32)
        for s in range(3):
            total = total + ends[n][phase][s].astype(F32)
        return total

    def second(n):
        for s in range(3):
            links.arrival((n, 1, s), ends[n][1].at[s])
        accs[n][2][...] = summed(n, 1).astype(BF16)
        for s, by in enumerate(BYS):
            links.launch((n, 2, s), accs[n][2].at[at(n, 2, by)], ends[n][2].at[s], to(n, 2, by))

    def last(n):
        part, row, rows, col, cols, _ = PIECES[n]
        for s in range(3):
            links.arrival((n, 2, s), ends[n][2].at[s])
        out[row : row + rows, part * 256 + col : part * 256 + col + cols] = summed(n, 2)

    for pieces in Q_PARTS:
        products(pieces)
        for c in CHUNKS:
            for n in pieces:
                send_far(n, c)
    for c in CHUNKS:
        for n in Q_PIECES:
            send_near(n, c)
    for c in CHUNKS:
        for n in Q_PIECES:
            relay(n, c)

    load_w.wait()

    def input_slice(k, _):
        total = None
        for part in range(3):
            lhs = grads[0, :, part * 256 : part * 256 + 256]
            rows = w[part, lax.div(k, 8), lax.rem(lax.div(k, 2), 4), lax.rem(k, 2)].reshape(512, 256)
            term = lax.dot_general(lhs, rows, (((1,), (1,)), ((), ())), preferred_element_type=F32)
            total = term if total is None else total + term
        grad_tok[:, pl.ds(pl.multiple_of(k * 512, 512), 512)] = total.astype(BF16)
        return 0

    stores = []

    def inputs(quarter):
        lax.fori_loop(quarter * 4, quarter * 4 + 4, input_slice, 0)
        cols = pl.ds(quarter * 2048, 2048)
        copy = pltpu.make_async_copy(grad_tok.at[:, cols], tokens_out.at[:, cols], copy_sem.at[2 + quarter])
        copy.start()
        stores.append(copy)

    for k in range(1, 8):
        links.arrival(("kv", k), landed.at[k - 1])
    keyval = terms[ctx].astype(F32)
    for k in range(7):
        keyval = keyval + landed[k].astype(F32)
    key = keyval[:, 0:128]
    grads[0, :, 512:640] = (key * tables[0] - turn_half(key) * tables[1]).astype(BF16)
    grads[0, :, 640:768] = keyval[:, 128:256].astype(BF16)
    columns = pl.ds(512, 256)
    links.launch("grad_kv", grads.at[0, :, columns], grads.at[1, :, columns], twin)
    inputs(0)
    links.arrival("grad_kv", grads.at[1, :, columns])

    products(KV_PIECES)
    for c in CHUNKS:
        for n in KV_PIECES:
            send_direct(n, c)
    for k, c in enumerate(CHUNKS):
        for n in Q_PIECES:
            chunk_in(n, c)
        if k < 3:
            inputs(k + 1)
    for n in Q_PIECES:
        second(n)
    for c in CHUNKS:
        for n in KV_PIECES:
            chunk_in(n, c)
    for n in KV_PIECES:
        second(n)
    for n in Q_PIECES + KV_PIECES:
        last(n)
    for copy in stores:
        copy.wait()
    links.finish()


def scatter_grads(turned, w_all, grad_q, terms, tables):
    vmem, anywhere = pl.BlockSpec(memory_space=pltpu.VMEM), pl.BlockSpec(memory_space=pl.ANY)
    shape = jax.ShapeDtypeStruct
    buffers = []
    for n, (_, _, rows, _, cols, _) in enumerate(PIECES):
        half, whole = (rows // 2, cols), (rows, cols)
        later = ((4, 4) + whole, (4,) + whole), ((3, 4) + whole, (3,) + whole)
        if n in KV_PIECES:
            first = (4, 4, 4) + whole, (3, 4, 4) + whole, (8, 128)
        else:
            first = (4, 2, 4, 4) + half, (2, 2, 4, 4) + half, (2, 4, 4) + half
        for shape_of in (first[0], *later[0], first[1], *later[1], first[2]):
            buffers.append(pltpu.VMEM(shape_of, BF16))
    return pl.pallas_call(
        scatter_kernel,
        out_shape=(shape((256, 8192), BF16), shape((64, 768), F32)),
        in_specs=[anywhere, anywhere, vmem, vmem, vmem],
        out_specs=(anywhere, vmem),
        scratch_shapes=[
            pltpu.VMEM((8, 512, 512), BF16),
            pltpu.VMEM((3, 2, 4, 2, 2, 4, 64, 256), BF16),
            pltpu.VMEM((2, 256, 768), BF16),
            pltpu.VMEM((7, 256, 256), BF16),
            pltpu.VMEM((256, 8192), BF16),
            pltpu.SemaphoreType.DMA((6,)),
            pltpu.SemaphoreType.DMA((216,)),
            pltpu.SemaphoreType.DMA((216,)),
            *buffers,
        ],
        compiler_params=pltpu.CompilerParams(
            collective_id=1, has_side_effects=True, vmem_limit_bytes=48 * 2**20
        ),
        name="scatter_grads",
    )(turned, w_all, grad_q, terms, tables)


def rope_tables(positions_in, head_dim):
    half_width = head_dim // 2
    exponent = jnp.arange(half_width).astype(F32) * (2.0 / head_dim)
    frequency = jnp.power(ROPE_BASE, -exponent)
    angles = positions_in.astype(F32)[:, None] * frequency[None, :]
    cos, sin = jnp.cos(angles), jnp.sin(angles)
    return jnp.stack([jnp.concatenate([cos, cos], axis=1), jnp.concatenate([-sin, sin], axis=1)])


def body(tokens, positions, query_weight, key_weight, value_weight, grad_output):
    own_positions = lax.dynamic_slice_in_dim(positions, lax.axis_index("ctx") * 256, 256)
    tables = rope_tables(own_positions, 128)
    w_all, turned, q, kv = gather_weights(
        tokens[0], query_weight, key_weight, value_weight, tables
    )
    attention, grad_q, terms = attend(
        positions, own_positions[None], q, kv, grad_output[0], tables
    )
    grad_tokens, grads = scatter_grads(turned, w_all, grad_q, terms, tables)
    return attention[None], grad_tokens[None], grads[:, :512], grads[:, 512:640], grads[:, 640:]


def solution(mesh):
    in_specs = (
        P("dp", "ctx", None),
        P(),
        P(("dp", "ctx"), None),
        P(("dp", "ctx"), None),
        P(("dp", "ctx"), None),
        P("dp", "ctx", None),
    )
    out_specs = (
        P("dp", "ctx", None),
        P("dp", "ctx", None),
        P(("dp", "ctx"), None),
        P(("dp", "ctx"), None),
        P(("dp", "ctx"), None),
    )
    return jax.shard_map(body, mesh=mesh, in_specs=in_specs, out_specs=out_specs, check_vma=False)
```

```python
import functools

import jax
import jax.numpy as jnp
from jax import lax
from jax.experimental import pallas as pl
from jax.experimental.pallas import tpu as pltpu
from jax.sharding import PartitionSpec as P

ROPE_BASE = 1000000.0
MASKED = -1e30
MESH = pl.DeviceIdType.MESH
BF16 = jnp.bfloat16
F32 = jnp.float32
AXES = ("x", "y", "z")
PIECES = (
    (2, 0, 48, 0, 128, ("z", "y", "x")),
    (2, 0, 48, 128, 128, ("x", "z", "y")),
    (2, 48, 16, 0, 256, ("y", "x", "z")),
    (0, 0, 64, 0, 128, ("z", "y", "x")),
    (0, 0, 64, 128, 128, ("x", "z", "y")),
    (1, 0, 64, 0, 128, ("y", "x", "z")),
    (1, 0, 32, 128, 128, ("y", "z", "x")),
    (1, 32, 32, 128, 128, ("z", "x", "y")),
)
KV_PIECES = (0, 1, 2)
Q_PIECES = (3, 4, 5, 6, 7)
Q_PARTS = ((3, 4), (5, 6, 7))
SCALE = 128 ** (-0.5)
LOG2E = 1.4426950408889634


def place():
    dp, ctx = lax.axis_index("dp"), lax.axis_index("ctx")
    return {
        "x": lax.div(dp, 8) * 2 + lax.div(ctx, 4),
        "y": lax.rem(lax.div(dp, 2), 4),
        "z": lax.rem(ctx, 4),
        "core": lax.rem(dp, 2),
    }


def device(at):
    return (
        lax.div(at["x"], 2) * 8 + at["y"] * 2 + at["core"],
        lax.rem(at["x"], 2) * 4 + at["z"],
    )


def moved(at, axis, by):
    return {**at, axis: lax.rem(at[axis] + 4 + by, 4)}


def sibling(at):
    return {**at, "core": 1 - at["core"]}


def greet(targets):
    barrier = pltpu.get_barrier_semaphore()
    for target in targets:
        pl.semaphore_signal(barrier, inc=1, device_id=target, device_id_type=MESH)
    pl.semaphore_wait(barrier, len(targets))


def partners(at):
    near = [device(moved(at, axis, by)) for axis in AXES for by in (1, -1, 2)]
    return near + [device(sibling(at))] + ctx_peers()


def ctx_peers():
    dp, ctx = lax.axis_index("dp"), lax.axis_index("ctx")
    return [(dp, lax.rem(ctx + k, 8)) for k in range(1, 8)]


def remote(src, dst, send, recv, target):
    return pltpu.make_async_remote_copy(
        src_ref=src, dst_ref=dst, send_sem=send, recv_sem=recv, device_id=target, device_id_type=MESH
    )


class Links:
    def __init__(self, send, recv, twin):
        self.send, self.recv, self.twin = send, recv, twin
        self.slots, self.started = {}, []

    def slot(self, key):
        return self.slots.setdefault(key, len(self.slots))

    def launch(self, key, src, dst, target):
        k = self.slot(key)
        copy = remote(src, dst, self.send.at[k], self.recv.at[k], target)
        copy.start()
        self.started.append(copy)

    def arrival(self, key, ref):
        k = self.slot(key)
        remote(ref, ref, self.send.at[k], self.recv.at[k], self.twin).wait_recv()

    def finish(self):
        for copy in self.started:
            copy.wait_send()


def turn_half(a):
    return pltpu.roll(a, 64, 1)


BYS = (2, 1, -1)


def gather_kernel(
    tokens, wq_hbm, wk_hbm, wv_hbm, tables_hbm,
    w_out, turned_out, q_out, kv_out,
    w, tok, twin_tok, turned, wq, wk, wv, tables, copy_sem, send, recv,
):
    me = place()
    core = me["core"]
    twin = device(sibling(me))
    links = Links(send, recv, twin)
    loads = [
        pltpu.make_async_copy(src, dst, copy_sem.at[k])
        for k, (src, dst) in enumerate(
            ((wq_hbm, wq), (wk_hbm, wk), (wv_hbm, wv), (tables_hbm, tables), (tokens, tok))
        )
    ]
    for copy in loads:
        copy.start()
    for copy in loads[:3]:
        copy.wait()
    x_hi, x_lo = lax.div(me["x"], 2), lax.rem(me["x"], 2)
    w[2, x_hi, me["y"], core, x_lo, me["z"], :, 0:128] = wk[...].astype(BF16)
    w[2, x_hi, me["y"], core, x_lo, me["z"], :, 128:256] = wv[...].astype(BF16)
    w[0, x_hi, me["y"], core, x_lo, me["z"]] = wq[:, 0:256].astype(BF16)
    w[1, x_hi, me["y"], core, x_lo, me["z"]] = wq[:, 256:512].astype(BF16)

    def block(n, first, second, third, core_at=core, half=None):
        part, row, rows, col, cols, order = PIECES[n]
        if half is not None:
            rows = rows // 2
            row = row + half * rows
        at = dict(zip(order, (first, second, third)))
        x, y, z = (at[axis] for axis in AXES)
        return w.at[
            part,
            slice(None) if x is None else lax.div(x, 2),
            slice(None) if y is None else y,
            core_at,
            slice(None) if x is None else lax.rem(x, 2),
            slice(None) if z is None else z,
            pl.ds(row, rows),
            pl.ds(col, cols),
        ]

    def to(n, phase, by):
        return device(moved(me, PIECES[n][5][phase], by))

    def index(n, phase, by=0):
        axis = PIECES[n][5][phase]
        return moved(me, axis, by)[axis]

    greet(partners(me))
    everything = KV_PIECES + Q_PIECES
    for n in everything:
        mine = block(n, index(n, 0), index(n, 1), index(n, 2))
        for by in BYS:
            links.launch((n, 0, by), mine, mine, to(n, 0, by))
    for k in range(8):
        columns = tokens.at[:, pl.ds(pl.multiple_of(k * 1024 + (1 - core) * 512, 512), 512)]
        links.launch(("tokens", k), columns, twin_tok.at[k], twin)

    def send_chunk(n, c):
        chunk = block(n, None, index(n, 1, c), index(n, 2))
        for by in BYS if n in KV_PIECES else (1, -1):
            links.launch((n, 2, c, by), chunk, chunk, to(n, 2, by))

    def pass_on(pieces, c):
        for n in pieces:
            second = index(n, 1, c)
            for half, by in enumerate((1, -1)):
                third = index(n, 2, -by)
                links.arrival((n, 2, c, by), block(n, None, second, third))
                part = block(n, None, second, third, half=half)
                links.launch((n, 3, c, by), part, part, to(n, 2, by))

    for pieces in (KV_PIECES, Q_PIECES):
        for n in pieces:
            second, third = index(n, 1), index(n, 2)
            for by in BYS:
                links.arrival((n, 0, by), block(n, index(n, 0, -by), second, third))
            line = block(n, None, second, third)
            for by in BYS:
                links.launch((n, 1, by), line, line, to(n, 1, by))
            send_chunk(n, 0)
        for n in pieces:
            for by in BYS:
                links.arrival((n, 1, by), block(n, None, index(n, 1, -by), index(n, 2)))
                send_chunk(n, -by)

    CHUNKS = (0,) + tuple(-by for by in BYS)

    def chunk_in(n, c):
        second = index(n, 1, c)
        if n in KV_PIECES:
            for by in BYS:
                links.arrival((n, 2, c, by), block(n, None, second, index(n, 2, -by)))
        else:
            for half, by in enumerate((1, -1)):
                links.arrival((n, 3, c, by), block(n, None, second, index(n, 2, 2), half=half))
        whole = block(n, None, second, None)
        links.launch((n, "twin", c), whole, whole, twin)

    def twin_in(n, c):
        links.arrival((n, "twin", c), block(n, None, index(n, 1, c), None, 1 - core))

    for copy in loads[3:]:
        copy.wait()
    for k in range(8):
        links.arrival(("tokens", k), twin_tok.at[k])

    def turn(k, _):
        at = pl.multiple_of(k * 1024 + core * 512, 512)
        turned[k, :, 0:256] = tok[:, pl.ds(at, 512)].T
        turned[k, :, 256:512] = twin_tok[k].T
        return 0

    lax.fori_loop(0, 4, turn, 0)
    keep = []

    def store(k, src, dst):
        copy = pltpu.make_async_copy(src, dst, copy_sem.at[k])
        copy.start()
        keep.append(copy)

    for n in KV_PIECES:
        chunk_in(n, CHUNKS[0])
    pass_on(Q_PIECES, CHUNKS[0])
    for c in CHUNKS[1:]:
        for n in KV_PIECES:
            chunk_in(n, c)
    pass_on(Q_PIECES, CHUNKS[1])
    for c in CHUNKS:
        for n in KV_PIECES:
            twin_in(n, c)
    store(5, w.at[2], w_out.at[2])

    def project(part):
        def add(k, total):
            lhs = tok[:, pl.ds(pl.multiple_of(k * 2048, 2048), 2048)]
            rows = w[part, lax.div(k, 2), pl.ds(lax.rem(k, 2) * 2, 2)].reshape(2048, 256)
            return total + jnp.dot(lhs, rows, preferred_element_type=F32)

        return lax.fori_loop(0, 4, add, jnp.zeros((256, 256), F32))

    both = project(2)
    cos, sin = tables[0], tables[1]
    ctx = lax.axis_index("ctx")
    key = both[:, 0:128]
    kv_out[ctx, :, 0:128] = (key * cos + turn_half(key) * sin).astype(BF16)
    kv_out[ctx, :, 128:256] = both[:, 128:256].astype(BF16)
    peers = ctx_peers()
    for k in (4, 2, 6, 1, 3, 5, 7):
        links.launch(("kv", k), kv_out.at[ctx], kv_out.at[ctx], peers[k - 1])

    pass_on(Q_PIECES, CHUNKS[2])
    pass_on(Q_PIECES, CHUNKS[3])
    lax.fori_loop(4, 8, turn, 0)
    store(8, turned, turned_out)
    for c in CHUNKS:
        for n in Q_PIECES:
            chunk_in(n, c)
    for part in range(2):
        for c in CHUNKS:
            for n in Q_PARTS[part]:
                twin_in(n, c)
        store(6 + part, w.at[part], w_out.at[part])
        both = project(part)
        for h in range(2):
            query = both[:, h * 128 : h * 128 + 128]
            rotated = (query * cos + turn_half(query) * sin).astype(BF16)
            q_out[:, part * 256 + h * 128 : part * 256 + h * 128 + 128] = rotated
    for k in range(1, 8):
        links.arrival(("kv", k), kv_out.at[lax.rem(ctx + 8 - k, 8)])
    for copy in keep:
        copy.wait()
    links.finish()


def gather_weights(tokens, wq, wk, wv, tables):
    vmem, anywhere = pl.BlockSpec(memory_space=pltpu.VMEM), pl.BlockSpec(memory_space=pl.ANY)
    shape = jax.ShapeDtypeStruct
    return pl.pallas_call(
        gather_kernel,
        out_shape=(
            shape((3, 2, 4, 2, 2, 4, 64, 256), BF16),
            shape((8, 512, 512), BF16),
            shape((256, 512), BF16),
            shape((8, 256, 256), BF16),
        ),
        in_specs=[anywhere] * 5,
        out_specs=(anywhere, anywhere, vmem, vmem),
        scratch_shapes=[
            pltpu.VMEM((3, 2, 4, 2, 2, 4, 64, 256), BF16),
            pltpu.VMEM((256, 8192), BF16),
            pltpu.VMEM((8, 256, 512), BF16),
            pltpu.VMEM((8, 512, 512), BF16),
            pltpu.VMEM((64, 512), F32),
            pltpu.VMEM((64, 128), F32),
            pltpu.VMEM((64, 128), F32),
            pltpu.VMEM((2, 256, 128), F32),
            pltpu.SemaphoreType.DMA((9,)),
            pltpu.SemaphoreType.DMA((212,)),
            pltpu.SemaphoreType.DMA((212,)),
        ],
        compiler_params=pltpu.CompilerParams(
            collective_id=0, has_side_effects=True, vmem_limit_bytes=60 * 2**20
        ),
        name="gather_weights",
    )(tokens, wq, wk, wv, tables)


def attention_kernel(
    positions, own_positions, q, kv, grad, tables,
    attention, grad_q, terms,
    qs, gs, gs_t, keys_t, values_t, scores, top, total, att_t, gq_t,
):
    for h in range(4):
        rows = slice(h * 256, h * 256 + 256)
        qs[rows] = q[:, h * 128 : h * 128 + 128]
        gs[rows] = grad[:, h * 128 : h * 128 + 128]
        gs_t[:, rows] = grad[:, h * 128 : h * 128 + 128].T
    for k in range(8):
        cols = slice(k * 256, k * 256 + 256)
        keys_t[:, cols] = kv[k, :, 0:128].T
        values_t[:, cols] = kv[k, :, 128:256].T
    nt = (((1,), (1,)), ((), ()))
    lead = own_positions[...] - lax.broadcasted_iota(jnp.int32, (128, 256), 0)
    top[...] = jnp.full(top.shape, MASKED, F32)

    def score(k, _):
        for h in range(4):
            cols = slice(h * 256, h * 256 + 256)
            s = lax.dot_general(kv[k, :, 0:128], qs[cols], nt, preferred_element_type=F32)
            upper = jnp.where(lead >= positions[k * 256], s[0:128], MASKED)
            lower = jnp.where(lead >= positions[k * 256 + 128], s[128:256], MASKED)
            scores[k, 0:128, cols] = upper
            scores[k, 128:256, cols] = lower
            high = jnp.max(jnp.maximum(upper, lower), axis=0, keepdims=True)
            top[:, cols] = jnp.maximum(top[:, cols], high)
        return 0

    lax.fori_loop(0, 8, score, 0)
    total[...] = jnp.zeros(total.shape, F32)
    att_t[...] = jnp.zeros(att_t.shape, F32)

    def weigh(k, _):
        at = pl.ds(pl.multiple_of(k * 256, 256), 256)
        for h in range(4):
            cols = slice(h * 256, h * 256 + 256)
            weight = jnp.exp2((scores[k, :, cols] - top[:, cols]) * (SCALE * LOG2E))
            scores[k, :, cols] = weight
            total[:, cols] += jnp.sum(weight, axis=0, keepdims=True)
            att_t[:, cols] += jnp.dot(values_t[:, at], weight.astype(BF16), preferred_element_type=F32)
        return 0

    lax.fori_loop(0, 8, weigh, 0)
    for h in range(4):
        cols = slice(h * 256, h * 256 + 256)
        inverse = 1.0 / total[:, cols]
        out = (att_t[:, cols] / total[:, cols]).astype(BF16)
        attention[:, h * 128 : h * 128 + 128] = out.T
        total[:, cols] = inverse
        top[:, cols] = jnp.sum(gs_t[:, cols].astype(F32) * out.astype(F32), axis=0, keepdims=True)
    gq_t[...] = jnp.zeros(gq_t.shape, F32)

    def back(k, _):
        at = pl.ds(pl.multiple_of(k * 256, 256), 256)
        key_term = jnp.zeros((256, 128), F32)
        value_term = jnp.zeros((256, 128), F32)
        for h in range(4):
            cols = slice(h * 256, h * 256 + 256)
            probs = scores[k, :, cols] * total[:, cols]
            grad_probs = lax.dot_general(kv[k, :, 128:256], gs[cols], nt, preferred_element_type=F32)
            dscore = (probs * (grad_probs - top[:, cols])).astype(BF16)
            key_term += jnp.dot(dscore, qs[cols], preferred_element_type=F32)
            value_term += jnp.dot(probs.astype(BF16), gs[cols], preferred_element_type=F32)
            gq_t[:, cols] += jnp.dot(keys_t[:, at], dscore, preferred_element_type=F32)
        terms[k, :, 0:128] = (key_term * SCALE).astype(BF16)
        terms[k, :, 128:256] = value_term.astype(BF16)
        return 0

    lax.fori_loop(0, 8, back, 0)
    for h in range(4):
        a = gq_t[:, h * 256 : h * 256 + 256].T * SCALE
        unrotated = a * tables[0] - turn_half(a) * tables[1]
        grad_q[:, h * 128 : h * 128 + 128] = unrotated.astype(BF16)


def attend(positions, own_positions, q, kv, grad, tables):
    vmem = pl.BlockSpec(memory_space=pltpu.VMEM)
    shape = jax.ShapeDtypeStruct
    return pl.pallas_call(
        attention_kernel,
        out_shape=(shape((256, 512), BF16), shape((256, 512), BF16), shape((8, 256, 256), BF16)),
        in_specs=[pl.BlockSpec(memory_space=pltpu.SMEM)] + [vmem] * 5,
        out_specs=(vmem, vmem, vmem),
        scratch_shapes=[
            pltpu.VMEM((1024, 128), BF16),
            pltpu.VMEM((1024, 128), BF16),
            pltpu.VMEM((128, 1024), BF16),
            pltpu.VMEM((128, 2048), BF16),
            pltpu.VMEM((128, 2048), BF16),
            pltpu.VMEM((8, 256, 1024), F32),
            pltpu.VMEM((1, 1024), F32),
            pltpu.VMEM((1, 1024), F32),
            pltpu.VMEM((128, 1024), F32),
            pltpu.VMEM((128, 1024), F32),
        ],
        compiler_params=pltpu.CompilerParams(vmem_limit_bytes=32 * 2**20),
        name="attend",
    )(positions, own_positions, q, kv, grad, tables)


def scatter_kernel(
    turned, w_all, grad_q, terms, tables,
    tokens_out, out,
    held, w, grads, landed, grad_tok, copy_sem, send, recv, *buffers,
):
    me = place()
    core = me["core"]
    ctx = lax.axis_index("ctx")
    twin = device(sibling(me))
    links = Links(send, recv, twin)
    accs = [buffers[7 * n : 7 * n + 3] for n in range(len(PIECES))]
    ends = [buffers[7 * n + 3 : 7 * n + 6] for n in range(len(PIECES))]
    vias = [buffers[7 * n + 6] for n in range(len(PIECES))]
    load = pltpu.make_async_copy(turned, held, copy_sem.at[0])
    load.start()
    load_w = pltpu.make_async_copy(w_all, w, copy_sem.at[1])
    load_w.start()
    greet(partners(me))
    links.launch("grad_q", grad_q, grads.at[1, :, pl.ds(0, 512)], twin)
    peers = ctx_peers()
    for k in (4, 2, 6, 1, 3, 5, 7):
        links.launch(("kv", k), terms.at[lax.rem(ctx + k, 8)], landed.at[k - 1], peers[k - 1])
    grads[0, :, 0:512] = grad_q[...]
    load.wait()
    links.arrival("grad_q", grads.at[1, :, pl.ds(0, 512)])

    def axes(n):
        return tuple(reversed(PIECES[n][5]))

    def to(n, phase, by):
        return device(moved(me, axes(n)[phase], by))

    def at(n, phase, by=0):
        axis = axes(n)[phase]
        return moved(me, axis, by)[axis]

    def product(pieces, x, y):
        part = PIECES[pieces[0]][0]
        k = lax.div(x, 2) * 4 + y
        lhs = held[k, pl.ds(pl.multiple_of(lax.rem(x, 2) * 256, 256), 256)]
        rhs = grads[:, :, part * 256 : part * 256 + 256].reshape(512, 256)
        term = jnp.dot(lhs, rhs, preferred_element_type=F32).astype(BF16)
        for n in pieces:
            _, row, rows, col, cols, _ = PIECES[n]
            for z in range(4):
                first, second, third = ({"x": x, "y": y, "z": z}[axis] for axis in axes(n))
                start = z * 64 + row
                if n in KV_PIECES:
                    accs[n][0][first, second, third] = term[start : start + rows, col : col + cols]
                    continue
                for half in range(2):
                    start = z * 64 + row + half * (rows // 2)
                    accs[n][0][first, half, second, third] = term[
                        start : start + rows // 2, col : col + cols
                    ]

    CHUNKS = (2, 1, -1, 0)

    def products(pieces):
        def one(k, _):
            product(pieces, lax.div(k, 4), lax.rem(k, 4))
            return 0

        lax.fori_loop(0, 16, one, 0)

    def send_direct(n, c):
        j = at(n, 1, c)
        for s, by in enumerate(BYS):
            src = accs[n][0].at[at(n, 0, by), j]
            links.launch((n, 0, c, s), src, ends[n][0].at[s, j], to(n, 0, by))

    def send_far(n, c):
        j = at(n, 1, c)
        for d, by in enumerate((1, -1)):
            src = accs[n][0].at[at(n, 0, 2), d, j]
            links.launch((n, "via", c, d), src, vias[n].at[d, j], to(n, 0, by))

    def send_near(n, c):
        j = at(n, 1, c)
        for d, by in enumerate((1, -1)):
            src = accs[n][0].at[at(n, 0, by), 1 - d, j]
            links.launch((n, "end", c, d, 1 - d), src, ends[n][0].at[d, 1 - d, j], to(n, 0, by))

    def relay(n, c):
        j = at(n, 1, c)
        acc, via, end = accs[n][0], vias[n], ends[n][0]
        for d, by in enumerate((1, -1)):
            links.arrival((n, "via", c, d), via.at[d, j])
            i = at(n, 0, by)
            acc[i, d, j] = (acc[i, d, j].astype(F32) + via[d, j].astype(F32)).astype(BF16)
            links.launch((n, "end", c, d, d), acc.at[i, d, j], end.at[d, d, j], to(n, 0, by))

    def chunk_in(n, c):
        j = at(n, 1, c)
        acc, end = accs[n][0], ends[n][0]
        rows = PIECES[n][2] // 2
        if n in KV_PIECES:
            for s in range(3):
                links.arrival((n, 0, c, s), end.at[s, j])
            total = acc[at(n, 0), j].astype(F32)
            for s in range(3):
                total = total + end[s, j].astype(F32)
            accs[n][1][j] = total.astype(BF16)
        for h in range(2) if n in Q_PIECES else ():
            for d in range(2):
                links.arrival((n, "end", c, d, h), end.at[d, h, j])
            total = acc[at(n, 0), h, j].astype(F32)
            total = total + end[0, h, j].astype(F32) + end[1, h, j].astype(F32)
            accs[n][1][j, :, h * rows : h * rows + rows] = total.astype(BF16)
        if c != 0:
            s = BYS.index(c)
            links.launch((n, 1, s), accs[n][1].at[j], ends[n][1].at[s], to(n, 1, c))

    def summed(n, phase):
        total = accs[n][phase][at(n, phase)].astype(F32)
        for s in range(3):
            total = total + ends[n][phase][s].astype(F32)
        return total

    def second(n):
        for s in range(3):
            links.arrival((n, 1, s), ends[n][1].at[s])
        accs[n][2][...] = summed(n, 1).astype(BF16)
        for s, by in enumerate(BYS):
            links.launch((n, 2, s), accs[n][2].at[at(n, 2, by)], ends[n][2].at[s], to(n, 2, by))

    def last(n):
        part, row, rows, col, cols, _ = PIECES[n]
        for s in range(3):
            links.arrival((n, 2, s), ends[n][2].at[s])
        out[row : row + rows, part * 256 + col : part * 256 + col + cols] = summed(n, 2)

    for pieces in Q_PARTS:
        products(pieces)
        for c in CHUNKS:
            for n in pieces:
                send_far(n, c)
    for c in CHUNKS:
        for n in Q_PIECES:
            send_near(n, c)
    for c in CHUNKS:
        for n in Q_PIECES:
            if axes(n)[0] != "z":
                relay(n, c)

    def input_slice(k, _):
        total = None
        for part in range(3):
            lhs = grads[0, :, part * 256 : part * 256 + 256]
            rows = w[part, lax.div(k, 8), lax.rem(lax.div(k, 2), 4), lax.rem(k, 2)].reshape(512, 256)
            term = lax.dot_general(lhs, rows, (((1,), (1,)), ((), ())), preferred_element_type=F32)
            total = term if total is None else total + term
        grad_tok[:, pl.ds(pl.multiple_of(k * 512, 512), 512)] = total.astype(BF16)
        return 0

    stores = []

    def inputs(quarter):
        lax.fori_loop(quarter * 4, quarter * 4 + 4, input_slice, 0)
        cols = pl.ds(quarter * 2048, 2048)
        copy = pltpu.make_async_copy(grad_tok.at[:, cols], tokens_out.at[:, cols], copy_sem.at[2 + quarter])
        copy.start()
        stores.append(copy)

    for k in range(1, 8):
        links.arrival(("kv", k), landed.at[k - 1])
    keyval = terms[ctx].astype(F32)
    for k in range(7):
        keyval = keyval + landed[k].astype(F32)
    key = keyval[:, 0:128]
    grads[0, :, 512:640] = (key * tables[0] - turn_half(key) * tables[1]).astype(BF16)
    grads[0, :, 640:768] = keyval[:, 128:256].astype(BF16)
    columns = pl.ds(512, 256)
    links.launch("grad_kv", grads.at[0, :, columns], grads.at[1, :, columns], twin)
    for c in CHUNKS:
        for n in Q_PIECES:
            if axes(n)[0] == "z":
                relay(n, c)
    load_w.wait()
    inputs(0)
    links.arrival("grad_kv", grads.at[1, :, columns])

    products(KV_PIECES)
    for c in CHUNKS:
        for n in KV_PIECES:
            send_direct(n, c)
    for k, c in enumerate(CHUNKS):
        for n in Q_PIECES:
            chunk_in(n, c)
        if k < 3:
            inputs(k + 1)
    for n in Q_PIECES:
        second(n)
    for c in CHUNKS:
        for n in KV_PIECES:
            chunk_in(n, c)
    for n in KV_PIECES:
        second(n)
    for n in Q_PIECES + KV_PIECES:
        last(n)
    for copy in stores:
        copy.wait()
    links.finish()


def scatter_grads(turned, w_all, grad_q, terms, tables):
    vmem, anywhere = pl.BlockSpec(memory_space=pltpu.VMEM), pl.BlockSpec(memory_space=pl.ANY)
    shape = jax.ShapeDtypeStruct
    buffers = []
    for n, (_, _, rows, _, cols, _) in enumerate(PIECES):
        half, whole = (rows // 2, cols), (rows, cols)
        later = ((4, 4) + whole, (4,) + whole), ((3, 4) + whole, (3,) + whole)
        if n in KV_PIECES:
            first = (4, 4, 4) + whole, (3, 4, 4) + whole, (8, 128)
        else:
            first = (4, 2, 4, 4) + half, (2, 2, 4, 4) + half, (2, 4, 4) + half
        for shape_of in (first[0], *later[0], first[1], *later[1], first[2]):
            buffers.append(pltpu.VMEM(shape_of, BF16))
    return pl.pallas_call(
        scatter_kernel,
        out_shape=(shape((256, 8192), BF16), shape((64, 768), F32)),
        in_specs=[anywhere, anywhere, vmem, vmem, vmem],
        out_specs=(anywhere, vmem),
        scratch_shapes=[
            pltpu.VMEM((8, 512, 512), BF16),
            pltpu.VMEM((3, 2, 4, 2, 2, 4, 64, 256), BF16),
            pltpu.VMEM((2, 256, 768), BF16),
            pltpu.VMEM((7, 256, 256), BF16),
            pltpu.VMEM((256, 8192), BF16),
            pltpu.SemaphoreType.DMA((6,)),
            pltpu.SemaphoreType.DMA((216,)),
            pltpu.SemaphoreType.DMA((216,)),
            *buffers,
        ],
        compiler_params=pltpu.CompilerParams(
            collective_id=1, has_side_effects=True, vmem_limit_bytes=48 * 2**20
        ),
        name="scatter_grads",
    )(turned, w_all, grad_q, terms, tables)


def rope_tables(positions_in, head_dim):
    half_width = head_dim // 2
    exponent = jnp.arange(half_width).astype(F32) * (2.0 / head_dim)
    frequency = jnp.power(ROPE_BASE, -exponent)
    angles = positions_in.astype(F32)[:, None] * frequency[None, :]
    cos, sin = jnp.cos(angles), jnp.sin(angles)
    return jnp.stack([jnp.concatenate([cos, cos], axis=1), jnp.concatenate([-sin, sin], axis=1)])


def body(tokens, positions, query_weight, key_weight, value_weight, grad_output):
    own_positions = lax.dynamic_slice_in_dim(positions, lax.axis_index("ctx") * 256, 256)
    tables = rope_tables(own_positions, 128)
    w_all, turned, q, kv = gather_weights(
        tokens[0], query_weight, key_weight, value_weight, tables
    )
    attention, grad_q, terms = attend(
        positions, own_positions[None], q, kv, grad_output[0], tables
    )
    grad_tokens, grads = scatter_grads(turned, w_all, grad_q, terms, tables)
    return attention[None], grad_tokens[None], grads[:, :512], grads[:, 512:640], grads[:, 640:]


def solution(mesh):
    in_specs = (
        P("dp", "ctx", None),
        P(),
        P(("dp", "ctx"), None),
        P(("dp", "ctx"), None),
        P(("dp", "ctx"), None),
        P("dp", "ctx", None),
    )
    out_specs = (
        P("dp", "ctx", None),
        P("dp", "ctx", None),
        P(("dp", "ctx"), None),
        P(("dp", "ctx"), None),
        P(("dp", "ctx"), None),
    )
    return jax.shard_map(body, mesh=mesh, in_specs=in_specs, out_specs=out_specs, check_vma=False)
```

```python
import functools

import jax
import jax.numpy as jnp
from jax import lax
from jax.experimental import pallas as pl
from jax.experimental.pallas import tpu as pltpu
from jax.sharding import PartitionSpec as P

ROPE_BASE = 1000000.0
MASKED = -1e30
MESH = pl.DeviceIdType.MESH
BF16 = jnp.bfloat16
F32 = jnp.float32
AXES = ("x", "y", "z")
PIECES = (
    (2, 0, 48, 0, 128, ("z", "y", "x")),
    (2, 0, 48, 128, 128, ("x", "z", "y")),
    (2, 48, 16, 0, 256, ("y", "x", "z")),
    (0, 0, 64, 0, 128, ("z", "y", "x")),
    (0, 0, 64, 128, 128, ("x", "z", "y")),
    (1, 0, 64, 0, 128, ("y", "x", "z")),
    (1, 0, 32, 128, 128, ("y", "z", "x")),
    (1, 32, 32, 128, 128, ("z", "x", "y")),
)
KV_PIECES = (0, 1, 2)
Q_PIECES = (3, 4, 5, 6, 7)
Q_PARTS = ((3, 4), (5, 6, 7))
SCALE = 128 ** (-0.5)
LOG2E = 1.4426950408889634


def place():
    dp, ctx = lax.axis_index("dp"), lax.axis_index("ctx")
    return {
        "x": lax.div(dp, 8) * 2 + lax.div(ctx, 4),
        "y": lax.rem(lax.div(dp, 2), 4),
        "z": lax.rem(ctx, 4),
        "core": lax.rem(dp, 2),
    }


def device(at):
    return (
        lax.div(at["x"], 2) * 8 + at["y"] * 2 + at["core"],
        lax.rem(at["x"], 2) * 4 + at["z"],
    )


def moved(at, axis, by):
    return {**at, axis: lax.rem(at[axis] + 4 + by, 4)}


def sibling(at):
    return {**at, "core": 1 - at["core"]}


def greet(targets):
    barrier = pltpu.get_barrier_semaphore()
    for target in targets:
        pl.semaphore_signal(barrier, inc=1, device_id=target, device_id_type=MESH)
    pl.semaphore_wait(barrier, len(targets))


def partners(at):
    near = [device(moved(at, axis, by)) for axis in AXES for by in (1, -1, 2)]
    return near + [device(sibling(at))] + ctx_peers()


def ctx_peers():
    dp, ctx = lax.axis_index("dp"), lax.axis_index("ctx")
    return [(dp, lax.rem(ctx + k, 8)) for k in range(1, 8)]


def remote(src, dst, send, recv, target):
    return pltpu.make_async_remote_copy(
        src_ref=src, dst_ref=dst, send_sem=send, recv_sem=recv, device_id=target, device_id_type=MESH
    )


class Links:
    def __init__(self, send, recv, twin):
        self.send, self.recv, self.twin = send, recv, twin
        self.slots, self.started = {}, []

    def slot(self, key):
        return self.slots.setdefault(key, len(self.slots))

    def launch(self, key, src, dst, target):
        k = self.slot(key)
        copy = remote(src, dst, self.send.at[k], self.recv.at[k], target)
        copy.start()
        self.started.append(copy)

    def arrival(self, key, ref):
        k = self.slot(key)
        remote(ref, ref, self.send.at[k], self.recv.at[k], self.twin).wait_recv()

    def finish(self):
        for copy in self.started:
            copy.wait_send()


def turn_half(a):
    return pltpu.roll(a, 64, 1)


BYS = (2, 1, -1)


def gather_kernel(
    tokens, wq_hbm, wk_hbm, wv_hbm, tables_hbm,
    w_out, turned_out, q_out, kv_out,
    w, tok, twin_tok, turned, wq, wk, wv, tables, copy_sem, send, recv,
):
    me = place()
    core = me["core"]
    twin = device(sibling(me))
    links = Links(send, recv, twin)
    loads = [
        pltpu.make_async_copy(src, dst, copy_sem.at[k])
        for k, (src, dst) in enumerate(
            ((wq_hbm, wq), (wk_hbm, wk), (wv_hbm, wv), (tables_hbm, tables), (tokens, tok))
        )
    ]
    for copy in loads:
        copy.start()
    for copy in loads[:3]:
        copy.wait()
    x_hi, x_lo = lax.div(me["x"], 2), lax.rem(me["x"], 2)
    w[2, x_hi, me["y"], core, x_lo, me["z"], :, 0:128] = wk[...].astype(BF16)
    w[2, x_hi, me["y"], core, x_lo, me["z"], :, 128:256] = wv[...].astype(BF16)
    w[0, x_hi, me["y"], core, x_lo, me["z"]] = wq[:, 0:256].astype(BF16)
    w[1, x_hi, me["y"], core, x_lo, me["z"]] = wq[:, 256:512].astype(BF16)

    def block(n, first, second, third, core_at=core):
        part, row, rows, col, cols, order = PIECES[n]
        at = dict(zip(order, (first, second, third)))
        x, y, z = (at[axis] for axis in AXES)
        return w.at[
            part,
            slice(None) if x is None else lax.div(x, 2),
            slice(None) if y is None else y,
            core_at,
            slice(None) if x is None else lax.rem(x, 2),
            slice(None) if z is None else z,
            pl.ds(row, rows),
            pl.ds(col, cols),
        ]

    def to(n, phase, by):
        return device(moved(me, PIECES[n][5][phase], by))

    def index(n, phase, by=0):
        axis = PIECES[n][5][phase]
        return moved(me, axis, by)[axis]

    greet(partners(me))
    everything = KV_PIECES + Q_PIECES
    for n in everything:
        mine = block(n, index(n, 0), index(n, 1), index(n, 2))
        for by in BYS:
            links.launch((n, 0, by), mine, mine, to(n, 0, by))
    for k in range(8):
        columns = tokens.at[:, pl.ds(pl.multiple_of(k * 1024 + (1 - core) * 512, 512), 512)]
        links.launch(("tokens", k), columns, twin_tok.at[k], twin)

    def send_chunk(n, c):
        chunk = block(n, None, index(n, 1, c), index(n, 2))
        for by in BYS:
            links.launch((n, 2, c, by), chunk, chunk, to(n, 2, by))

    for n in everything:
        second, third = index(n, 1), index(n, 2)
        for by in BYS:
            links.arrival((n, 0, by), block(n, index(n, 0, -by), second, third))
        line = block(n, None, second, third)
        for by in BYS:
            links.launch((n, 1, by), line, line, to(n, 1, by))
        send_chunk(n, 0)
    for n in everything:
        for by in BYS:
            links.arrival((n, 1, by), block(n, None, index(n, 1, -by), index(n, 2)))
            send_chunk(n, -by)

    CHUNKS = (0,) + tuple(-by for by in BYS)

    def chunk_in(n, c):
        second = index(n, 1, c)
        for by in BYS:
            links.arrival((n, 2, c, by), block(n, None, second, index(n, 2, -by)))
        whole = block(n, None, second, None)
        links.launch((n, "twin", c), whole, whole, twin)

    def twin_in(n, c):
        links.arrival((n, "twin", c), block(n, None, index(n, 1, c), None, 1 - core))

    for copy in loads[3:]:
        copy.wait()
    for k in range(8):
        links.arrival(("tokens", k), twin_tok.at[k])

    def turn(k, _):
        at = pl.multiple_of(k * 1024 + core * 512, 512)
        turned[k, :, 0:256] = tok[:, pl.ds(at, 512)].T
        turned[k, :, 256:512] = twin_tok[k].T
        return 0

    lax.fori_loop(0, 4, turn, 0)
    keep = []

    def store(k, src, dst):
        copy = pltpu.make_async_copy(src, dst, copy_sem.at[k])
        copy.start()
        keep.append(copy)

    for c in CHUNKS:
        for n in KV_PIECES:
            chunk_in(n, c)
    for c in CHUNKS:
        for n in KV_PIECES:
            twin_in(n, c)
    store(5, w.at[2], w_out.at[2])

    def project(part):
        def add(k, total):
            lhs = tok[:, pl.ds(pl.multiple_of(k * 2048, 2048), 2048)]
            rows = w[part, lax.div(k, 2), pl.ds(lax.rem(k, 2) * 2, 2)].reshape(2048, 256)
            return total + jnp.dot(lhs, rows, preferred_element_type=F32)

        return lax.fori_loop(0, 4, add, jnp.zeros((256, 256), F32))

    both = project(2)
    cos, sin = tables[0], tables[1]
    ctx = lax.axis_index("ctx")
    key = both[:, 0:128]
    kv_out[ctx, :, 0:128] = (key * cos + turn_half(key) * sin).astype(BF16)
    kv_out[ctx, :, 128:256] = both[:, 128:256].astype(BF16)
    peers = ctx_peers()
    for k in (4, 2, 6, 1, 3, 5, 7):
        links.launch(("kv", k), kv_out.at[ctx], kv_out.at[ctx], peers[k - 1])

    lax.fori_loop(4, 8, turn, 0)
    store(8, turned, turned_out)
    for c in CHUNKS:
        for n in Q_PIECES:
            chunk_in(n, c)
    for part in range(2):
        for c in CHUNKS:
            for n in Q_PARTS[part]:
                twin_in(n, c)
        store(6 + part, w.at[part], w_out.at[part])
        both = project(part)
        for h in range(2):
            query = both[:, h * 128 : h * 128 + 128]
            rotated = (query * cos + turn_half(query) * sin).astype(BF16)
            q_out[:, part * 256 + h * 128 : part * 256 + h * 128 + 128] = rotated
    for k in range(1, 8):
        links.arrival(("kv", k), kv_out.at[lax.rem(ctx + 8 - k, 8)])
    for copy in keep:
        copy.wait()
    links.finish()


def gather_weights(tokens, wq, wk, wv, tables):
    vmem, anywhere = pl.BlockSpec(memory_space=pltpu.VMEM), pl.BlockSpec(memory_space=pl.ANY)
    shape = jax.ShapeDtypeStruct
    return pl.pallas_call(
        gather_kernel,
        out_shape=(
            shape((3, 2, 4, 2, 2, 4, 64, 256), BF16),
            shape((8, 512, 512), BF16),
            shape((256, 512), BF16),
            shape((8, 256, 256), BF16),
        ),
        in_specs=[anywhere] * 5,
        out_specs=(anywhere, anywhere, vmem, vmem),
        scratch_shapes=[
            pltpu.VMEM((3, 2, 4, 2, 2, 4, 64, 256), BF16),
            pltpu.VMEM((256, 8192), BF16),
            pltpu.VMEM((8, 256, 512), BF16),
            pltpu.VMEM((8, 512, 512), BF16),
            pltpu.VMEM((64, 512), F32),
            pltpu.VMEM((64, 128), F32),
            pltpu.VMEM((64, 128), F32),
            pltpu.VMEM((2, 256, 128), F32),
            pltpu.SemaphoreType.DMA((9,)),
            pltpu.SemaphoreType.DMA((212,)),
            pltpu.SemaphoreType.DMA((212,)),
        ],
        compiler_params=pltpu.CompilerParams(
            collective_id=0, has_side_effects=True, vmem_limit_bytes=60 * 2**20
        ),
        name="gather_weights",
    )(tokens, wq, wk, wv, tables)


def attention_kernel(
    positions, own_positions, q, kv, grad, tables,
    attention, grad_q, terms,
    qs, gs, gs_t, keys_t, values_t, scores, top, total, att_t, gq_t,
):
    for h in range(4):
        rows = slice(h * 256, h * 256 + 256)
        qs[rows] = q[:, h * 128 : h * 128 + 128]
        gs[rows] = grad[:, h * 128 : h * 128 + 128]
        gs_t[:, rows] = grad[:, h * 128 : h * 128 + 128].T
    for k in range(8):
        cols = slice(k * 256, k * 256 + 256)
        keys_t[:, cols] = kv[k, :, 0:128].T
        values_t[:, cols] = kv[k, :, 128:256].T
    nt = (((1,), (1,)), ((), ()))
    lead = own_positions[...] - lax.broadcasted_iota(jnp.int32, (128, 256), 0)
    top[...] = jnp.full(top.shape, MASKED, F32)

    def tile(k, cols):
        return kv[pl.ds(k * 2, 2), :, cols].reshape(512, 128)

    def score(k, _):
        for h in range(4):
            cols = slice(h * 256, h * 256 + 256)
            s = lax.dot_general(tile(k, slice(0, 128)), qs[cols], nt, preferred_element_type=F32)
            high = None
            for r in range(4):
                rows = slice(r * 128, r * 128 + 128)
                run = jnp.where(lead >= positions[k * 512 + r * 128], s[rows], MASKED)
                scores[k, rows, cols] = run
                high = run if high is None else jnp.maximum(high, run)
            top[:, cols] = jnp.maximum(top[:, cols], jnp.max(high, axis=0, keepdims=True))
        return 0

    lax.fori_loop(0, 4, score, 0)
    total[...] = jnp.zeros(total.shape, F32)
    att_t[...] = jnp.zeros(att_t.shape, F32)

    def weigh(k, _):
        at = pl.ds(pl.multiple_of(k * 512, 512), 512)
        for h in range(4):
            cols = slice(h * 256, h * 256 + 256)
            weight = jnp.exp2((scores[k, :, cols] - top[:, cols]) * (SCALE * LOG2E))
            scores[k, :, cols] = weight
            total[:, cols] += jnp.sum(weight, axis=0, keepdims=True)
            att_t[:, cols] += jnp.dot(values_t[:, at], weight.astype(BF16), preferred_element_type=F32)
        return 0

    lax.fori_loop(0, 4, weigh, 0)
    for h in range(4):
        cols = slice(h * 256, h * 256 + 256)
        inverse = 1.0 / total[:, cols]
        out = (att_t[:, cols] / total[:, cols]).astype(BF16)
        attention[:, h * 128 : h * 128 + 128] = out.T
        total[:, cols] = inverse
        top[:, cols] = jnp.sum(gs_t[:, cols].astype(F32) * out.astype(F32), axis=0, keepdims=True)
    gq_t[...] = jnp.zeros(gq_t.shape, F32)

    def back(k, _):
        at = pl.ds(pl.multiple_of(k * 512, 512), 512)
        key_term = jnp.zeros((512, 128), F32)
        value_term = jnp.zeros((512, 128), F32)
        for h in range(4):
            cols = slice(h * 256, h * 256 + 256)
            probs = scores[k, :, cols] * total[:, cols]
            grad_probs = lax.dot_general(tile(k, slice(128, 256)), gs[cols], nt, preferred_element_type=F32)
            dscore = (probs * (grad_probs - top[:, cols])).astype(BF16)
            key_term += jnp.dot(dscore, qs[cols], preferred_element_type=F32)
            value_term += jnp.dot(probs.astype(BF16), gs[cols], preferred_element_type=F32)
            gq_t[:, cols] += jnp.dot(keys_t[:, at], dscore, preferred_element_type=F32)
        terms[pl.ds(k * 2, 2), :, 0:128] = (key_term * SCALE).astype(BF16).reshape(2, 256, 128)
        terms[pl.ds(k * 2, 2), :, 128:256] = value_term.astype(BF16).reshape(2, 256, 128)
        return 0

    lax.fori_loop(0, 4, back, 0)
    for h in range(4):
        a = gq_t[:, h * 256 : h * 256 + 256].T * SCALE
        unrotated = a * tables[0] - turn_half(a) * tables[1]
        grad_q[:, h * 128 : h * 128 + 128] = unrotated.astype(BF16)


def attend(positions, own_positions, q, kv, grad, tables):
    vmem = pl.BlockSpec(memory_space=pltpu.VMEM)
    shape = jax.ShapeDtypeStruct
    return pl.pallas_call(
        attention_kernel,
        out_shape=(shape((256, 512), BF16), shape((256, 512), BF16), shape((8, 256, 256), BF16)),
        in_specs=[pl.BlockSpec(memory_space=pltpu.SMEM)] + [vmem] * 5,
        out_specs=(vmem, vmem, vmem),
        scratch_shapes=[
            pltpu.VMEM((1024, 128), BF16),
            pltpu.VMEM((1024, 128), BF16),
            pltpu.VMEM((128, 1024), BF16),
            pltpu.VMEM((128, 2048), BF16),
            pltpu.VMEM((128, 2048), BF16),
            pltpu.VMEM((4, 512, 1024), F32),
            pltpu.VMEM((1, 1024), F32),
            pltpu.VMEM((1, 1024), F32),
            pltpu.VMEM((128, 1024), F32),
            pltpu.VMEM((128, 1024), F32),
        ],
        compiler_params=pltpu.CompilerParams(vmem_limit_bytes=32 * 2**20),
        name="attend",
    )(positions, own_positions, q, kv, grad, tables)


def scatter_kernel(
    turned, w_all, grad_q, terms, tables,
    tokens_out, out,
    held, w, grads, landed, grad_tok, copy_sem, send, recv, *buffers,
):
    me = place()
    core = me["core"]
    ctx = lax.axis_index("ctx")
    twin = device(sibling(me))
    links = Links(send, recv, twin)
    accs = [buffers[7 * n : 7 * n + 3] for n in range(len(PIECES))]
    ends = [buffers[7 * n + 3 : 7 * n + 6] for n in range(len(PIECES))]
    vias = [buffers[7 * n + 6] for n in range(len(PIECES))]
    load = pltpu.make_async_copy(turned, held, copy_sem.at[0])
    load.start()
    load_w = pltpu.make_async_copy(w_all, w, copy_sem.at[1])
    load_w.start()
    greet(partners(me))
    links.launch("grad_q", grad_q, grads.at[1, :, pl.ds(0, 512)], twin)
    peers = ctx_peers()
    for k in (4, 2, 6, 1, 3, 5, 7):
        links.launch(("kv", k), terms.at[lax.rem(ctx + k, 8)], landed.at[k - 1], peers[k - 1])
    grads[0, :, 0:512] = grad_q[...]
    load.wait()
    links.arrival("grad_q", grads.at[1, :, pl.ds(0, 512)])

    def axes(n):
        return tuple(reversed(PIECES[n][5]))

    def to(n, phase, by):
        return device(moved(me, axes(n)[phase], by))

    def at(n, phase, by=0):
        axis = axes(n)[phase]
        return moved(me, axis, by)[axis]

    def product(pieces, x, y):
        part = PIECES[pieces[0]][0]
        k = lax.div(x, 2) * 4 + y
        lhs = held[k, pl.ds(pl.multiple_of(lax.rem(x, 2) * 256, 256), 256)]
        rhs = grads[:, :, part * 256 : part * 256 + 256].reshape(512, 256)
        term = jnp.dot(lhs, rhs, preferred_element_type=F32).astype(BF16)
        for n in pieces:
            _, row, rows, col, cols, _ = PIECES[n]
            for z in range(4):
                first, second, third = ({"x": x, "y": y, "z": z}[axis] for axis in axes(n))
                start = z * 64 + row
                if n in KV_PIECES:
                    accs[n][0][first, second, third] = term[start : start + rows, col : col + cols]
                    continue
                for half in range(2):
                    start = z * 64 + row + half * (rows // 2)
                    accs[n][0][first, half, second, third] = term[
                        start : start + rows // 2, col : col + cols
                    ]

    CHUNKS = (2, 1, -1, 0)

    def products(pieces):
        def one(k, _):
            product(pieces, lax.div(k, 4), lax.rem(k, 4))
            return 0

        lax.fori_loop(0, 16, one, 0)

    def send_direct(n, c):
        j = at(n, 1, c)
        for s, by in enumerate(BYS):
            src = accs[n][0].at[at(n, 0, by), j]
            links.launch((n, 0, c, s), src, ends[n][0].at[s, j], to(n, 0, by))

    def send_far(n, c):
        j = at(n, 1, c)
        for d, by in enumerate((1, -1)):
            src = accs[n][0].at[at(n, 0, 2), d, j]
            links.launch((n, "via", c, d), src, vias[n].at[d, j], to(n, 0, by))

    def send_near(n, c):
        j = at(n, 1, c)
        for d, by in enumerate((1, -1)):
            src = accs[n][0].at[at(n, 0, by), 1 - d, j]
            links.launch((n, "end", c, d, 1 - d), src, ends[n][0].at[d, 1 - d, j], to(n, 0, by))

    def relay(n, c):
        j = at(n, 1, c)
        acc, via, end = accs[n][0], vias[n], ends[n][0]
        for d, by in enumerate((1, -1)):
            links.arrival((n, "via", c, d), via.at[d, j])
            i = at(n, 0, by)
            acc[i, d, j] = (acc[i, d, j].astype(F32) + via[d, j].astype(F32)).astype(BF16)
            links.launch((n, "end", c, d, d), acc.at[i, d, j], end.at[d, d, j], to(n, 0, by))

    def chunk_in(n, c):
        j = at(n, 1, c)
        acc, end = accs[n][0], ends[n][0]
        rows = PIECES[n][2] // 2
        if n in KV_PIECES:
            for s in range(3):
                links.arrival((n, 0, c, s), end.at[s, j])
            total = acc[at(n, 0), j].astype(F32)
            for s in range(3):
                total = total + end[s, j].astype(F32)
            accs[n][1][j] = total.astype(BF16)
        for h in range(2) if n in Q_PIECES else ():
            for d in range(2):
                links.arrival((n, "end", c, d, h), end.at[d, h, j])
            total = acc[at(n, 0), h, j].astype(F32)
            total = total + end[0, h, j].astype(F32) + end[1, h, j].astype(F32)
            accs[n][1][j, :, h * rows : h * rows + rows] = total.astype(BF16)
        if c != 0:
            s = BYS.index(c)
            links.launch((n, 1, s), accs[n][1].at[j], ends[n][1].at[s], to(n, 1, c))

    def summed(n, phase):
        total = accs[n][phase][at(n, phase)].astype(F32)
        for s in range(3):
            total = total + ends[n][phase][s].astype(F32)
        return total

    def second(n):
        for s in range(3):
            links.arrival((n, 1, s), ends[n][1].at[s])
        accs[n][2][...] = summed(n, 1).astype(BF16)
        for s, by in enumerate(BYS):
            links.launch((n, 2, s), accs[n][2].at[at(n, 2, by)], ends[n][2].at[s], to(n, 2, by))

    def last(n):
        part, row, rows, col, cols, _ = PIECES[n]
        for s in range(3):
            links.arrival((n, 2, s), ends[n][2].at[s])
        out[row : row + rows, part * 256 + col : part * 256 + col + cols] = summed(n, 2)

    for pieces in Q_PARTS:
        products(pieces)
        for c in CHUNKS:
            for n in pieces:
                send_far(n, c)
    for c in CHUNKS:
        for n in Q_PIECES:
            send_near(n, c)
    for c in CHUNKS:
        for n in Q_PIECES:
            if axes(n)[0] != "z":
                relay(n, c)

    def input_slice(k, _):
        total = None
        for part in range(3):
            lhs = grads[0, :, part * 256 : part * 256 + 256]
            rows = w[part, lax.div(k, 8), lax.rem(lax.div(k, 2), 4), lax.rem(k, 2)].reshape(512, 256)
            term = lax.dot_general(lhs, rows, (((1,), (1,)), ((), ())), preferred_element_type=F32)
            total = term if total is None else total + term
        grad_tok[:, pl.ds(pl.multiple_of(k * 512, 512), 512)] = total.astype(BF16)
        return 0

    stores = []

    def inputs(quarter):
        lax.fori_loop(quarter * 4, quarter * 4 + 4, input_slice, 0)
        cols = pl.ds(quarter * 2048, 2048)
        copy = pltpu.make_async_copy(grad_tok.at[:, cols], tokens_out.at[:, cols], copy_sem.at[2 + quarter])
        copy.start()
        stores.append(copy)

    for k in range(1, 8):
        links.arrival(("kv", k), landed.at[k - 1])
    keyval = terms[ctx].astype(F32)
    for k in range(7):
        keyval = keyval + landed[k].astype(F32)
    key = keyval[:, 0:128]
    grads[0, :, 512:640] = (key * tables[0] - turn_half(key) * tables[1]).astype(BF16)
    grads[0, :, 640:768] = keyval[:, 128:256].astype(BF16)
    columns = pl.ds(512, 256)
    links.launch("grad_kv", grads.at[0, :, columns], grads.at[1, :, columns], twin)
    for c in CHUNKS:
        for n in Q_PIECES:
            if axes(n)[0] == "z":
                relay(n, c)
    load_w.wait()
    inputs(0)
    links.arrival("grad_kv", grads.at[1, :, columns])

    products(KV_PIECES)
    for c in CHUNKS:
        for n in KV_PIECES:
            send_direct(n, c)
    for k, c in enumerate(CHUNKS):
        for n in Q_PIECES:
            chunk_in(n, c)
        if k < 3:
            inputs(k + 1)
    for n in Q_PIECES:
        second(n)
    for c in CHUNKS:
        for n in KV_PIECES:
            chunk_in(n, c)
    for n in KV_PIECES:
        second(n)
    for n in Q_PIECES + KV_PIECES:
        last(n)
    for copy in stores:
        copy.wait()
    links.finish()


def scatter_grads(turned, w_all, grad_q, terms, tables):
    vmem, anywhere = pl.BlockSpec(memory_space=pltpu.VMEM), pl.BlockSpec(memory_space=pl.ANY)
    shape = jax.ShapeDtypeStruct
    buffers = []
    for n, (_, _, rows, _, cols, _) in enumerate(PIECES):
        half, whole = (rows // 2, cols), (rows, cols)
        later = ((4, 4) + whole, (4,) + whole), ((3, 4) + whole, (3,) + whole)
        if n in KV_PIECES:
            first = (4, 4, 4) + whole, (3, 4, 4) + whole, (8, 128)
        else:
            first = (4, 2, 4, 4) + half, (2, 2, 4, 4) + half, (2, 4, 4) + half
        for shape_of in (first[0], *later[0], first[1], *later[1], first[2]):
            buffers.append(pltpu.VMEM(shape_of, BF16))
    return pl.pallas_call(
        scatter_kernel,
        out_shape=(shape((256, 8192), BF16), shape((64, 768), F32)),
        in_specs=[anywhere, anywhere, vmem, vmem, vmem],
        out_specs=(anywhere, vmem),
        scratch_shapes=[
            pltpu.VMEM((8, 512, 512), BF16),
            pltpu.VMEM((3, 2, 4, 2, 2, 4, 64, 256), BF16),
            pltpu.VMEM((2, 256, 768), BF16),
            pltpu.VMEM((7, 256, 256), BF16),
            pltpu.VMEM((256, 8192), BF16),
            pltpu.SemaphoreType.DMA((6,)),
            pltpu.SemaphoreType.DMA((216,)),
            pltpu.SemaphoreType.DMA((216,)),
            *buffers,
        ],
        compiler_params=pltpu.CompilerParams(
            collective_id=1, has_side_effects=True, vmem_limit_bytes=48 * 2**20
        ),
        name="scatter_grads",
    )(turned, w_all, grad_q, terms, tables)


def rope_tables(positions_in, head_dim):
    half_width = head_dim // 2
    exponent = jnp.arange(half_width).astype(F32) * (2.0 / head_dim)
    frequency = jnp.power(ROPE_BASE, -exponent)
    angles = positions_in.astype(F32)[:, None] * frequency[None, :]
    cos, sin = jnp.cos(angles), jnp.sin(angles)
    return jnp.stack([jnp.concatenate([cos, cos], axis=1), jnp.concatenate([-sin, sin], axis=1)])


def body(tokens, positions, query_weight, key_weight, value_weight, grad_output):
    own_positions = lax.dynamic_slice_in_dim(positions, lax.axis_index("ctx") * 256, 256)
    tables = rope_tables(own_positions, 128)
    w_all, turned, q, kv = gather_weights(
        tokens[0], query_weight, key_weight, value_weight, tables
    )
    attention, grad_q, terms = attend(
        positions, own_positions[None], q, kv, grad_output[0], tables
    )
    grad_tokens, grads = scatter_grads(turned, w_all, grad_q, terms, tables)
    return attention[None], grad_tokens[None], grads[:, :512], grads[:, 512:640], grads[:, 640:]


def solution(mesh):
    in_specs = (
        P("dp", "ctx", None),
        P(),
        P(("dp", "ctx"), None),
        P(("dp", "ctx"), None),
        P(("dp", "ctx"), None),
        P("dp", "ctx", None),
    )
    out_specs = (
        P("dp", "ctx", None),
        P("dp", "ctx", None),
        P(("dp", "ctx"), None),
        P(("dp", "ctx"), None),
        P(("dp", "ctx"), None),
    )
    return jax.shard_map(body, mesh=mesh, in_specs=in_specs, out_specs=out_specs, check_vma=False)
```

```python
import functools

import jax
import jax.numpy as jnp
from jax import lax
from jax.experimental import pallas as pl
from jax.experimental.pallas import tpu as pltpu
from jax.sharding import PartitionSpec as P

ROPE_BASE = 1000000.0
MASKED = -1e30
MESH = pl.DeviceIdType.MESH
BF16 = jnp.bfloat16
F32 = jnp.float32
AXES = ("x", "y", "z")
PIECES = (
    (2, 0, 48, 0, 128, ("z", "y", "x")),
    (2, 0, 48, 128, 128, ("x", "z", "y")),
    (2, 48, 16, 0, 256, ("y", "x", "z")),
    (0, 0, 64, 0, 128, ("z", "y", "x")),
    (0, 0, 64, 128, 128, ("x", "z", "y")),
    (1, 0, 64, 0, 128, ("y", "x", "z")),
    (1, 0, 32, 128, 128, ("y", "z", "x")),
    (1, 32, 32, 128, 128, ("z", "x", "y")),
)
KV_PIECES = (0, 1, 2)
Q_PIECES = (3, 4, 5, 6, 7)
Q_PARTS = ((3, 4), (5, 6, 7))
SCALE = 128 ** (-0.5)
LOG2E = 1.4426950408889634


def place():
    dp, ctx = lax.axis_index("dp"), lax.axis_index("ctx")
    return {
        "x": lax.div(dp, 8) * 2 + lax.div(ctx, 4),
        "y": lax.rem(lax.div(dp, 2), 4),
        "z": lax.rem(ctx, 4),
        "core": lax.rem(dp, 2),
    }


def device(at):
    return (
        lax.div(at["x"], 2) * 8 + at["y"] * 2 + at["core"],
        lax.rem(at["x"], 2) * 4 + at["z"],
    )


def moved(at, axis, by):
    return {**at, axis: lax.rem(at[axis] + 4 + by, 4)}


def sibling(at):
    return {**at, "core": 1 - at["core"]}


def greet(targets):
    barrier = pltpu.get_barrier_semaphore()
    for target in targets:
        pl.semaphore_signal(barrier, inc=1, device_id=target, device_id_type=MESH)
    pl.semaphore_wait(barrier, len(targets))


def partners(at):
    near = [device(moved(at, axis, by)) for axis in AXES for by in (1, -1, 2)]
    return near + [device(sibling(at))] + ctx_peers()


def ctx_peers():
    dp, ctx = lax.axis_index("dp"), lax.axis_index("ctx")
    return [(dp, lax.rem(ctx + k, 8)) for k in range(1, 8)]


def remote(src, dst, send, recv, target):
    return pltpu.make_async_remote_copy(
        src_ref=src, dst_ref=dst, send_sem=send, recv_sem=recv, device_id=target, device_id_type=MESH
    )


class Links:
    def __init__(self, send, recv, twin):
        self.send, self.recv, self.twin = send, recv, twin
        self.slots, self.started = {}, []

    def slot(self, key):
        return self.slots.setdefault(key, len(self.slots))

    def launch(self, key, src, dst, target):
        k = self.slot(key)
        copy = remote(src, dst, self.send.at[k], self.recv.at[k], target)
        copy.start()
        self.started.append(copy)

    def arrival(self, key, ref):
        k = self.slot(key)
        remote(ref, ref, self.send.at[k], self.recv.at[k], self.twin).wait_recv()

    def finish(self):
        for copy in self.started:
            copy.wait_send()


def turn_half(a):
    return pltpu.roll(a, 64, 1)


BYS = (2, 1, -1)


def gather_kernel(
    tokens, wq_hbm, wk_hbm, wv_hbm, tables_hbm,
    w_out, turned_out, q_out, kv_out,
    w, tok, twin_tok, turned, wq, wk, wv, tables, copy_sem, send, recv,
):
    me = place()
    core = me["core"]
    twin = device(sibling(me))
    links = Links(send, recv, twin)
    loads = [
        pltpu.make_async_copy(src, dst, copy_sem.at[k])
        for k, (src, dst) in enumerate(
            ((wq_hbm, wq), (wk_hbm, wk), (wv_hbm, wv), (tables_hbm, tables), (tokens, tok))
        )
    ]
    for copy in loads:
        copy.start()
    for copy in loads[:3]:
        copy.wait()
    x_hi, x_lo = lax.div(me["x"], 2), lax.rem(me["x"], 2)
    w[2, x_hi, me["y"], core, x_lo, me["z"], :, 0:128] = wk[...].astype(BF16)
    w[2, x_hi, me["y"], core, x_lo, me["z"], :, 128:256] = wv[...].astype(BF16)
    w[0, x_hi, me["y"], core, x_lo, me["z"]] = wq[:, 0:256].astype(BF16)
    w[1, x_hi, me["y"], core, x_lo, me["z"]] = wq[:, 256:512].astype(BF16)

    def block(n, first, second, third, core_at=core):
        part, row, rows, col, cols, order = PIECES[n]
        at = dict(zip(order, (first, second, third)))
        x, y, z = (at[axis] for axis in AXES)
        return w.at[
            part,
            slice(None) if x is None else lax.div(x, 2),
            slice(None) if y is None else y,
            core_at,
            slice(None) if x is None else lax.rem(x, 2),
            slice(None) if z is None else z,
            pl.ds(row, rows),
            pl.ds(col, cols),
        ]

    def to(n, phase, by):
        return device(moved(me, PIECES[n][5][phase], by))

    def index(n, phase, by=0):
        axis = PIECES[n][5][phase]
        return moved(me, axis, by)[axis]

    greet(partners(me))
    everything = KV_PIECES + Q_PIECES
    for n in everything:
        mine = block(n, index(n, 0), index(n, 1), index(n, 2))
        for by in BYS:
            links.launch((n, 0, by), mine, mine, to(n, 0, by))
    for k in range(8):
        columns = tokens.at[:, pl.ds(pl.multiple_of(k * 1024 + (1 - core) * 512, 512), 512)]
        links.launch(("tokens", k), columns, twin_tok.at[k], twin)

    def send_chunk(n, c):
        chunk = block(n, None, index(n, 1, c), index(n, 2))
        for by in BYS:
            links.launch((n, 2, c, by), chunk, chunk, to(n, 2, by))

    for n in everything:
        second, third = index(n, 1), index(n, 2)
        for by in BYS:
            links.arrival((n, 0, by), block(n, index(n, 0, -by), second, third))
        line = block(n, None, second, third)
        for by in BYS:
            links.launch((n, 1, by), line, line, to(n, 1, by))
        send_chunk(n, 0)
    for n in everything:
        for by in BYS:
            links.arrival((n, 1, by), block(n, None, index(n, 1, -by), index(n, 2)))
            send_chunk(n, -by)

    CHUNKS = (0,) + tuple(-by for by in BYS)

    def chunk_in(n, c):
        second = index(n, 1, c)
        for by in BYS:
            links.arrival((n, 2, c, by), block(n, None, second, index(n, 2, -by)))
        whole = block(n, None, second, None)
        links.launch((n, "twin", c), whole, whole, twin)

    def twin_in(n, c):
        links.arrival((n, "twin", c), block(n, None, index(n, 1, c), None, 1 - core))

    for copy in loads[3:]:
        copy.wait()
    for k in range(8):
        links.arrival(("tokens", k), twin_tok.at[k])

    def turn(k, _):
        at = pl.multiple_of(k * 1024 + core * 512, 512)
        turned[k, :, 0:256] = tok[:, pl.ds(at, 512)].T
        turned[k, :, 256:512] = twin_tok[k].T
        return 0

    lax.fori_loop(0, 4, turn, 0)
    keep = []

    def store(k, src, dst):
        copy = pltpu.make_async_copy(src, dst, copy_sem.at[k])
        copy.start()
        keep.append(copy)

    for c in CHUNKS:
        for n in KV_PIECES:
            chunk_in(n, c)
    for c in CHUNKS:
        for n in KV_PIECES:
            twin_in(n, c)
    store(5, w.at[2], w_out.at[2])

    def project(part):
        def add(k, total):
            lhs = tok[:, pl.ds(pl.multiple_of(k * 2048, 2048), 2048)]
            rows = w[part, lax.div(k, 2), pl.ds(lax.rem(k, 2) * 2, 2)].reshape(2048, 256)
            return total + jnp.dot(lhs, rows, preferred_element_type=F32)

        return lax.fori_loop(0, 4, add, jnp.zeros((256, 256), F32))

    both = project(2)
    cos, sin = tables[0], tables[1]
    ctx = lax.axis_index("ctx")
    key = both[:, 0:128]
    kv_out[ctx, :, 0:128] = (key * cos + turn_half(key) * sin).astype(BF16)
    kv_out[ctx, :, 128:256] = both[:, 128:256].astype(BF16)
    peers = ctx_peers()
    for k in (4, 2, 6, 1, 3, 5, 7):
        links.launch(("kv", k), kv_out.at[ctx], kv_out.at[ctx], peers[k - 1])

    lax.fori_loop(4, 8, turn, 0)
    store(8, turned, turned_out)
    for n in Q_PIECES[:3]:
        for c in CHUNKS:
            chunk_in(n, c)
    for part in range(2):
        if part == 1:
            for c in CHUNKS:
                for n in Q_PIECES[3:]:
                    chunk_in(n, c)
        for c in CHUNKS:
            for n in Q_PARTS[part]:
                twin_in(n, c)
        store(6 + part, w.at[part], w_out.at[part])
        both = project(part)
        for h in range(2):
            query = both[:, h * 128 : h * 128 + 128]
            rotated = (query * cos + turn_half(query) * sin).astype(BF16)
            q_out[:, part * 256 + h * 128 : part * 256 + h * 128 + 128] = rotated
    for k in range(1, 8):
        links.arrival(("kv", k), kv_out.at[lax.rem(ctx + 8 - k, 8)])
    for copy in keep:
        copy.wait()
    links.finish()


def gather_weights(tokens, wq, wk, wv, tables):
    vmem, anywhere = pl.BlockSpec(memory_space=pltpu.VMEM), pl.BlockSpec(memory_space=pl.ANY)
    shape = jax.ShapeDtypeStruct
    return pl.pallas_call(
        gather_kernel,
        out_shape=(
            shape((3, 2, 4, 2, 2, 4, 64, 256), BF16),
            shape((8, 512, 512), BF16),
            shape((256, 512), BF16),
            shape((8, 256, 256), BF16),
        ),
        in_specs=[anywhere] * 5,
        out_specs=(anywhere, anywhere, vmem, vmem),
        scratch_shapes=[
            pltpu.VMEM((3, 2, 4, 2, 2, 4, 64, 256), BF16),
            pltpu.VMEM((256, 8192), BF16),
            pltpu.VMEM((8, 256, 512), BF16),
            pltpu.VMEM((8, 512, 512), BF16),
            pltpu.VMEM((64, 512), F32),
            pltpu.VMEM((64, 128), F32),
            pltpu.VMEM((64, 128), F32),
            pltpu.VMEM((2, 256, 128), F32),
            pltpu.SemaphoreType.DMA((9,)),
            pltpu.SemaphoreType.DMA((212,)),
            pltpu.SemaphoreType.DMA((212,)),
        ],
        compiler_params=pltpu.CompilerParams(
            collective_id=0, has_side_effects=True, vmem_limit_bytes=60 * 2**20
        ),
        name="gather_weights",
    )(tokens, wq, wk, wv, tables)


def attention_kernel(
    positions, own_positions, q, kv, grad, tables,
    attention, grad_q, terms,
    qs, gs, gs_t, keys_t, values_t, scores, top, total, att_t, gq_t,
):
    for h in range(4):
        rows = slice(h * 256, h * 256 + 256)
        qs[rows] = q[:, h * 128 : h * 128 + 128]
        gs[rows] = grad[:, h * 128 : h * 128 + 128]
        gs_t[:, rows] = grad[:, h * 128 : h * 128 + 128].T
    for k in range(8):
        cols = slice(k * 256, k * 256 + 256)
        keys_t[:, cols] = kv[k, :, 0:128].T
        values_t[:, cols] = kv[k, :, 128:256].T
    nt = (((1,), (1,)), ((), ()))
    lead = own_positions[...] - lax.broadcasted_iota(jnp.int32, (128, 256), 0)
    top[...] = jnp.full(top.shape, MASKED, F32)

    def tile(k, cols):
        return kv[pl.ds(k * 4, 4), :, cols].reshape(1024, 128)

    def score(k, _):
        for h in range(4):
            cols = slice(h * 256, h * 256 + 256)
            s = lax.dot_general(tile(k, slice(0, 128)), qs[cols], nt, preferred_element_type=F32)
            high = None
            for r in range(8):
                rows = slice(r * 128, r * 128 + 128)
                run = jnp.where(lead >= positions[k * 1024 + r * 128], s[rows], MASKED)
                scores[k, rows, cols] = run
                high = run if high is None else jnp.maximum(high, run)
            top[:, cols] = jnp.maximum(top[:, cols], jnp.max(high, axis=0, keepdims=True))
        return 0

    lax.fori_loop(0, 2, score, 0)
    total[...] = jnp.zeros(total.shape, F32)
    att_t[...] = jnp.zeros(att_t.shape, F32)

    def weigh(k, _):
        at = pl.ds(pl.multiple_of(k * 1024, 1024), 1024)
        for h in range(4):
            cols = slice(h * 256, h * 256 + 256)
            weight = jnp.exp2((scores[k, :, cols] - top[:, cols]) * (SCALE * LOG2E))
            scores[k, :, cols] = weight
            total[:, cols] += jnp.sum(weight, axis=0, keepdims=True)
            att_t[:, cols] += jnp.dot(values_t[:, at], weight.astype(BF16), preferred_element_type=F32)
        return 0

    lax.fori_loop(0, 2, weigh, 0)
    for h in range(4):
        cols = slice(h * 256, h * 256 + 256)
        inverse = 1.0 / total[:, cols]
        out = (att_t[:, cols] / total[:, cols]).astype(BF16)
        attention[:, h * 128 : h * 128 + 128] = out.T
        total[:, cols] = inverse
        top[:, cols] = jnp.sum(gs_t[:, cols].astype(F32) * out.astype(F32), axis=0, keepdims=True)
    gq_t[...] = jnp.zeros(gq_t.shape, F32)

    def back(k, _):
        at = pl.ds(pl.multiple_of(k * 1024, 1024), 1024)
        key_term = jnp.zeros((1024, 128), F32)
        value_term = jnp.zeros((1024, 128), F32)
        for h in range(4):
            cols = slice(h * 256, h * 256 + 256)
            probs = scores[k, :, cols] * total[:, cols]
            grad_probs = lax.dot_general(tile(k, slice(128, 256)), gs[cols], nt, preferred_element_type=F32)
            dscore = (probs * (grad_probs - top[:, cols])).astype(BF16)
            key_term += jnp.dot(dscore, qs[cols], preferred_element_type=F32)
            value_term += jnp.dot(probs.astype(BF16), gs[cols], preferred_element_type=F32)
            gq_t[:, cols] += jnp.dot(keys_t[:, at], dscore, preferred_element_type=F32)
        terms[pl.ds(k * 4, 4), :, 0:128] = (key_term * SCALE).astype(BF16).reshape(4, 256, 128)
        terms[pl.ds(k * 4, 4), :, 128:256] = value_term.astype(BF16).reshape(4, 256, 128)
        return 0

    lax.fori_loop(0, 2, back, 0)
    for h in range(4):
        a = gq_t[:, h * 256 : h * 256 + 256].T * SCALE
        unrotated = a * tables[0] - turn_half(a) * tables[1]
        grad_q[:, h * 128 : h * 128 + 128] = unrotated.astype(BF16)


def attend(positions, own_positions, q, kv, grad, tables):
    vmem = pl.BlockSpec(memory_space=pltpu.VMEM)
    shape = jax.ShapeDtypeStruct
    return pl.pallas_call(
        attention_kernel,
        out_shape=(shape((256, 512), BF16), shape((256, 512), BF16), shape((8, 256, 256), BF16)),
        in_specs=[pl.BlockSpec(memory_space=pltpu.SMEM)] + [vmem] * 5,
        out_specs=(vmem, vmem, vmem),
        scratch_shapes=[
            pltpu.VMEM((1024, 128), BF16),
            pltpu.VMEM((1024, 128), BF16),
            pltpu.VMEM((128, 1024), BF16),
            pltpu.VMEM((128, 2048), BF16),
            pltpu.VMEM((128, 2048), BF16),
            pltpu.VMEM((2, 1024, 1024), F32),
            pltpu.VMEM((1, 1024), F32),
            pltpu.VMEM((1, 1024), F32),
            pltpu.VMEM((128, 1024), F32),
            pltpu.VMEM((128, 1024), F32),
        ],
        compiler_params=pltpu.CompilerParams(vmem_limit_bytes=32 * 2**20),
        name="attend",
    )(positions, own_positions, q, kv, grad, tables)


def scatter_kernel(
    turned, w_all, grad_q, terms, tables,
    tokens_out, out,
    held, w, grads, landed, grad_tok, copy_sem, send, recv, *buffers,
):
    me = place()
    core = me["core"]
    ctx = lax.axis_index("ctx")
    twin = device(sibling(me))
    links = Links(send, recv, twin)
    accs = [buffers[6 * n : 6 * n + 3] for n in range(len(PIECES))]
    ends = [buffers[6 * n + 3 : 6 * n + 6] for n in range(len(PIECES))]
    load = pltpu.make_async_copy(turned, held, copy_sem.at[0])
    load.start()
    load_w = pltpu.make_async_copy(w_all, w, copy_sem.at[1])
    load_w.start()
    greet(partners(me))
    links.launch("grad_q", grad_q, grads.at[1, :, pl.ds(0, 512)], twin)
    peers = ctx_peers()
    for k in (4, 2, 6, 1, 3, 5, 7):
        links.launch(("kv", k), terms.at[lax.rem(ctx + k, 8)], landed.at[k - 1], peers[k - 1])
    grads[0, :, 0:512] = grad_q[...]
    load.wait()
    links.arrival("grad_q", grads.at[1, :, pl.ds(0, 512)])

    def axes(n):
        return tuple(reversed(PIECES[n][5]))

    def to(n, phase, by):
        return device(moved(me, axes(n)[phase], by))

    def at(n, phase, by=0):
        axis = axes(n)[phase]
        return moved(me, axis, by)[axis]

    def product(pieces, x, y):
        part = PIECES[pieces[0]][0]
        k = lax.div(x, 2) * 4 + y
        lhs = held[k, pl.ds(pl.multiple_of(lax.rem(x, 2) * 256, 256), 256)]
        rhs = grads[:, :, part * 256 : part * 256 + 256].reshape(512, 256)
        term = jnp.dot(lhs, rhs, preferred_element_type=F32).astype(BF16)
        for n in pieces:
            _, row, rows, col, cols, _ = PIECES[n]
            for z in range(4):
                first, second, third = ({"x": x, "y": y, "z": z}[axis] for axis in axes(n))
                start = z * 64 + row
                accs[n][0][first, second, third] = term[start : start + rows, col : col + cols]

    CHUNKS = (2, 1, -1, 0)

    def products(pieces):
        def one(k, _):
            product(pieces, lax.div(k, 4), lax.rem(k, 4))
            return 0

        lax.fori_loop(0, 16, one, 0)

    def send_direct(n, c):
        j = at(n, 1, c)
        for s, by in enumerate(BYS):
            src = accs[n][0].at[at(n, 0, by), j]
            links.launch((n, 0, c, s), src, ends[n][0].at[s, j], to(n, 0, by))

    def chunk_in(n, c):
        j = at(n, 1, c)
        acc, end = accs[n][0], ends[n][0]
        for s in range(3):
            links.arrival((n, 0, c, s), end.at[s, j])
        total = acc[at(n, 0), j].astype(F32)
        for s in range(3):
            total = total + end[s, j].astype(F32)
        accs[n][1][j] = total.astype(BF16)
        if c != 0:
            s = BYS.index(c)
            links.launch((n, 1, s), accs[n][1].at[j], ends[n][1].at[s], to(n, 1, c))

    def summed(n, phase):
        total = accs[n][phase][at(n, phase)].astype(F32)
        for s in range(3):
            total = total + ends[n][phase][s].astype(F32)
        return total

    def second(n):
        for s in range(3):
            links.arrival((n, 1, s), ends[n][1].at[s])
        accs[n][2][...] = summed(n, 1).astype(BF16)
        for s, by in enumerate(BYS):
            links.launch((n, 2, s), accs[n][2].at[at(n, 2, by)], ends[n][2].at[s], to(n, 2, by))

    def last(n):
        part, row, rows, col, cols, _ = PIECES[n]
        for s in range(3):
            links.arrival((n, 2, s), ends[n][2].at[s])
        out[row : row + rows, part * 256 + col : part * 256 + col + cols] = summed(n, 2)

    for pieces in Q_PARTS:
        products(pieces)
        for c in CHUNKS:
            for n in pieces:
                send_direct(n, c)

    def input_slice(k, _):
        total = None
        for part in range(3):
            lhs = grads[0, :, part * 256 : part * 256 + 256]
            rows = w[part, lax.div(k, 8), lax.rem(lax.div(k, 2), 4), lax.rem(k, 2)].reshape(512, 256)
            term = lax.dot_general(lhs, rows, (((1,), (1,)), ((), ())), preferred_element_type=F32)
            total = term if total is None else total + term
        grad_tok[:, pl.ds(pl.multiple_of(k * 512, 512), 512)] = total.astype(BF16)
        return 0

    stores = []

    def inputs(quarter):
        lax.fori_loop(quarter * 4, quarter * 4 + 4, input_slice, 0)
        cols = pl.ds(quarter * 2048, 2048)
        copy = pltpu.make_async_copy(grad_tok.at[:, cols], tokens_out.at[:, cols], copy_sem.at[2 + quarter])
        copy.start()
        stores.append(copy)

    for k in range(1, 8):
        links.arrival(("kv", k), landed.at[k - 1])
    keyval = terms[ctx].astype(F32)
    for k in range(7):
        keyval = keyval + landed[k].astype(F32)
    key = keyval[:, 0:128]
    grads[0, :, 512:640] = (key * tables[0] - turn_half(key) * tables[1]).astype(BF16)
    grads[0, :, 640:768] = keyval[:, 128:256].astype(BF16)
    columns = pl.ds(512, 256)
    links.launch("grad_kv", grads.at[0, :, columns], grads.at[1, :, columns], twin)
    load_w.wait()
    inputs(0)
    links.arrival("grad_kv", grads.at[1, :, columns])

    products(KV_PIECES)
    for c in CHUNKS:
        for n in KV_PIECES:
            send_direct(n, c)
    for k, c in enumerate(CHUNKS):
        for n in Q_PIECES:
            chunk_in(n, c)
        if k < 3:
            inputs(k + 1)
    for n in Q_PIECES:
        second(n)
    for c in CHUNKS:
        for n in KV_PIECES:
            chunk_in(n, c)
    for n in KV_PIECES:
        second(n)
    for n in Q_PIECES + KV_PIECES:
        last(n)
    for copy in stores:
        copy.wait()
    links.finish()


def scatter_grads(turned, w_all, grad_q, terms, tables):
    vmem, anywhere = pl.BlockSpec(memory_space=pltpu.VMEM), pl.BlockSpec(memory_space=pl.ANY)
    shape = jax.ShapeDtypeStruct
    buffers = []
    for _, _, rows, _, cols, _ in PIECES:
        for lead in ((4, 4, 4), (4, 4), (4,), (3, 4, 4), (3, 4), (3,)):
            buffers.append(pltpu.VMEM(lead + (rows, cols), BF16))
    return pl.pallas_call(
        scatter_kernel,
        out_shape=(shape((256, 8192), BF16), shape((64, 768), F32)),
        in_specs=[anywhere, anywhere, vmem, vmem, vmem],
        out_specs=(anywhere, vmem),
        scratch_shapes=[
            pltpu.VMEM((8, 512, 512), BF16),
            pltpu.VMEM((3, 2, 4, 2, 2, 4, 64, 256), BF16),
            pltpu.VMEM((2, 256, 768), BF16),
            pltpu.VMEM((7, 256, 256), BF16),
            pltpu.VMEM((256, 8192), BF16),
            pltpu.SemaphoreType.DMA((6,)),
            pltpu.SemaphoreType.DMA((216,)),
            pltpu.SemaphoreType.DMA((216,)),
            *buffers,
        ],
        compiler_params=pltpu.CompilerParams(
            collective_id=1, has_side_effects=True, vmem_limit_bytes=48 * 2**20
        ),
        name="scatter_grads",
    )(turned, w_all, grad_q, terms, tables)


def rope_tables(positions_in, head_dim):
    half_width = head_dim // 2
    exponent = jnp.arange(half_width).astype(F32) * (2.0 / head_dim)
    frequency = jnp.power(ROPE_BASE, -exponent)
    angles = positions_in.astype(F32)[:, None] * frequency[None, :]
    cos, sin = jnp.cos(angles), jnp.sin(angles)
    return jnp.stack([jnp.concatenate([cos, cos], axis=1), jnp.concatenate([-sin, sin], axis=1)])


def body(tokens, positions, query_weight, key_weight, value_weight, grad_output):
    own_positions = lax.dynamic_slice_in_dim(positions, lax.axis_index("ctx") * 256, 256)
    tables = rope_tables(own_positions, 128)
    w_all, turned, q, kv = gather_weights(
        tokens[0], query_weight, key_weight, value_weight, tables
    )
    attention, grad_q, terms = attend(
        positions, own_positions[None], q, kv, grad_output[0], tables
    )
    grad_tokens, grads = scatter_grads(turned, w_all, grad_q, terms, tables)
    return attention[None], grad_tokens[None], grads[:, :512], grads[:, 512:640], grads[:, 640:]


def solution(mesh):
    in_specs = (
        P("dp", "ctx", None),
        P(),
        P(("dp", "ctx"), None),
        P(("dp", "ctx"), None),
        P(("dp", "ctx"), None),
        P("dp", "ctx", None),
    )
    out_specs = (
        P("dp", "ctx", None),
        P("dp", "ctx", None),
        P(("dp", "ctx"), None),
        P(("dp", "ctx"), None),
        P(("dp", "ctx"), None),
    )
    return jax.shard_map(body, mesh=mesh, in_specs=in_specs, out_specs=out_specs, check_vma=False)
```

```python
import functools

import jax
import jax.numpy as jnp
from jax import lax
from jax.experimental import pallas as pl
from jax.experimental.pallas import tpu as pltpu
from jax.sharding import PartitionSpec as P

ROPE_BASE = 1000000.0
MASKED = -1e30
MESH = pl.DeviceIdType.MESH
BF16 = jnp.bfloat16
F32 = jnp.float32
AXES = ("x", "y", "z")
PIECES = (
    (2, 0, 48, 0, 128, ("z", "y", "x")),
    (2, 0, 48, 128, 128, ("x", "z", "y")),
    (2, 48, 16, 0, 256, ("y", "x", "z")),
    (0, 0, 64, 0, 128, ("z", "y", "x")),
    (0, 0, 64, 128, 128, ("x", "z", "y")),
    (1, 0, 64, 0, 128, ("y", "x", "z")),
    (1, 0, 32, 128, 128, ("y", "z", "x")),
    (1, 32, 32, 128, 128, ("z", "x", "y")),
)
KV_PIECES = (0, 1, 2)
Q_PIECES = (3, 4, 5, 6, 7)
Q_PARTS = ((3, 4), (5, 6, 7))
SCALE = 128 ** (-0.5)
LOG2E = 1.4426950408889634


def place():
    dp, ctx = lax.axis_index("dp"), lax.axis_index("ctx")
    return {
        "x": lax.div(dp, 8) * 2 + lax.div(ctx, 4),
        "y": lax.rem(lax.div(dp, 2), 4),
        "z": lax.rem(ctx, 4),
        "core": lax.rem(dp, 2),
    }


def device(at):
    return (
        lax.div(at["x"], 2) * 8 + at["y"] * 2 + at["core"],
        lax.rem(at["x"], 2) * 4 + at["z"],
    )


def moved(at, axis, by):
    return {**at, axis: lax.rem(at[axis] + 4 + by, 4)}


def sibling(at):
    return {**at, "core": 1 - at["core"]}


def greet(targets):
    barrier = pltpu.get_barrier_semaphore()
    for target in targets:
        pl.semaphore_signal(barrier, inc=1, device_id=target, device_id_type=MESH)
    pl.semaphore_wait(barrier, len(targets))


def partners(at):
    near = [device(moved(at, axis, by)) for axis in AXES for by in (1, -1, 2)]
    return near + [device(sibling(at))] + ctx_peers()


def ctx_peers():
    dp, ctx = lax.axis_index("dp"), lax.axis_index("ctx")
    return [(dp, lax.rem(ctx + k, 8)) for k in range(1, 8)]


def remote(src, dst, send, recv, target):
    return pltpu.make_async_remote_copy(
        src_ref=src, dst_ref=dst, send_sem=send, recv_sem=recv, device_id=target, device_id_type=MESH
    )


class Links:
    def __init__(self, send, recv, twin):
        self.send, self.recv, self.twin = send, recv, twin
        self.slots, self.started = {}, []

    def slot(self, key):
        return self.slots.setdefault(key, len(self.slots))

    def launch(self, key, src, dst, target):
        k = self.slot(key)
        copy = remote(src, dst, self.send.at[k], self.recv.at[k], target)
        copy.start()
        self.started.append(copy)

    def arrival(self, key, ref):
        k = self.slot(key)
        remote(ref, ref, self.send.at[k], self.recv.at[k], self.twin).wait_recv()

    def finish(self):
        for copy in self.started:
            copy.wait_send()


def turn_half(a):
    return pltpu.roll(a, 64, 1)


BYS = (2, 1, -1)


def gather_kernel(
    tokens, wq_hbm, wk_hbm, wv_hbm, tables_hbm,
    w_out, turned_out, q_out, kv_out,
    w, tok, twin_tok, turned, wq, wk, wv, tables, copy_sem, send, recv,
):
    me = place()
    core = me["core"]
    twin = device(sibling(me))
    links = Links(send, recv, twin)
    loads = [
        pltpu.make_async_copy(src, dst, copy_sem.at[k])
        for k, (src, dst) in enumerate(
            ((wq_hbm, wq), (wk_hbm, wk), (wv_hbm, wv), (tables_hbm, tables), (tokens, tok))
        )
    ]
    for copy in loads:
        copy.start()
    for copy in loads[:3]:
        copy.wait()
    x_hi, x_lo = lax.div(me["x"], 2), lax.rem(me["x"], 2)
    w[2, x_hi, me["y"], core, x_lo, me["z"], :, 0:128] = wk[...].astype(BF16)
    w[2, x_hi, me["y"], core, x_lo, me["z"], :, 128:256] = wv[...].astype(BF16)
    w[0, x_hi, me["y"], core, x_lo, me["z"]] = wq[:, 0:256].astype(BF16)
    w[1, x_hi, me["y"], core, x_lo, me["z"]] = wq[:, 256:512].astype(BF16)

    def block(n, first, second, third, core_at=core):
        part, row, rows, col, cols, order = PIECES[n]
        at = dict(zip(order, (first, second, third)))
        x, y, z = (at[axis] for axis in AXES)
        return w.at[
            part,
            slice(None) if x is None else lax.div(x, 2),
            slice(None) if y is None else y,
            core_at,
            slice(None) if x is None else lax.rem(x, 2),
            slice(None) if z is None else z,
            pl.ds(row, rows),
            pl.ds(col, cols),
        ]

    def to(n, phase, by):
        return device(moved(me, PIECES[n][5][phase], by))

    def index(n, phase, by=0):
        axis = PIECES[n][5][phase]
        return moved(me, axis, by)[axis]

    greet(partners(me))
    everything = KV_PIECES + Q_PIECES
    for n in everything:
        mine = block(n, index(n, 0), index(n, 1), index(n, 2))
        for by in BYS:
            links.launch((n, 0, by), mine, mine, to(n, 0, by))
    for k in range(8):
        columns = tokens.at[:, pl.ds(pl.multiple_of(k * 1024 + (1 - core) * 512, 512), 512)]
        links.launch(("tokens", k), columns, twin_tok.at[k], twin)

    def send_chunk(n, c):
        chunk = block(n, None, index(n, 1, c), index(n, 2))
        for by in BYS:
            links.launch((n, 2, c, by), chunk, chunk, to(n, 2, by))

    for n in everything:
        second, third = index(n, 1), index(n, 2)
        for by in BYS:
            links.arrival((n, 0, by), block(n, index(n, 0, -by), second, third))
        line = block(n, None, second, third)
        for by in BYS:
            links.launch((n, 1, by), line, line, to(n, 1, by))
        send_chunk(n, 0)
    for n in everything:
        for by in BYS:
            links.arrival((n, 1, by), block(n, None, index(n, 1, -by), index(n, 2)))
            send_chunk(n, -by)

    CHUNKS = (0,) + tuple(-by for by in BYS)

    def chunk_in(n, c):
        second = index(n, 1, c)
        for by in BYS:
            links.arrival((n, 2, c, by), block(n, None, second, index(n, 2, -by)))
        whole = block(n, None, second, None)
        links.launch((n, "twin", c), whole, whole, twin)

    def twin_in(n, c):
        links.arrival((n, "twin", c), block(n, None, index(n, 1, c), None, 1 - core))

    for copy in loads[3:]:
        copy.wait()
    for k in range(8):
        links.arrival(("tokens", k), twin_tok.at[k])

    def turn(k, _):
        at = pl.multiple_of(k * 1024 + core * 512, 512)
        turned[k, :, 0:256] = tok[:, pl.ds(at, 512)].T
        turned[k, :, 256:512] = twin_tok[k].T
        return 0

    lax.fori_loop(0, 4, turn, 0)
    keep = []

    def store(k, src, dst):
        copy = pltpu.make_async_copy(src, dst, copy_sem.at[k])
        copy.start()
        keep.append(copy)

    for c in CHUNKS:
        for n in KV_PIECES:
            chunk_in(n, c)
    for c in CHUNKS:
        for n in KV_PIECES:
            twin_in(n, c)
    store(5, w.at[2], w_out.at[2])

    def project(part):
        def add(k, total):
            lhs = tok[:, pl.ds(pl.multiple_of(k * 2048, 2048), 2048)]
            rows = w[part, lax.div(k, 2), pl.ds(lax.rem(k, 2) * 2, 2)].reshape(2048, 256)
            return total + jnp.dot(lhs, rows, preferred_element_type=F32)

        return lax.fori_loop(0, 4, add, jnp.zeros((256, 256), F32))

    both = project(2)
    cos, sin = tables[0], tables[1]
    ctx = lax.axis_index("ctx")
    key = both[:, 0:128]
    kv_out[ctx, :, 0:128] = (key * cos + turn_half(key) * sin).astype(BF16)
    kv_out[ctx, :, 128:256] = both[:, 128:256].astype(BF16)
    peers = ctx_peers()
    for k in (4, 2, 6, 1, 3, 5, 7):
        links.launch(("kv", k), kv_out.at[ctx], kv_out.at[ctx], peers[k - 1])

    lax.fori_loop(4, 8, turn, 0)
    store(8, turned, turned_out)
    for n in Q_PIECES[:3]:
        for c in CHUNKS:
            chunk_in(n, c)
    for part in range(2):
        if part == 1:
            for c in CHUNKS:
                for n in Q_PIECES[3:]:
                    chunk_in(n, c)
        for c in CHUNKS:
            for n in Q_PARTS[part]:
                twin_in(n, c)
        store(6 + part, w.at[part], w_out.at[part])
        both = project(part)
        for h in range(2):
            query = both[:, h * 128 : h * 128 + 128]
            rotated = (query * cos + turn_half(query) * sin).astype(BF16)
            q_out[:, part * 256 + h * 128 : part * 256 + h * 128 + 128] = rotated
    for k in range(1, 8):
        links.arrival(("kv", k), kv_out.at[lax.rem(ctx + 8 - k, 8)])
    for copy in keep:
        copy.wait()
    links.finish()


def gather_weights(tokens, wq, wk, wv, tables):
    vmem, anywhere = pl.BlockSpec(memory_space=pltpu.VMEM), pl.BlockSpec(memory_space=pl.ANY)
    shape = jax.ShapeDtypeStruct
    return pl.pallas_call(
        gather_kernel,
        out_shape=(
            shape((3, 2, 4, 2, 2, 4, 64, 256), BF16),
            shape((8, 512, 512), BF16),
            shape((256, 512), BF16),
            shape((8, 256, 256), BF16),
        ),
        in_specs=[anywhere] * 5,
        out_specs=(anywhere, anywhere, vmem, vmem),
        scratch_shapes=[
            pltpu.VMEM((3, 2, 4, 2, 2, 4, 64, 256), BF16),
            pltpu.VMEM((256, 8192), BF16),
            pltpu.VMEM((8, 256, 512), BF16),
            pltpu.VMEM((8, 512, 512), BF16),
            pltpu.VMEM((64, 512), F32),
            pltpu.VMEM((64, 128), F32),
            pltpu.VMEM((64, 128), F32),
            pltpu.VMEM((2, 256, 128), F32),
            pltpu.SemaphoreType.DMA((9,)),
            pltpu.SemaphoreType.DMA((212,)),
            pltpu.SemaphoreType.DMA((212,)),
        ],
        compiler_params=pltpu.CompilerParams(
            collective_id=0, has_side_effects=True, vmem_limit_bytes=60 * 2**20
        ),
        name="gather_weights",
    )(tokens, wq, wk, wv, tables)


def attention_kernel(
    positions, own_positions, q, kv, grad, tables,
    attention, grad_q, terms,
    qs, gs, gs_t, keys_t, values_t, scores, top, total, att_t, gq_t,
):
    for h in range(4):
        rows = slice(h * 256, h * 256 + 256)
        qs[rows] = q[:, h * 128 : h * 128 + 128]
        gs[rows] = grad[:, h * 128 : h * 128 + 128]
        gs_t[:, rows] = grad[:, h * 128 : h * 128 + 128].T
    for k in range(8):
        cols = slice(k * 256, k * 256 + 256)
        keys_t[:, cols] = kv[k, :, 0:128].T
        values_t[:, cols] = kv[k, :, 128:256].T
    nt = (((1,), (1,)), ((), ()))
    lead = own_positions[...] - lax.broadcasted_iota(jnp.int32, (128, 256), 0)
    top[...] = jnp.full(top.shape, MASKED, F32)

    def tile(k, cols):
        return kv[pl.ds(k * 4, 4), :, cols].reshape(1024, 128)

    def score(k, _):
        for h in range(4):
            cols = slice(h * 256, h * 256 + 256)
            s = lax.dot_general(tile(k, slice(0, 128)), qs[cols], nt, preferred_element_type=F32)
            high = None
            for r in range(8):
                rows = slice(r * 128, r * 128 + 128)
                run = jnp.where(lead >= positions[k * 1024 + r * 128], s[rows], MASKED)
                scores[k, rows, cols] = run
                high = run if high is None else jnp.maximum(high, run)
            top[:, cols] = jnp.maximum(top[:, cols], jnp.max(high, axis=0, keepdims=True))
        return 0

    lax.fori_loop(0, 2, score, 0)
    total[...] = jnp.zeros(total.shape, F32)
    att_t[...] = jnp.zeros(att_t.shape, F32)

    def weigh(k, _):
        at = pl.ds(pl.multiple_of(k * 1024, 1024), 1024)
        for h in range(4):
            cols = slice(h * 256, h * 256 + 256)
            weight = jnp.exp2((scores[k, :, cols] - top[:, cols]) * (SCALE * LOG2E))
            scores[k, :, cols] = weight
            total[:, cols] += jnp.sum(weight, axis=0, keepdims=True)
            att_t[:, cols] += jnp.dot(values_t[:, at], weight.astype(BF16), preferred_element_type=F32)
        return 0

    lax.fori_loop(0, 2, weigh, 0)
    for h in range(4):
        cols = slice(h * 256, h * 256 + 256)
        inverse = 1.0 / total[:, cols]
        out = (att_t[:, cols] / total[:, cols]).astype(BF16)
        attention[:, h * 128 : h * 128 + 128] = out.T
        total[:, cols] = inverse
        top[:, cols] = jnp.sum(gs_t[:, cols].astype(F32) * out.astype(F32), axis=0, keepdims=True)
    gq_t[...] = jnp.zeros(gq_t.shape, F32)

    def back(k, _):
        at = pl.ds(pl.multiple_of(k * 1024, 1024), 1024)
        key_term = jnp.zeros((1024, 128), F32)
        value_term = jnp.zeros((1024, 128), F32)
        for h in range(4):
            cols = slice(h * 256, h * 256 + 256)
            probs = scores[k, :, cols] * total[:, cols]
            grad_probs = lax.dot_general(tile(k, slice(128, 256)), gs[cols], nt, preferred_element_type=F32)
            dscore = (probs * (grad_probs - top[:, cols])).astype(BF16)
            key_term += jnp.dot(dscore, qs[cols], preferred_element_type=F32)
            value_term += jnp.dot(probs.astype(BF16), gs[cols], preferred_element_type=F32)
            gq_t[:, cols] += jnp.dot(keys_t[:, at], dscore, preferred_element_type=F32)
        terms[pl.ds(k * 4, 4), :, 0:128] = (key_term * SCALE).astype(BF16).reshape(4, 256, 128)
        terms[pl.ds(k * 4, 4), :, 128:256] = value_term.astype(BF16).reshape(4, 256, 128)
        return 0

    lax.fori_loop(0, 2, back, 0)
    for h in range(4):
        a = gq_t[:, h * 256 : h * 256 + 256].T * SCALE
        unrotated = a * tables[0] - turn_half(a) * tables[1]
        grad_q[:, h * 128 : h * 128 + 128] = unrotated.astype(BF16)


def attend(positions, own_positions, q, kv, grad, tables):
    vmem = pl.BlockSpec(memory_space=pltpu.VMEM)
    shape = jax.ShapeDtypeStruct
    return pl.pallas_call(
        attention_kernel,
        out_shape=(shape((256, 512), BF16), shape((256, 512), BF16), shape((8, 256, 256), BF16)),
        in_specs=[pl.BlockSpec(memory_space=pltpu.SMEM)] + [vmem] * 5,
        out_specs=(vmem, vmem, vmem),
        scratch_shapes=[
            pltpu.VMEM((1024, 128), BF16),
            pltpu.VMEM((1024, 128), BF16),
            pltpu.VMEM((128, 1024), BF16),
            pltpu.VMEM((128, 2048), BF16),
            pltpu.VMEM((128, 2048), BF16),
            pltpu.VMEM((2, 1024, 1024), F32),
            pltpu.VMEM((1, 1024), F32),
            pltpu.VMEM((1, 1024), F32),
            pltpu.VMEM((128, 1024), F32),
            pltpu.VMEM((128, 1024), F32),
        ],
        compiler_params=pltpu.CompilerParams(vmem_limit_bytes=32 * 2**20),
        name="attend",
    )(positions, own_positions, q, kv, grad, tables)


def scatter_kernel(
    turned, w_all, grad_q, terms, tables,
    tokens_out, out,
    held, w, grads, landed, grad_tok, copy_sem, send, recv, *buffers,
):
    me = place()
    core = me["core"]
    ctx = lax.axis_index("ctx")
    twin = device(sibling(me))
    links = Links(send, recv, twin)
    accs = [buffers[7 * n : 7 * n + 3] for n in range(len(PIECES))]
    ends = [buffers[7 * n + 3 : 7 * n + 6] for n in range(len(PIECES))]
    vias = [buffers[7 * n + 6] for n in range(len(PIECES))]
    load = pltpu.make_async_copy(turned, held, copy_sem.at[0])
    load.start()
    load_w = pltpu.make_async_copy(w_all, w, copy_sem.at[1])
    load_w.start()
    greet(partners(me))
    links.launch("grad_q", grad_q, grads.at[1, :, pl.ds(0, 512)], twin)
    peers = ctx_peers()
    for k in (4, 2, 6, 1, 3, 5, 7):
        links.launch(("kv", k), terms.at[lax.rem(ctx + k, 8)], landed.at[k - 1], peers[k - 1])
    grads[0, :, 0:512] = grad_q[...]
    load.wait()
    links.arrival("grad_q", grads.at[1, :, pl.ds(0, 512)])

    def axes(n):
        return tuple(reversed(PIECES[n][5]))

    def to(n, phase, by):
        return device(moved(me, axes(n)[phase], by))

    def at(n, phase, by=0):
        axis = axes(n)[phase]
        return moved(me, axis, by)[axis]

    def product(pieces, x, y):
        part = PIECES[pieces[0]][0]
        k = lax.div(x, 2) * 4 + y
        lhs = held[k, pl.ds(pl.multiple_of(lax.rem(x, 2) * 256, 256), 256)]
        rhs = grads[:, :, part * 256 : part * 256 + 256].reshape(512, 256)
        term = jnp.dot(lhs, rhs, preferred_element_type=F32).astype(BF16)
        for n in pieces:
            _, row, rows, col, cols, _ = PIECES[n]
            for z in range(4):
                first, second, third = ({"x": x, "y": y, "z": z}[axis] for axis in axes(n))
                start = z * 64 + row
                if n in KV_PIECES:
                    accs[n][0][first, second, third] = term[start : start + rows, col : col + cols]
                    continue
                for half in range(2):
                    start = z * 64 + row + half * (rows // 2)
                    accs[n][0][first, half, second, third] = term[
                        start : start + rows // 2, col : col + cols
                    ]

    CHUNKS = (2, 1, -1, 0)

    def products(pieces):
        def one(k, _):
            product(pieces, lax.div(k, 4), lax.rem(k, 4))
            return 0

        lax.fori_loop(0, 16, one, 0)

    def send_direct(n, c):
        j = at(n, 1, c)
        for s, by in enumerate(BYS):
            src = accs[n][0].at[at(n, 0, by), j]
            links.launch((n, 0, c, s), src, ends[n][0].at[s, j], to(n, 0, by))

    def send_far(n, c):
        j = at(n, 1, c)
        for d, by in enumerate((1, -1)):
            src = accs[n][0].at[at(n, 0, 2), d, j]
            links.launch((n, "via", c, d), src, vias[n].at[d, j], to(n, 0, by))

    def send_near(n, c):
        j = at(n, 1, c)
        for d, by in enumerate((1, -1)):
            src = accs[n][0].at[at(n, 0, by), 1 - d, j]
            links.launch((n, "end", c, d, 1 - d), src, ends[n][0].at[d, 1 - d, j], to(n, 0, by))

    def relay(n, c):
        j = at(n, 1, c)
        acc, via, end = accs[n][0], vias[n], ends[n][0]
        for d, by in enumerate((1, -1)):
            links.arrival((n, "via", c, d), via.at[d, j])
            i = at(n, 0, by)
            acc[i, d, j] = (acc[i, d, j].astype(F32) + via[d, j].astype(F32)).astype(BF16)
            links.launch((n, "end", c, d, d), acc.at[i, d, j], end.at[d, d, j], to(n, 0, by))

    def chunk_in(n, c):
        j = at(n, 1, c)
        acc, end = accs[n][0], ends[n][0]
        rows = PIECES[n][2] // 2
        if n in KV_PIECES:
            for s in range(3):
                links.arrival((n, 0, c, s), end.at[s, j])
            total = acc[at(n, 0), j].astype(F32)
            for s in range(3):
                total = total + end[s, j].astype(F32)
            accs[n][1][j] = total.astype(BF16)
        for h in range(2) if n in Q_PIECES else ():
            for d in range(2):
                links.arrival((n, "end", c, d, h), end.at[d, h, j])
            total = acc[at(n, 0), h, j].astype(F32)
            total = total + end[0, h, j].astype(F32) + end[1, h, j].astype(F32)
            accs[n][1][j, :, h * rows : h * rows + rows] = total.astype(BF16)
        if c != 0:
            s = BYS.index(c)
            links.launch((n, 1, s), accs[n][1].at[j], ends[n][1].at[s], to(n, 1, c))

    def summed(n, phase):
        total = accs[n][phase][at(n, phase)].astype(F32)
        for s in range(3):
            total = total + ends[n][phase][s].astype(F32)
        return total

    def second(n):
        for s in range(3):
            links.arrival((n, 1, s), ends[n][1].at[s])
        accs[n][2][...] = summed(n, 1).astype(BF16)
        for s, by in enumerate(BYS):
            links.launch((n, 2, s), accs[n][2].at[at(n, 2, by)], ends[n][2].at[s], to(n, 2, by))

    def last(n):
        part, row, rows, col, cols, _ = PIECES[n]
        for s in range(3):
            links.arrival((n, 2, s), ends[n][2].at[s])
        out[row : row + rows, part * 256 + col : part * 256 + col + cols] = summed(n, 2)

    for pieces in Q_PARTS:
        products(pieces)
        for c in CHUNKS:
            for n in pieces:
                send_far(n, c)
    for c in CHUNKS:
        for n in Q_PIECES:
            send_near(n, c)
    for c in CHUNKS:
        for n in Q_PIECES:
            if axes(n)[0] != "z":
                relay(n, c)

    def input_slice(k, _):
        total = None
        for part in range(3):
            lhs = grads[0, :, part * 256 : part * 256 + 256]
            rows = w[part, lax.div(k, 8), lax.rem(lax.div(k, 2), 4), lax.rem(k, 2)].reshape(512, 256)
            term = lax.dot_general(lhs, rows, (((1,), (1,)), ((), ())), preferred_element_type=F32)
            total = term if total is None else total + term
        grad_tok[:, pl.ds(pl.multiple_of(k * 512, 512), 512)] = total.astype(BF16)
        return 0

    stores = []

    def inputs(quarter):
        lax.fori_loop(quarter * 4, quarter * 4 + 4, input_slice, 0)
        cols = pl.ds(quarter * 2048, 2048)
        copy = pltpu.make_async_copy(grad_tok.at[:, cols], tokens_out.at[:, cols], copy_sem.at[2 + quarter])
        copy.start()
        stores.append(copy)

    for k in range(1, 8):
        links.arrival(("kv", k), landed.at[k - 1])
    keyval = terms[ctx].astype(F32)
    for k in range(7):
        keyval = keyval + landed[k].astype(F32)
    key = keyval[:, 0:128]
    grads[0, :, 512:640] = (key * tables[0] - turn_half(key) * tables[1]).astype(BF16)
    grads[0, :, 640:768] = keyval[:, 128:256].astype(BF16)
    columns = pl.ds(512, 256)
    links.launch("grad_kv", grads.at[0, :, columns], grads.at[1, :, columns], twin)
    for c in CHUNKS:
        for n in Q_PIECES:
            if axes(n)[0] == "z":
                relay(n, c)
    load_w.wait()
    inputs(0)
    links.arrival("grad_kv", grads.at[1, :, columns])

    products(KV_PIECES)
    for c in CHUNKS:
        for n in KV_PIECES:
            send_direct(n, c)
    for k, c in enumerate(CHUNKS):
        for n in Q_PIECES:
            chunk_in(n, c)
        if k < 3:
            inputs(k + 1)
    for n in Q_PIECES:
        second(n)
    for c in CHUNKS:
        for n in KV_PIECES:
            chunk_in(n, c)
    for n in KV_PIECES:
        second(n)
    for n in Q_PIECES + KV_PIECES:
        last(n)
    for copy in stores:
        copy.wait()
    links.finish()


def scatter_grads(turned, w_all, grad_q, terms, tables):
    vmem, anywhere = pl.BlockSpec(memory_space=pltpu.VMEM), pl.BlockSpec(memory_space=pl.ANY)
    shape = jax.ShapeDtypeStruct
    buffers = []
    for n, (_, _, rows, _, cols, _) in enumerate(PIECES):
        half, whole = (rows // 2, cols), (rows, cols)
        later = ((4, 4) + whole, (4,) + whole), ((3, 4) + whole, (3,) + whole)
        if n in KV_PIECES:
            first = (4, 4, 4) + whole, (3, 4, 4) + whole, (8, 128)
        else:
            first = (4, 2, 4, 4) + half, (2, 2, 4, 4) + half, (2, 4, 4) + half
        for shape_of in (first[0], *later[0], first[1], *later[1], first[2]):
            buffers.append(pltpu.VMEM(shape_of, BF16))
    return pl.pallas_call(
        scatter_kernel,
        out_shape=(shape((256, 8192), BF16), shape((64, 768), F32)),
        in_specs=[anywhere, anywhere, vmem, vmem, vmem],
        out_specs=(anywhere, vmem),
        scratch_shapes=[
            pltpu.VMEM((8, 512, 512), BF16),
            pltpu.VMEM((3, 2, 4, 2, 2, 4, 64, 256), BF16),
            pltpu.VMEM((2, 256, 768), BF16),
            pltpu.VMEM((7, 256, 256), BF16),
            pltpu.VMEM((256, 8192), BF16),
            pltpu.SemaphoreType.DMA((6,)),
            pltpu.SemaphoreType.DMA((216,)),
            pltpu.SemaphoreType.DMA((216,)),
            *buffers,
        ],
        compiler_params=pltpu.CompilerParams(
            collective_id=1, has_side_effects=True, vmem_limit_bytes=48 * 2**20
        ),
        name="scatter_grads",
    )(turned, w_all, grad_q, terms, tables)


def rope_tables(positions_in, head_dim):
    half_width = head_dim // 2
    exponent = jnp.arange(half_width).astype(F32) * (2.0 / head_dim)
    frequency = jnp.power(ROPE_BASE, -exponent)
    angles = positions_in.astype(F32)[:, None] * frequency[None, :]
    cos, sin = jnp.cos(angles), jnp.sin(angles)
    return jnp.stack([jnp.concatenate([cos, cos], axis=1), jnp.concatenate([-sin, sin], axis=1)])


def body(tokens, positions, query_weight, key_weight, value_weight, grad_output):
    own_positions = lax.dynamic_slice_in_dim(positions, lax.axis_index("ctx") * 256, 256)
    tables = rope_tables(own_positions, 128)
    w_all, turned, q, kv = gather_weights(
        tokens[0], query_weight, key_weight, value_weight, tables
    )
    attention, grad_q, terms = attend(
        positions, own_positions[None], q, kv, grad_output[0], tables
    )
    grad_tokens, grads = scatter_grads(turned, w_all, grad_q, terms, tables)
    return attention[None], grad_tokens[None], grads[:, :512], grads[:, 512:640], grads[:, 640:]


def solution(mesh):
    in_specs = (
        P("dp", "ctx", None),
        P(),
        P(("dp", "ctx"), None),
        P(("dp", "ctx"), None),
        P(("dp", "ctx"), None),
        P("dp", "ctx", None),
    )
    out_specs = (
        P("dp", "ctx", None),
        P("dp", "ctx", None),
        P(("dp", "ctx"), None),
        P(("dp", "ctx"), None),
        P(("dp", "ctx"), None),
    )
    return jax.shard_map(body, mesh=mesh, in_specs=in_specs, out_specs=out_specs, check_vma=False)
```

```python
import functools

import jax
import jax.numpy as jnp
from jax import lax
from jax.experimental import pallas as pl
from jax.experimental.pallas import tpu as pltpu
from jax.sharding import PartitionSpec as P

ROPE_BASE = 1000000.0
MASKED = -1e30
MESH = pl.DeviceIdType.MESH
BF16 = jnp.bfloat16
F32 = jnp.float32
AXES = ("x", "y", "z")
PIECES = (
    (2, 0, 48, 0, 128, ("z", "y", "x")),
    (2, 0, 48, 128, 128, ("x", "z", "y")),
    (2, 48, 16, 0, 256, ("y", "x", "z")),
    (0, 0, 64, 0, 128, ("z", "y", "x")),
    (0, 0, 64, 128, 128, ("x", "z", "y")),
    (1, 0, 64, 0, 128, ("y", "x", "z")),
    (1, 0, 32, 128, 128, ("y", "z", "x")),
    (1, 32, 32, 128, 128, ("z", "x", "y")),
)
KV_PIECES = (0, 1, 2)
Q_PIECES = (3, 4, 5, 6, 7)
Q_PARTS = ((3, 4), (5, 6, 7))
SCALE = 128 ** (-0.5)
LOG2E = 1.4426950408889634


def place():
    dp, ctx = lax.axis_index("dp"), lax.axis_index("ctx")
    return {
        "x": lax.div(dp, 8) * 2 + lax.div(ctx, 4),
        "y": lax.rem(lax.div(dp, 2), 4),
        "z": lax.rem(ctx, 4),
        "core": lax.rem(dp, 2),
    }


def device(at):
    return (
        lax.div(at["x"], 2) * 8 + at["y"] * 2 + at["core"],
        lax.rem(at["x"], 2) * 4 + at["z"],
    )


def moved(at, axis, by):
    return {**at, axis: lax.rem(at[axis] + 4 + by, 4)}


def sibling(at):
    return {**at, "core": 1 - at["core"]}


def greet(targets):
    barrier = pltpu.get_barrier_semaphore()
    for target in targets:
        pl.semaphore_signal(barrier, inc=1, device_id=target, device_id_type=MESH)
    pl.semaphore_wait(barrier, len(targets))


def partners(at):
    near = [device(moved(at, axis, by)) for axis in AXES for by in (1, -1, 2)]
    return near + [device(sibling(at))] + ctx_peers()


def ctx_peers():
    dp, ctx = lax.axis_index("dp"), lax.axis_index("ctx")
    return [(dp, lax.rem(ctx + k, 8)) for k in range(1, 8)]


def remote(src, dst, send, recv, target):
    return pltpu.make_async_remote_copy(
        src_ref=src, dst_ref=dst, send_sem=send, recv_sem=recv, device_id=target, device_id_type=MESH
    )


class Links:
    def __init__(self, send, recv, twin):
        self.send, self.recv, self.twin = send, recv, twin
        self.slots, self.started = {}, []

    def slot(self, key):
        return self.slots.setdefault(key, len(self.slots))

    def launch(self, key, src, dst, target):
        k = self.slot(key)
        copy = remote(src, dst, self.send.at[k], self.recv.at[k], target)
        copy.start()
        self.started.append(copy)

    def arrival(self, key, ref):
        k = self.slot(key)
        remote(ref, ref, self.send.at[k], self.recv.at[k], self.twin).wait_recv()

    def finish(self):
        for copy in self.started:
            copy.wait_send()


def turn_half(a):
    return pltpu.roll(a, 64, 1)


BYS = (2, 1, -1)


def gather_kernel(
    tokens, wq_hbm, wk_hbm, wv_hbm, tables_hbm,
    w_out, turned_out, q_out, kv_out,
    w, tok, twin_tok, turned, wq, wk, wv, tables, copy_sem, send, recv,
):
    me = place()
    core = me["core"]
    twin = device(sibling(me))
    links = Links(send, recv, twin)
    loads = [
        pltpu.make_async_copy(src, dst, copy_sem.at[k])
        for k, (src, dst) in enumerate(
            ((wq_hbm, wq), (wk_hbm, wk), (wv_hbm, wv), (tables_hbm, tables), (tokens, tok))
        )
    ]
    for copy in loads:
        copy.start()
    for copy in loads[:3]:
        copy.wait()
    x_hi, x_lo = lax.div(me["x"], 2), lax.rem(me["x"], 2)
    w[2, x_hi, me["y"], core, x_lo, me["z"], :, 0:128] = wk[...].astype(BF16)
    w[2, x_hi, me["y"], core, x_lo, me["z"], :, 128:256] = wv[...].astype(BF16)
    w[0, x_hi, me["y"], core, x_lo, me["z"]] = wq[:, 0:256].astype(BF16)
    w[1, x_hi, me["y"], core, x_lo, me["z"]] = wq[:, 256:512].astype(BF16)

    def block(n, first, second, third, core_at=core):
        part, row, rows, col, cols, order = PIECES[n]
        at = dict(zip(order, (first, second, third)))
        x, y, z = (at[axis] for axis in AXES)
        return w.at[
            part,
            slice(None) if x is None else lax.div(x, 2),
            slice(None) if y is None else y,
            core_at,
            slice(None) if x is None else lax.rem(x, 2),
            slice(None) if z is None else z,
            pl.ds(row, rows),
            pl.ds(col, cols),
        ]

    def to(n, phase, by):
        return device(moved(me, PIECES[n][5][phase], by))

    def index(n, phase, by=0):
        axis = PIECES[n][5][phase]
        return moved(me, axis, by)[axis]

    greet(partners(me))
    everything = KV_PIECES + Q_PIECES
    for n in everything:
        mine = block(n, index(n, 0), index(n, 1), index(n, 2))
        for by in BYS:
            links.launch((n, 0, by), mine, mine, to(n, 0, by))
    for k in range(8):
        columns = tokens.at[:, pl.ds(pl.multiple_of(k * 1024 + (1 - core) * 512, 512), 512)]
        links.launch(("tokens", k), columns, twin_tok.at[k], twin)

    def send_chunk(n, c):
        chunk = block(n, None, index(n, 1, c), index(n, 2))
        for by in BYS:
            links.launch((n, 2, c, by), chunk, chunk, to(n, 2, by))

    for n in everything:
        second, third = index(n, 1), index(n, 2)
        for by in BYS:
            links.arrival((n, 0, by), block(n, index(n, 0, -by), second, third))
        line = block(n, None, second, third)
        for by in BYS:
            links.launch((n, 1, by), line, line, to(n, 1, by))
        send_chunk(n, 0)
    for n in everything:
        for by in BYS:
            links.arrival((n, 1, by), block(n, None, index(n, 1, -by), index(n, 2)))
            send_chunk(n, -by)

    CHUNKS = (0,) + tuple(-by for by in BYS)

    def chunk_in(n, c):
        second = index(n, 1, c)
        for by in BYS:
            links.arrival((n, 2, c, by), block(n, None, second, index(n, 2, -by)))
        whole = block(n, None, second, None)
        links.launch((n, "twin", c), whole, whole, twin)

    def twin_in(n, c):
        links.arrival((n, "twin", c), block(n, None, index(n, 1, c), None, 1 - core))

    for copy in loads[3:]:
        copy.wait()
    for k in range(8):
        links.arrival(("tokens", k), twin_tok.at[k])

    def turn(k, _):
        at = pl.multiple_of(k * 1024 + core * 512, 512)
        turned[k, :, 0:256] = tok[:, pl.ds(at, 512)].T
        turned[k, :, 256:512] = twin_tok[k].T
        return 0

    lax.fori_loop(0, 4, turn, 0)
    keep = []

    def store(k, src, dst):
        copy = pltpu.make_async_copy(src, dst, copy_sem.at[k])
        copy.start()
        keep.append(copy)

    for c in CHUNKS:
        for n in KV_PIECES:
            chunk_in(n, c)
    for c in CHUNKS:
        for n in KV_PIECES:
            twin_in(n, c)
    store(5, w.at[2], w_out.at[2])

    def project(part):
        def add(k, total):
            lhs = tok[:, pl.ds(pl.multiple_of(k * 2048, 2048), 2048)]
            rows = w[part, lax.div(k, 2), pl.ds(lax.rem(k, 2) * 2, 2)].reshape(2048, 256)
            return total + jnp.dot(lhs, rows, preferred_element_type=F32)

        return lax.fori_loop(0, 4, add, jnp.zeros((256, 256), F32))

    both = project(2)
    cos, sin = tables[0], tables[1]
    ctx = lax.axis_index("ctx")
    key = both[:, 0:128]
    kv_out[ctx, :, 0:128] = (key * cos + turn_half(key) * sin).astype(BF16)
    kv_out[ctx, :, 128:256] = both[:, 128:256].astype(BF16)
    peers = ctx_peers()
    for k in (4, 2, 6, 1, 3, 5, 7):
        links.launch(("kv", k), kv_out.at[ctx], kv_out.at[ctx], peers[k - 1])

    lax.fori_loop(4, 8, turn, 0)
    store(8, turned, turned_out)
    for n in Q_PIECES[:3]:
        for c in CHUNKS:
            chunk_in(n, c)
    for part in range(2):
        if part == 1:
            for c in CHUNKS:
                for n in Q_PIECES[3:]:
                    chunk_in(n, c)
        for c in CHUNKS:
            for n in Q_PARTS[part]:
                twin_in(n, c)
        store(6 + part, w.at[part], w_out.at[part])
        both = project(part)
        for h in range(2):
            query = both[:, h * 128 : h * 128 + 128]
            rotated = (query * cos + turn_half(query) * sin).astype(BF16)
            q_out[:, part * 256 + h * 128 : part * 256 + h * 128 + 128] = rotated
    for k in range(1, 8):
        links.arrival(("kv", k), kv_out.at[lax.rem(ctx + 8 - k, 8)])
    for copy in keep:
        copy.wait()
    links.finish()


def gather_weights(tokens, wq, wk, wv, tables):
    vmem, anywhere = pl.BlockSpec(memory_space=pltpu.VMEM), pl.BlockSpec(memory_space=pl.ANY)
    shape = jax.ShapeDtypeStruct
    return pl.pallas_call(
        gather_kernel,
        out_shape=(
            shape((3, 2, 4, 2, 2, 4, 64, 256), BF16),
            shape((8, 512, 512), BF16),
            shape((256, 512), BF16),
            shape((8, 256, 256), BF16),
        ),
        in_specs=[anywhere] * 5,
        out_specs=(anywhere, anywhere, vmem, vmem),
        scratch_shapes=[
            pltpu.VMEM((3, 2, 4, 2, 2, 4, 64, 256), BF16),
            pltpu.VMEM((256, 8192), BF16),
            pltpu.VMEM((8, 256, 512), BF16),
            pltpu.VMEM((8, 512, 512), BF16),
            pltpu.VMEM((64, 512), F32),
            pltpu.VMEM((64, 128), F32),
            pltpu.VMEM((64, 128), F32),
            pltpu.VMEM((2, 256, 128), F32),
            pltpu.SemaphoreType.DMA((9,)),
            pltpu.SemaphoreType.DMA((212,)),
            pltpu.SemaphoreType.DMA((212,)),
        ],
        compiler_params=pltpu.CompilerParams(
            collective_id=0, has_side_effects=True, vmem_limit_bytes=60 * 2**20
        ),
        name="gather_weights",
    )(tokens, wq, wk, wv, tables)


def attention_kernel(
    positions, own_positions, q, kv, grad, tables,
    attention, grad_q, terms,
    qs, gs, gs_t, keys_t, values_t, scores, top, total, att_t, gq_t,
):
    for h in range(4):
        rows = slice(h * 256, h * 256 + 256)
        qs[rows] = q[:, h * 128 : h * 128 + 128]
        gs[rows] = grad[:, h * 128 : h * 128 + 128]
        gs_t[:, rows] = grad[:, h * 128 : h * 128 + 128].T
    for k in range(8):
        cols = slice(k * 256, k * 256 + 256)
        keys_t[:, cols] = kv[k, :, 0:128].T
        values_t[:, cols] = kv[k, :, 128:256].T
    nt = (((1,), (1,)), ((), ()))
    lead = own_positions[...] - lax.broadcasted_iota(jnp.int32, (128, 256), 0)
    top[...] = jnp.full(top.shape, MASKED, F32)

    def tile(k, cols):
        return kv[:, :, cols].reshape(2048, 128)

    def score(k, _):
        for h in range(4):
            cols = slice(h * 256, h * 256 + 256)
            s = lax.dot_general(tile(k, slice(0, 128)), qs[cols], nt, preferred_element_type=F32)
            high = None
            for r in range(16):
                rows = slice(r * 128, r * 128 + 128)
                run = jnp.where(lead >= positions[r * 128], s[rows], MASKED)
                scores[k, rows, cols] = run
                high = run if high is None else jnp.maximum(high, run)
            top[:, cols] = jnp.maximum(top[:, cols], jnp.max(high, axis=0, keepdims=True))
        return 0

    score(0, 0)
    total[...] = jnp.zeros(total.shape, F32)
    att_t[...] = jnp.zeros(att_t.shape, F32)

    def weigh(k, _):
        at = slice(0, 2048)
        for h in range(4):
            cols = slice(h * 256, h * 256 + 256)
            weight = jnp.exp2((scores[k, :, cols] - top[:, cols]) * (SCALE * LOG2E))
            scores[k, :, cols] = weight
            total[:, cols] += jnp.sum(weight, axis=0, keepdims=True)
            att_t[:, cols] += jnp.dot(values_t[:, at], weight.astype(BF16), preferred_element_type=F32)
        return 0

    weigh(0, 0)
    for h in range(4):
        cols = slice(h * 256, h * 256 + 256)
        inverse = 1.0 / total[:, cols]
        out = (att_t[:, cols] / total[:, cols]).astype(BF16)
        attention[:, h * 128 : h * 128 + 128] = out.T
        total[:, cols] = inverse
        top[:, cols] = jnp.sum(gs_t[:, cols].astype(F32) * out.astype(F32), axis=0, keepdims=True)
    gq_t[...] = jnp.zeros(gq_t.shape, F32)

    def back(k, _):
        at = slice(0, 2048)
        key_term = jnp.zeros((2048, 128), F32)
        value_term = jnp.zeros((2048, 128), F32)
        for h in range(4):
            cols = slice(h * 256, h * 256 + 256)
            probs = scores[k, :, cols] * total[:, cols]
            grad_probs = lax.dot_general(tile(k, slice(128, 256)), gs[cols], nt, preferred_element_type=F32)
            dscore = (probs * (grad_probs - top[:, cols])).astype(BF16)
            key_term += jnp.dot(dscore, qs[cols], preferred_element_type=F32)
            value_term += jnp.dot(probs.astype(BF16), gs[cols], preferred_element_type=F32)
            gq_t[:, cols] += jnp.dot(keys_t[:, at], dscore, preferred_element_type=F32)
        terms[:, :, 0:128] = (key_term * SCALE).astype(BF16).reshape(8, 256, 128)
        terms[:, :, 128:256] = value_term.astype(BF16).reshape(8, 256, 128)
        return 0

    back(0, 0)
    for h in range(4):
        a = gq_t[:, h * 256 : h * 256 + 256].T * SCALE
        unrotated = a * tables[0] - turn_half(a) * tables[1]
        grad_q[:, h * 128 : h * 128 + 128] = unrotated.astype(BF16)


def attend(positions, own_positions, q, kv, grad, tables):
    vmem = pl.BlockSpec(memory_space=pltpu.VMEM)
    shape = jax.ShapeDtypeStruct
    return pl.pallas_call(
        attention_kernel,
        out_shape=(shape((256, 512), BF16), shape((256, 512), BF16), shape((8, 256, 256), BF16)),
        in_specs=[pl.BlockSpec(memory_space=pltpu.SMEM)] + [vmem] * 5,
        out_specs=(vmem, vmem, vmem),
        scratch_shapes=[
            pltpu.VMEM((1024, 128), BF16),
            pltpu.VMEM((1024, 128), BF16),
            pltpu.VMEM((128, 1024), BF16),
            pltpu.VMEM((128, 2048), BF16),
            pltpu.VMEM((128, 2048), BF16),
            pltpu.VMEM((1, 2048, 1024), F32),
            pltpu.VMEM((1, 1024), F32),
            pltpu.VMEM((1, 1024), F32),
            pltpu.VMEM((128, 1024), F32),
            pltpu.VMEM((128, 1024), F32),
        ],
        compiler_params=pltpu.CompilerParams(vmem_limit_bytes=32 * 2**20),
        name="attend",
    )(positions, own_positions, q, kv, grad, tables)


def scatter_kernel(
    turned, w_all, grad_q, terms, tables,
    tokens_out, out,
    held, w, grads, landed, grad_tok, copy_sem, send, recv, *buffers,
):
    me = place()
    core = me["core"]
    ctx = lax.axis_index("ctx")
    twin = device(sibling(me))
    links = Links(send, recv, twin)
    accs = [buffers[7 * n : 7 * n + 3] for n in range(len(PIECES))]
    ends = [buffers[7 * n + 3 : 7 * n + 6] for n in range(len(PIECES))]
    vias = [buffers[7 * n + 6] for n in range(len(PIECES))]
    load = pltpu.make_async_copy(turned, held, copy_sem.at[0])
    load.start()
    load_w = pltpu.make_async_copy(w_all, w, copy_sem.at[1])
    load_w.start()
    greet(partners(me))
    links.launch("grad_q", grad_q, grads.at[1, :, pl.ds(0, 512)], twin)
    peers = ctx_peers()
    for k in (4, 2, 6, 1, 3, 5, 7):
        links.launch(("kv", k), terms.at[lax.rem(ctx + k, 8)], landed.at[k - 1], peers[k - 1])
    grads[0, :, 0:512] = grad_q[...]
    load.wait()
    links.arrival("grad_q", grads.at[1, :, pl.ds(0, 512)])

    def axes(n):
        return tuple(reversed(PIECES[n][5]))

    def to(n, phase, by):
        return device(moved(me, axes(n)[phase], by))

    def at(n, phase, by=0):
        axis = axes(n)[phase]
        return moved(me, axis, by)[axis]

    def product(pieces, x, y):
        part = PIECES[pieces[0]][0]
        k = lax.div(x, 2) * 4 + y
        lhs = held[k, pl.ds(pl.multiple_of(lax.rem(x, 2) * 256, 256), 256)]
        rhs = grads[:, :, part * 256 : part * 256 + 256].reshape(512, 256)
        term = jnp.dot(lhs, rhs, preferred_element_type=F32).astype(BF16)
        for n in pieces:
            _, row, rows, col, cols, _ = PIECES[n]
            for z in range(4):
                first, second, third = ({"x": x, "y": y, "z": z}[axis] for axis in axes(n))
                start = z * 64 + row
                if n in KV_PIECES:
                    accs[n][0][first, second, third] = term[start : start + rows, col : col + cols]
                    continue
                for half in range(2):
                    start = z * 64 + row + half * (rows // 2)
                    accs[n][0][first, half, second, third] = term[
                        start : start + rows // 2, col : col + cols
                    ]

    CHUNKS = (2, 1, -1, 0)

    def products(pieces):
        def one(k, _):
            product(pieces, lax.div(k, 4), lax.rem(k, 4))
            return 0

        lax.fori_loop(0, 16, one, 0)

    def send_direct(n, c):
        j = at(n, 1, c)
        for s, by in enumerate(BYS):
            src = accs[n][0].at[at(n, 0, by), j]
            links.launch((n, 0, c, s), src, ends[n][0].at[s, j], to(n, 0, by))

    def send_far(n, c):
        j = at(n, 1, c)
        for d, by in enumerate((1, -1)):
            src = accs[n][0].at[at(n, 0, 2), d, j]
            links.launch((n, "via", c, d), src, vias[n].at[d, j], to(n, 0, by))

    def send_near(n, c):
        j = at(n, 1, c)
        for d, by in enumerate((1, -1)):
            src = accs[n][0].at[at(n, 0, by), 1 - d, j]
            links.launch((n, "end", c, d, 1 - d), src, ends[n][0].at[d, 1 - d, j], to(n, 0, by))

    def relay(n, c):
        j = at(n, 1, c)
        acc, via, end = accs[n][0], vias[n], ends[n][0]
        for d, by in enumerate((1, -1)):
            links.arrival((n, "via", c, d), via.at[d, j])
            i = at(n, 0, by)
            acc[i, d, j] = (acc[i, d, j].astype(F32) + via[d, j].astype(F32)).astype(BF16)
            links.launch((n, "end", c, d, d), acc.at[i, d, j], end.at[d, d, j], to(n, 0, by))

    def chunk_in(n, c):
        j = at(n, 1, c)
        acc, end = accs[n][0], ends[n][0]
        rows = PIECES[n][2] // 2
        if n in KV_PIECES:
            for s in range(3):
                links.arrival((n, 0, c, s), end.at[s, j])
            total = acc[at(n, 0), j].astype(F32)
            for s in range(3):
                total = total + end[s, j].astype(F32)
            accs[n][1][j] = total.astype(BF16)
        for h in range(2) if n in Q_PIECES else ():
            for d in range(2):
                links.arrival((n, "end", c, d, h), end.at[d, h, j])
            total = acc[at(n, 0), h, j].astype(F32)
            total = total + end[0, h, j].astype(F32) + end[1, h, j].astype(F32)
            accs[n][1][j, :, h * rows : h * rows + rows] = total.astype(BF16)
        if c != 0:
            s = BYS.index(c)
            links.launch((n, 1, s), accs[n][1].at[j], ends[n][1].at[s], to(n, 1, c))

    def summed(n, phase):
        total = accs[n][phase][at(n, phase)].astype(F32)
        for s in range(3):
            total = total + ends[n][phase][s].astype(F32)
        return total

    def second(n):
        for s in range(3):
            links.arrival((n, 1, s), ends[n][1].at[s])
        accs[n][2][...] = summed(n, 1).astype(BF16)
        for s, by in enumerate(BYS):
            links.launch((n, 2, s), accs[n][2].at[at(n, 2, by)], ends[n][2].at[s], to(n, 2, by))

    def last(n):
        part, row, rows, col, cols, _ = PIECES[n]
        for s in range(3):
            links.arrival((n, 2, s), ends[n][2].at[s])
        out[row : row + rows, part * 256 + col : part * 256 + col + cols] = summed(n, 2)

    for pieces in Q_PARTS:
        products(pieces)
        for c in CHUNKS:
            for n in pieces:
                send_far(n, c)
    for c in CHUNKS:
        for n in Q_PIECES:
            send_near(n, c)
    for c in CHUNKS:
        for n in Q_PIECES:
            if axes(n)[0] != "z":
                relay(n, c)

    def input_slice(k, _):
        total = None
        for part in range(3):
            lhs = grads[0, :, part * 256 : part * 256 + 256]
            rows = w[part, lax.div(k, 8), lax.rem(lax.div(k, 2), 4), lax.rem(k, 2)].reshape(512, 256)
            term = lax.dot_general(lhs, rows, (((1,), (1,)), ((), ())), preferred_element_type=F32)
            total = term if total is None else total + term
        grad_tok[:, pl.ds(pl.multiple_of(k * 512, 512), 512)] = total.astype(BF16)
        return 0

    stores = []

    def inputs(quarter):
        lax.fori_loop(quarter * 4, quarter * 4 + 4, input_slice, 0)
        cols = pl.ds(quarter * 2048, 2048)
        copy = pltpu.make_async_copy(grad_tok.at[:, cols], tokens_out.at[:, cols], copy_sem.at[2 + quarter])
        copy.start()
        stores.append(copy)

    for k in range(1, 8):
        links.arrival(("kv", k), landed.at[k - 1])
    keyval = terms[ctx].astype(F32)
    for k in range(7):
        keyval = keyval + landed[k].astype(F32)
    key = keyval[:, 0:128]
    grads[0, :, 512:640] = (key * tables[0] - turn_half(key) * tables[1]).astype(BF16)
    grads[0, :, 640:768] = keyval[:, 128:256].astype(BF16)
    columns = pl.ds(512, 256)
    links.launch("grad_kv", grads.at[0, :, columns], grads.at[1, :, columns], twin)
    for c in CHUNKS:
        for n in Q_PIECES:
            if axes(n)[0] == "z":
                relay(n, c)
    load_w.wait()
    inputs(0)
    links.arrival("grad_kv", grads.at[1, :, columns])

    products(KV_PIECES)
    for c in CHUNKS:
        for n in KV_PIECES:
            send_direct(n, c)
    for k, c in enumerate(CHUNKS):
        for n in Q_PIECES:
            chunk_in(n, c)
        if k < 3:
            inputs(k + 1)
    for n in Q_PIECES:
        second(n)
    for c in CHUNKS:
        for n in KV_PIECES:
            chunk_in(n, c)
    for n in KV_PIECES:
        second(n)
    for n in Q_PIECES + KV_PIECES:
        last(n)
    for copy in stores:
        copy.wait()
    links.finish()


def scatter_grads(turned, w_all, grad_q, terms, tables):
    vmem, anywhere = pl.BlockSpec(memory_space=pltpu.VMEM), pl.BlockSpec(memory_space=pl.ANY)
    shape = jax.ShapeDtypeStruct
    buffers = []
    for n, (_, _, rows, _, cols, _) in enumerate(PIECES):
        half, whole = (rows // 2, cols), (rows, cols)
        later = ((4, 4) + whole, (4,) + whole), ((3, 4) + whole, (3,) + whole)
        if n in KV_PIECES:
            first = (4, 4, 4) + whole, (3, 4, 4) + whole, (8, 128)
        else:
            first = (4, 2, 4, 4) + half, (2, 2, 4, 4) + half, (2, 4, 4) + half
        for shape_of in (first[0], *later[0], first[1], *later[1], first[2]):
            buffers.append(pltpu.VMEM(shape_of, BF16))
    return pl.pallas_call(
        scatter_kernel,
        out_shape=(shape((256, 8192), BF16), shape((64, 768), F32)),
        in_specs=[anywhere, anywhere, vmem, vmem, vmem],
        out_specs=(anywhere, vmem),
        scratch_shapes=[
            pltpu.VMEM((8, 512, 512), BF16),
            pltpu.VMEM((3, 2, 4, 2, 2, 4, 64, 256), BF16),
            pltpu.VMEM((2, 256, 768), BF16),
            pltpu.VMEM((7, 256, 256), BF16),
            pltpu.VMEM((256, 8192), BF16),
            pltpu.SemaphoreType.DMA((6,)),
            pltpu.SemaphoreType.DMA((216,)),
            pltpu.SemaphoreType.DMA((216,)),
            *buffers,
        ],
        compiler_params=pltpu.CompilerParams(
            collective_id=1, has_side_effects=True, vmem_limit_bytes=48 * 2**20
        ),
        name="scatter_grads",
    )(turned, w_all, grad_q, terms, tables)


def rope_tables(positions_in, head_dim):
    half_width = head_dim // 2
    exponent = jnp.arange(half_width).astype(F32) * (2.0 / head_dim)
    frequency = jnp.power(ROPE_BASE, -exponent)
    angles = positions_in.astype(F32)[:, None] * frequency[None, :]
    cos, sin = jnp.cos(angles), jnp.sin(angles)
    return jnp.stack([jnp.concatenate([cos, cos], axis=1), jnp.concatenate([-sin, sin], axis=1)])


def body(tokens, positions, query_weight, key_weight, value_weight, grad_output):
    own_positions = lax.dynamic_slice_in_dim(positions, lax.axis_index("ctx") * 256, 256)
    tables = rope_tables(own_positions, 128)
    w_all, turned, q, kv = gather_weights(
        tokens[0], query_weight, key_weight, value_weight, tables
    )
    attention, grad_q, terms = attend(
        positions, own_positions[None], q, kv, grad_output[0], tables
    )
    grad_tokens, grads = scatter_grads(turned, w_all, grad_q, terms, tables)
    return attention[None], grad_tokens[None], grads[:, :512], grads[:, 512:640], grads[:, 640:]


def solution(mesh):
    in_specs = (
        P("dp", "ctx", None),
        P(),
        P(("dp", "ctx"), None),
        P(("dp", "ctx"), None),
        P(("dp", "ctx"), None),
        P("dp", "ctx", None),
    )
    out_specs = (
        P("dp", "ctx", None),
        P("dp", "ctx", None),
        P(("dp", "ctx"), None),
        P(("dp", "ctx"), None),
        P(("dp", "ctx"), None),
    )
    return jax.shard_map(body, mesh=mesh, in_specs=in_specs, out_specs=out_specs, check_vma=False)
```
